1024 devices in a mesh: lon: 128 (over y, x_lo, z), lat: 8 (over x_hi, core).
Axes of the slice: x: 8 (x_hi: 4, x_lo: 2; x = x_hi * 2 + x_lo), y: 8, z: 8, core: 2. Of those that a mesh axis runs over, the one named last changes fastest.
Arguments:
- zonal_flow_speed: float32 [62, 1024, 1024], P(None, 'lon', 'lat'), may hold values from -6 to 6
- meridional_flow_speed: float32 [62, 1024, 1024], P(None, 'lon', 'lat'), may hold values from -6 to 6
- first_scalar_concentration: float32 [62, 1024, 1024], P(None, 'lon', 'lat'), may hold values from -6 to 6
- second_scalar_concentration: float32 [62, 1024, 1024], P(None, 'lon', 'lat'), may hold values from -6 to 6
- water_point_indicator: int32 [1024, 1024], P('lon', 'lat'), may hold values 0 or 1
- water_layers_per_point: int32 [1024, 1024], P('lon', 'lat'), may hold values from 1 to 62
- elevation_operator_main_entry: float32 [1024, 1024], P('lon', 'lat'), may hold values from 0.02 to 0.2
- earlier_free_elevation: float32 [1024, 1024], P('lon', 'lat'), may hold values from -6 to 6
Outputs:
- zonal_next: float32 [62, 1024, 1024], P(None, 'lon', 'lat')
- meridional_next: float32 [62, 1024, 1024], P(None, 'lon', 'lat')
- temperature_next: float32 [62, 1024, 1024], P(None, 'lon', 'lat')
- salinity_next: float32 [62, 1024, 1024], P(None, 'lon', 'lat')
- surface_height: float32 [1024, 1024], P('lon', 'lat')
The draws below stay inside these ranges and needn't reach their ends.
Inputs may be any that keep to these rules, and one draw needn't show every extreme that they name: `water_layers_per_point`: every column has at least one and at most 62 levels.
All inputs are finite; a program needn't handle non-finite values. No bound on the sum of `water_point_indicator` on one device may be relied on, other than what follows from the above.
Results may differ from the reference program's by a relative error of at most 0.000026.
Values sent between devices are 32-bit elements; how exact they have to be, the bound alone decides.
No kernel may reach another device: no remote copies, remote signals or barrier semaphores. Data moves between devices by JAX's collectives and lax.ppermute only.
A program may use at most 32 MiB of HBM per device.

```python
import math
import jax
import jax.numpy as jnp
from jax import lax

LAYER_NUMBER = 62
ITERS = 8
MERIDIAN_NUMBER = 1024
PARALLEL_NUMBER = 1024


def set_ends(drawn, stream_key, least, largest):
    longest = drawn.shape.index(max(drawn.shape))
    spots = []
    for shift in (0, 1):
        where = [jax.random.randint(jax.random.fold_in(stream_key, axis), (), 0, length) for axis, length in enumerate(drawn.shape)]
        where[longest] = (where[longest] + shift) % drawn.shape[longest]
        spots.append(tuple(where))
    return drawn.at[spots[0]].set(least).at[spots[1]].set(largest)


def block_scale(stream_key, shape, split, low, high):
    loudness, own = 1.0, jax.random.fold_in(stream_key, 6)
    for position, blocks in split:
        heights = jnp.exp(jax.random.uniform(jax.random.fold_in(own, position), (blocks,), jnp.float32, low / len(split), high / len(split)))
        loudness = loudness * jnp.repeat(heights, shape[position] // blocks).reshape([-1 if axis == position else 1 for axis in range(len(shape))])
    return loudness


def bell_draw(key, extent, spread, most, split=(), dtype=jnp.bfloat16):
    level = block_scale(key, extent, split, -0.22, 0.18) if split else 1.0
    array = jax.random.normal(key, extent, jnp.float32) * spread * level
    return jnp.minimum(jnp.maximum(array, -most), most).astype(dtype)


def setup_inputs(seed: int = 0) -> dict:
    key_of = jax.random.split(jax.random.key(seed), 9)
    zonal_flow_speed = bell_draw(key_of[0], (LAYER_NUMBER, MERIDIAN_NUMBER, PARALLEL_NUMBER), 1.0, 6.0, ((1, 128), (2, 8)), jnp.float32)
    meridional_flow_speed = bell_draw(key_of[1], (LAYER_NUMBER, MERIDIAN_NUMBER, PARALLEL_NUMBER), 1.0, 6.0, ((1, 128), (2, 8)), jnp.float32)
    first_scalar_concentration = bell_draw(key_of[2], (LAYER_NUMBER, MERIDIAN_NUMBER, PARALLEL_NUMBER), 1.0, 6.0, ((1, 128), (2, 8)), jnp.float32)
    second_scalar_concentration = bell_draw(key_of[3], (LAYER_NUMBER, MERIDIAN_NUMBER, PARALLEL_NUMBER), 1.0, 6.0, ((1, 128), (2, 8)), jnp.float32)
    water_point_indicator = set_ends((jax.random.randint(key_of[4], (MERIDIAN_NUMBER, PARALLEL_NUMBER), 0, 4) < 3).astype(jnp.int32), jax.random.fold_in(key_of[4], 1), 0, 1)
    water_layers_per_point = set_ends(jax.random.randint(key_of[5], (MERIDIAN_NUMBER, PARALLEL_NUMBER), 1, LAYER_NUMBER + 1), jax.random.fold_in(key_of[5], 1), 1, LAYER_NUMBER).astype(jnp.int32)
    elevation_operator_main_entry = jnp.clip(jnp.exp(math.log(0.2) - 2.3025851 * jax.random.uniform(key_of[6], (MERIDIAN_NUMBER, PARALLEL_NUMBER), jnp.float32) ** block_scale(key_of[6], (MERIDIAN_NUMBER, PARALLEL_NUMBER), ((0, 128), (1, 8)), -0.2, 0.2)), 0.02, 0.2)
    earlier_free_elevation = bell_draw(key_of[7], (MERIDIAN_NUMBER, PARALLEL_NUMBER), 1.0, 6.0, ((0, 128), (1, 8)), jnp.float32)
    return {"zonal_flow_speed": zonal_flow_speed, "meridional_flow_speed": meridional_flow_speed, "first_scalar_concentration": first_scalar_concentration, "second_scalar_concentration": second_scalar_concentration, "water_point_indicator": water_point_indicator, "water_layers_per_point": water_layers_per_point, "elevation_operator_main_entry": elevation_operator_main_entry, "earlier_free_elevation": earlier_free_elevation}


spectrum_mid = 1.0
spectrum_half = 0.995


def advance(scalar_quantity_array, zonal, merid, ocean_cell_mask):
    columns = scalar_quantity_array.shape[2]
    padded = jnp.pad(scalar_quantity_array, ((0, 0), (0, 0), (2, 2)))

    def along_lon(shift):
        return jnp.roll(scalar_quantity_array, -shift, axis=1)

    def along_lat(shift):
        return padded[:, :, 2 + shift:2 + shift + columns]

    grad_lon = (8.0 * (along_lon(1) - along_lon(-1)) - (along_lon(2) - along_lon(-2))) / 12.0
    grad_lat = (8.0 * (along_lat(1) - along_lat(-1)) - (along_lat(2) - along_lat(-2))) / 12.0
    laplace = along_lon(1) + along_lon(-1) + along_lat(1) + along_lat(-1) - 4.0 * scalar_quantity_array
    vertical_pad = jnp.pad(scalar_quantity_array, ((1, 1), (0, 0), (0, 0)))
    vertical = vertical_pad[2:] + vertical_pad[:-2] - 2.0 * scalar_quantity_array
    tendency = -(zonal * grad_lon + merid * grad_lat) + 0.05 * laplace + 0.2 * vertical
    return ocean_cell_mask * (scalar_quantity_array + 0.1 * tendency)


def neighbours(shaded):
    padded = jnp.pad(shaded, ((0, 0), (1, 1)))
    return jnp.roll(shaded, -1, 0) + jnp.roll(shaded, 1, 0) + padded[:, 2:] + padded[:, :-2]


def reference(zonal_flow_speed, meridional_flow_speed, first_scalar_concentration, second_scalar_concentration, water_point_indicator, water_layers_per_point, elevation_operator_main_entry, earlier_free_elevation):
    shade = water_point_indicator.astype(jnp.float32)
    depth = lax.broadcasted_iota(jnp.int32, zonal_flow_speed.shape, 0)
    ocean_cell_mask = shade[None] * (depth < water_layers_per_point[None]).astype(jnp.float32)
    zonal = zonal_flow_speed * ocean_cell_mask
    merid = meridional_flow_speed * ocean_cell_mask
    results = []
    for scalar_quantity_array in (zonal_flow_speed, meridional_flow_speed, first_scalar_concentration, second_scalar_concentration):
        results.append(advance(scalar_quantity_array * ocean_cell_mask, zonal, merid, ocean_cell_mask))
    forcing = 0.1 * jnp.sum(0.7 * results[2] - 0.5 * results[3], axis=0)
    rhs = earlier_free_elevation + forcing
    sigma = spectrum_mid / spectrum_half
    ratio = 1.0 / sigma
    diagonal = elevation_operator_main_entry + 4.0
    inverse = 1.0 / diagonal
    residual = rhs
    previous = earlier_free_elevation
    iterate = earlier_free_elevation
    for step in range(ITERS):
        residual = residual - (diagonal * previous - shade * neighbours(shade * previous))
        if step == 0:
            direction = residual * inverse / spectrum_mid
        else:
            following = 1.0 / (2.0 * sigma - ratio)
            direction = following * ratio * previous + (2.0 * following / spectrum_half) * residual * inverse
            ratio = following
        iterate = iterate + direction
        previous = direction
    return results[0], results[1], results[2], results[3], iterate
```

```python
import jax
import jax.numpy as jnp
from jax import lax
from jax.experimental import pallas as pl
from jax.experimental.pallas import tpu as pltpu
from jax.sharding import PartitionSpec as P

ITERS = 8
LEVELS = 62
SPECTRUM_MID = 1.0
SPECTRUM_HALF = 0.995

ROWS = 8
LANES = 128
STRIP = 128
LON_ROWS = 4 * STRIP + 3 * ROWS
LAT_ROWS = 17 * ROWS
SOLVE_ROWS = 5 * ROWS + 32 + 8
VMEM = 12 * 1024 * 1024

F32 = jnp.float32
ADV = 0.1 / 12.0


def rows_of(shape=(ROWS, LANES)):
    return lax.broadcasted_iota(jnp.int32, shape, 0)


def lanes_of(shape=(ROWS, LANES)):
    return lax.broadcasted_iota(jnp.int32, shape, 1)


def by_rows(x, d):
    d %= ROWS
    return pltpu.roll(x, d, 0) if d else x


def by_lanes(x, d):
    d %= LANES
    return pltpu.roll(x, d, 1) if d else x


def scalar_mix(t, s):
    return 0.7 * t - 0.5 * s


def even(axis):
    return lax.axis_index(axis) % 2 == 0


def pack_lon(u, v, t, s, water, layers, diag, elev, parity, up_first, low_first):
    row = rows_of()
    group = row >> 1
    depth = water[...] * layers[...]
    is_even = parity[0] == 0

    def body(g, carry):
        for f, ref in enumerate((u, v, t, s)):
            top = None
            for i in range(4):
                k = 4 * g + i
                m = jnp.where(k < depth, ref[jnp.minimum(k, LEVELS - 1)], 0.0)
                a, b = by_rows(m, 2 * i), by_rows(m, 2 * i - 6)
                if top is None:
                    top, bottom = a, b
                else:
                    top, bottom = jnp.where(group == i, a, top), jnp.where(group == i, b, bottom)
            at = pl.ds(pl.multiple_of(f * STRIP + 8 * g, 8), 8)
            up_first[at, :] = jnp.where(is_even, top, bottom)
            low_first[at, :] = jnp.where(is_even, bottom, top)
        return carry

    lax.fori_loop(0, 16, body, 0)
    for ref in (up_first, low_first):
        ref[4 * STRIP : 4 * STRIP + 8, :] = elev[...]
        ref[4 * STRIP + 8 : 4 * STRIP + 16, :] = diag[...]
        ref[4 * STRIP + 16 : 4 * STRIP + 24, :] = depth.astype(F32)


def pack_lat(u, v, t, s, water, layers, diag, elev, parity, odd_out, even_out, partial):
    row, lane = rows_of(), lanes_of()
    slot = lane >> 3
    depth = water[...] * layers[...]
    is_even = parity[1] == 0

    def body(a, acc):
        left = [None] * 4
        right = [None] * 4
        for i in range(16):
            k = 16 * a + i
            wet = k < depth
            at = jnp.minimum(k, LEVELS - 1)
            m = [jnp.where(wet, ref[at], 0.0) for ref in (u, v, t, s)]
            for f in range(4):
                x, y = by_lanes(m[f], 8 * i), by_lanes(m[f], 8 * i - 120)
                left[f] = x if i == 0 else jnp.where(slot == i, x, left[f])
                right[f] = y if i == 0 else jnp.where(slot == i, y, right[f])
            w = scalar_mix(m[2], m[3])
            n1 = jnp.where(row < 7, by_rows(w, -1), 0.0)
            p1 = jnp.where(row > 0, by_rows(w, 1), 0.0)
            n2 = jnp.where(row < 6, by_rows(w, -2), 0.0)
            p2 = jnp.where(row > 1, by_rows(w, 2), 0.0)
            e1 = jnp.where(lane < 127, by_lanes(w, -1), 0.0)
            q1 = jnp.where(lane > 0, by_lanes(w, 1), 0.0)
            e2 = jnp.where(lane < 126, by_lanes(w, -2), 0.0)
            q2 = jnp.where(lane > 1, by_lanes(w, 2), 0.0)
            gx = 8.0 * (n1 - p1) - (n2 - p2)
            gy = 8.0 * (e1 - q1) - (e2 - q2)
            around = jnp.where(wet, (n1 + p1) + (e1 + q1), 0.0)
            column = jnp.where(k > 0, w, 0.0) + jnp.where(k + 1 < depth, w, 0.0)
            acc = acc + (
                0.94 * w + 0.02 * column + 0.005 * around - ADV * (m[0] * gx + m[1] * gy)
            )
        for f in range(4):
            where = pl.ds(pl.multiple_of(f * 32 + 8 * a, 8), 8)
            odd_out[where, :] = jnp.where(is_even, left[f], right[f])
            even_out[where, :] = jnp.where(is_even, right[f], left[f])
        return acc

    acc = 0.1 * lax.fori_loop(0, 4, body, jnp.zeros((ROWS, LANES), F32))
    partial[...] = acc
    flat = (acc, elev[...], diag[...], depth.astype(F32))
    left = right = None
    for i, x in enumerate(flat):
        a, b = by_lanes(x, 8 * i), by_lanes(x, 8 * i - 120)
        left = a if i == 0 else jnp.where(slot == i, a, left)
        right = b if i == 0 else jnp.where(slot == i, b, right)
    odd_out[128:136, :] = jnp.where(is_even, left, right)
    even_out[128:136, :] = jnp.where(is_even, right, left)


def tile_lanes(x):
    x = jnp.where(lanes_of() < 8, x, 0.0)
    for d in (8, 16, 32, 64):
        x = x + by_lanes(x, d)
    return x


def sum_slots(x):
    for d in (8, 16, 32, 64):
        x = x + by_lanes(x, d)
    return x


def wet_pack(depth, a):
    return (16 * a + (lanes_of() >> 3)).astype(F32) < depth


def lat_rims(a_v, a_w, a_depth, b_v, b_w, b_depth):
    column = lanes_of() & 7
    a_sum = b_sum = jnp.zeros((ROWS, LANES), F32)
    for i in range(4):
        y1, y2 = by_lanes(b_w[i], 7), by_lanes(b_w[i], 6)
        y1 = jnp.where(column == 7, y1, 0.0)
        y2 = jnp.where(column >= 6, y2, 0.0)
        a_sum = a_sum - ADV * a_v[i] * (8.0 * y1 - y2)
        a_sum = a_sum + 0.005 * jnp.where(wet_pack(a_depth, i), y1, 0.0)
        z1, z2 = by_lanes(a_w[i], -7), by_lanes(a_w[i], -6)
        z1 = jnp.where(column == 0, z1, 0.0)
        z2 = jnp.where(column <= 1, z2, 0.0)
        b_sum = b_sum - ADV * b_v[i] * (z2 - 8.0 * z1)
        b_sum = b_sum + 0.005 * jnp.where(wet_pack(b_depth, i), z1, 0.0)
    return 0.1 * sum_slots(a_sum), 0.1 * sum_slots(b_sum)


def pick(flag, a, b):
    return jnp.where(flag, a, b)


def four(ref, base, flag, other):
    at = [slice(base + 8 * i, base + 8 * i + 8) for i in range(4)]
    return [jnp.where(flag, ref[x, :], other[x, :]) for x in at]


def forcing(
    parity, own_odd_u, own_even_u, got_odd_ts, got_even_ts, flat2d,
    own_odd_lat, own_even_lat, got_odd_lat, got_even_lat, partial,
    odd_out, even_out,
):
    row, lane = rows_of(), lanes_of()
    lon_even, lat_even = parity[0] == 0, parity[1] == 0
    elev, diag, depth = (flat2d[8 * i : 8 * i + 8, :] for i in range(3))
    total = elev + partial[...]

    r = row & 1
    for lower in (True, False):
        rim = row < 2 if lower else row >= 6
        tiled = jnp.where(rim, depth, 0.0)
        tiled = tiled + by_rows(tiled, 2)
        tiled = tiled + by_rows(tiled, 4)
        acc = jnp.zeros((ROWS, LANES), F32)
        own_first = lon_even if lower else jnp.logical_not(lon_even)
        for g in range(16):
            at = slice(8 * g, 8 * g + 8)
            also = slice(STRIP + 8 * g, STRIP + 8 * g + 8)
            vel = jnp.where(own_first, own_odd_u[at, :], own_even_u[at, :])
            w = jnp.where(
                own_first,
                scalar_mix(got_odd_ts[at, :], got_odd_ts[also, :]),
                scalar_mix(got_even_ts[at, :], got_even_ts[also, :]),
            )
            wet = (4 * g + (row >> 1)).astype(F32) < tiled
            if lower:
                near = jnp.where(r == 0, by_rows(w, -1), 0.0)
                slope = w - 8.0 * near
            else:
                near = jnp.where(r == 1, by_rows(w, 1), 0.0)
                slope = 8.0 * near - w
            acc = acc + (0.005 * jnp.where(wet, near, 0.0) - ADV * vel * slope)
        acc = acc + by_rows(acc, 2)
        acc = acc + by_rows(acc, 4)
        total = total + jnp.where(rim, 0.1 * acc, 0.0)

    own_r = [four(own_even_lat, f * 32, lat_even, own_odd_lat) for f in range(1, 4)]
    own_l = [four(own_odd_lat, f * 32, lat_even, own_even_lat) for f in range(1, 4)]
    ext_r = [four(got_even_lat, f * 32, lat_even, got_odd_lat) for f in range(4)]
    ext_l = [four(got_odd_lat, f * 32, lat_even, got_even_lat) for f in range(4)]
    flat_r = jnp.where(lat_even, got_even_lat[128:136, :], got_odd_lat[128:136, :])
    flat_l = jnp.where(lat_even, got_odd_lat[128:136, :], got_even_lat[128:136, :])

    def mixed(pair):
        return [scalar_mix(x, y) for x, y in zip(*pair, strict=True)]

    w_r, w_l = mixed(ext_r[2:]), mixed(ext_l[2:])
    miss_own_r, miss_ext_r = lat_rims(
        own_r[0], mixed(own_r[1:]), tile_lanes(by_lanes(depth, 8)),
        ext_r[1], w_r, tile_lanes(by_lanes(flat_r, -24)),
    )
    miss_ext_l, miss_own_l = lat_rims(
        ext_l[1], w_l, tile_lanes(by_lanes(flat_l, -24)),
        own_l[0], mixed(own_l[1:]), tile_lanes(depth),
    )
    total = total + jnp.where(lane >= 126, miss_own_r, 0.0) + jnp.where(lane < 2, miss_own_l, 0.0)

    def side(i):
        return jnp.where(
            lane < 8,
            by_lanes(flat_r, -8 * i),
            jnp.where(lane >= 120, by_lanes(flat_l, 120 - 8 * i), 0.0),
        )

    elev_side = side(1)
    total_side = side(0) + elev_side
    total_side = total_side + jnp.where(lane < 2, miss_ext_r, 0.0)
    total_side = total_side + jnp.where(lane >= 126, miss_ext_l, 0.0)
    for ref in (odd_out, even_out):
        for i, x in enumerate((total, total_side, elev_side, side(2), side(3))):
            ref[8 * i : 8 * i + 8, :] = x
        ref[SOLVE_ROWS - 8 : SOLVE_ROWS, :] = jnp.zeros((8, LANES), F32)
    packs = ext_r[0] + ext_l[0] + w_r + w_l
    group = row >> 1
    for i in range(4):
        top = bottom = None
        for j in range(4):
            x = packs[4 * i + j]
            a, b = by_rows(x, 2 * j), by_rows(x, 2 * j - 6)
            top = a if j == 0 else jnp.where(group == j, a, top)
            bottom = b if j == 0 else jnp.where(group == j, b, bottom)
        at = slice(40 + 8 * i, 48 + 8 * i)
        odd_out[at, :] = jnp.where(lon_even, top, bottom)
        even_out[at, :] = jnp.where(lon_even, bottom, top)


def fields(
    parity, u, v, t, s, water, layers, odd_lon, even_lon, odd_lat, even_lat, *outs
):
    row, lane = rows_of(), lanes_of()
    depth = water[...] * layers[...]
    lon_even, lat_even = parity[0] == 0, parity[1] == 0
    refs = (u, v, t, s)

    def level(a, i, strips, packs):
        k = 16 * a + i
        wet = k < depth
        wet_below = k + 1 < depth
        below, above = jnp.minimum(k + 1, LEVELS - 1), jnp.maximum(k - 1, 0)
        center = [jnp.where(wet, ref[k], 0.0) for ref in refs]
        j = i % 4
        for f in range(4):
            m = center[f]
            upper, lower = strips[f]
            rim = jnp.where(row < 4, by_rows(upper, -2 * j), by_rows(lower, 6 - 2 * j))
            n1 = by_rows(jnp.where(row < 1, rim, m), -1)
            n2 = by_rows(jnp.where(row < 2, rim, m), -2)
            p1 = by_rows(jnp.where(row > 6, rim, m), 1)
            p2 = by_rows(jnp.where(row > 5, rim, m), 2)
            west, east = packs[f]
            beside = jnp.where(lane < 64, by_lanes(east, -8 * i), by_lanes(west, 120 - 8 * i))
            e1 = by_lanes(jnp.where(lane < 1, beside, m), -1)
            e2 = by_lanes(jnp.where(lane < 2, beside, m), -2)
            q1 = by_lanes(jnp.where(lane > 126, beside, m), 1)
            q2 = by_lanes(jnp.where(lane > 125, beside, m), 2)
            gx = 8.0 * (n1 - p1) - (n2 - p2)
            gy = 8.0 * (e1 - q1) - (e2 - q2)
            around = (n1 + p1) + (e1 + q1)
            column = jnp.where(wet_below, refs[f][below], 0.0) + jnp.where(
                k > 0, refs[f][above], 0.0
            )
            fresh = (
                0.94 * m
                + 0.02 * column
                + 0.005 * around
                - ADV * (center[0] * gx + center[1] * gy)
            )
            outs[f][k] = jnp.where(wet, fresh, 0.0)

    def body(a, carry):
        packs = []
        for f in range(4):
            at = pl.ds(pl.multiple_of(f * 32 + 8 * a, 8), 8)
            x, y = odd_lat[at, :], even_lat[at, :]
            packs.append((jnp.where(lat_even, x, y), jnp.where(lat_even, y, x)))
        for b in range(4):
            strips = []
            for f in range(4):
                at = pl.ds(pl.multiple_of(f * STRIP + 32 * a + 8 * b, 8), 8)
                x, y = odd_lon[at, :], even_lon[at, :]
                strips.append((jnp.where(lon_even, y, x), jnp.where(lon_even, x, y)))
            for i in range(4 * b, 4 * b + 4):
                if i < 14:
                    level(a, i, strips, packs)
                else:
                    pl.when(16 * a + i < LEVELS)(lambda i=i, s=strips: level(a, i, s, packs))
        return carry

    lax.fori_loop(0, 4, body, 0)


def solve(
    parity, own2d, odd2d, even2d, odd_lat, even_lat, own_b, odd_b, even_b, height
):
    row, lane = rows_of(), lanes_of()
    lon_even, lat_even = parity[0] == 0, parity[1] == 0
    lower = [jnp.where(lon_even, odd_b[8 * i : 8 * i + 8, :], even_b[8 * i : 8 * i + 8, :]) for i in range(10)]
    upper = [jnp.where(lon_even, even_b[8 * i : 8 * i + 8, :], odd_b[8 * i : 8 * i + 8, :]) for i in range(10)]
    own = [own_b[8 * i : 8 * i + 8, :] for i in range(5)]

    ext_r = [four(even_lat, f * 32, lat_even, odd_lat) for f in (0, 2, 3)]
    ext_l = [four(odd_lat, f * 32, lat_even, even_lat) for f in (0, 2, 3)]

    def lon_part(vel, wet, x1, x2):
        slope = jnp.where(row == 0, -8.0 * x1, jnp.where(row == 7, 8.0 * x1, 0.0))
        slope = slope + jnp.where(row < 2, x2, jnp.where(row >= 6, -x2, 0.0))
        near = jnp.where((row == 0) | (row == 7), x1, 0.0)
        return 0.005 * jnp.where(wet, near, 0.0) - ADV * vel * slope

    def rim_rows(tile, q, first):
        return by_rows(tile[5 + q // 4], first - 2 * (q % 4))

    def side_parts(ext, base, own_depth, near_depth):
        mine = theirs = jnp.zeros((ROWS, LANES), F32)
        for i in range(4):
            vel, w = ext[0][i], scalar_mix(ext[1][i], ext[2][i])
            qu, qw = base + i, 8 + base + i
            x2 = jnp.where(row < 4, rim_rows(lower, qw, 0), rim_rows(upper, qw, 6))
            x1 = jnp.where(row < 4, rim_rows(lower, qw, -1), rim_rows(upper, qw, 7))
            mine = mine + lon_part(vel, wet_pack(own_depth, i), x1, x2)
            y2 = jnp.where(row < 4, by_rows(w, 2), by_rows(w, -2))
            y1 = jnp.where(row < 4, by_rows(w, 1), by_rows(w, -1))
            other = jnp.where(row < 4, rim_rows(upper, qu, 0), rim_rows(lower, qu, 6))
            theirs = theirs + lon_part(other, wet_pack(near_depth, i), y1, y2)
        return 0.1 * sum_slots(mine), 0.1 * sum_slots(theirs)

    near_side = jnp.where(row < 4, upper[4], lower[4])
    mine_r, theirs_r = side_parts(ext_r, 0, tile_lanes(own[4]), tile_lanes(near_side))
    mine_l, theirs_l = side_parts(
        ext_l, 4, tile_lanes(by_lanes(own[4], 8)), tile_lanes(by_lanes(near_side, 8))
    )
    in_r, in_l = lane < 8, lane >= 120
    mine = jnp.where(in_r, mine_r, jnp.where(in_l, mine_l, 0.0))
    theirs = jnp.where(in_r, theirs_r, jnp.where(in_l, theirs_l, 0.0))

    flat_own = [own2d[8 * i : 8 * i + 8, :] for i in range(3)]
    flat_low = [jnp.where(lon_even, odd2d[8 * i : 8 * i + 8, :], even2d[8 * i : 8 * i + 8, :]) for i in range(3)]
    flat_up = [jnp.where(lon_even, even2d[8 * i : 8 * i + 8, :], odd2d[8 * i : 8 * i + 8, :]) for i in range(3)]

    rhs = [
        lower[0], own[0], upper[0],
        lower[1] + jnp.where(row >= 6, theirs, 0.0),
        own[1] + mine,
        upper[1] + jnp.where(row < 2, theirs, 0.0),
    ]
    elev = [flat_low[0], flat_own[0], flat_up[0], lower[2], own[2], upper[2]]
    diag = [flat_low[1], flat_own[1], flat_up[1], lower[3], own[3], upper[3]]
    wet = [x > 0.0 for x in (flat_low[2], flat_own[2], flat_up[2], lower[4], own[4], upper[4])]
    diag = [x + 4.0 for x in diag]
    inverse = [1.0 / x for x in diag]

    def neighbours(x):
        out = []
        up = [by_rows(y, -1) for y in x]
        down = [by_rows(y, 1) for y in x]
        east = [by_lanes(y, -1) for y in x]
        west = [by_lanes(y, 1) for y in x]
        for i in range(6):
            h, c = divmod(i, 3)
            base = 3 * h
            other = 3 * (1 - h) + c
            n = jnp.where(row < 7, up[i], up[base + (c + 1) % 3])
            p = jnp.where(row > 0, down[i], down[base + (c + 2) % 3])
            e = jnp.where(lane < 127, east[i], east[other])
            w = jnp.where(lane > 0, west[i], west[other])
            out.append((n + p) + (e + w))
        return out

    sigma = SPECTRUM_MID / SPECTRUM_HALF
    ratio = 1.0 / sigma
    residual = rhs
    previous = elev
    iterate = elev[1]
    for step in range(ITERS):
        around = neighbours([jnp.where(a, x, 0.0) for a, x in zip(wet, previous, strict=True)])
        residual = [
            res - (d * x - jnp.where(a, n, 0.0))
            for res, d, x, a, n in zip(residual, diag, previous, wet, around, strict=True)
        ]
        if step == 0:
            previous = [res * inv / SPECTRUM_MID for res, inv in zip(residual, inverse, strict=True)]
        else:
            following = 1.0 / (2.0 * sigma - ratio)
            keep, gain = following * ratio, 2.0 * following / SPECTRUM_HALF
            previous = [
                keep * x + gain * res * inv
                for x, res, inv in zip(previous, residual, inverse, strict=True)
            ]
            ratio = following
        iterate = iterate + previous[1]
    height[...] = iterate


def shaped(*shape):
    return jax.ShapeDtypeStruct(shape, F32)


def part(rows, index=0):
    return pl.BlockSpec((rows, LANES), lambda i: (index, 0))


def call(kernel, outs, ins, flops, moved, grid=()):
    return pl.pallas_call(
        kernel,
        grid=grid,
        out_shape=outs,
        in_specs=ins,
        compiler_params=pltpu.CompilerParams(vmem_limit_bytes=VMEM),
        cost_estimate=pl.CostEstimate(flops=flops, bytes_accessed=moved, transcendentals=0),
    )


def on_device(u, v, t, s, water, layers, diag, elev):
    lon, lat = lax.axis_size("lon"), lax.axis_size("lat")
    lon_even = [(i, i ^ 1) for i in range(lon)]
    lon_odd = [(i, (((i + 1) ^ 1) - 1) % lon) for i in range(lon)]
    lat_even = [(i, i ^ 1) for i in range(lat)]
    lat_odd = [(i, ((i + 1) ^ 1) - 1) for i in range(1, lat - 1)]
    parity = jnp.stack([lax.axis_index("lon") % 2, lax.axis_index("lat") % 2]).astype(jnp.int32)

    smem = pl.BlockSpec(memory_space=pltpu.SMEM)
    whole = pl.BlockSpec(memory_space=pltpu.VMEM)
    block = 4 * LEVELS * ROWS * LANES * 4
    raw = (u, v, t, s, water, layers, diag, elev)

    own_odd, own_even = call(
        pack_lon, (shaped(LON_ROWS, LANES),) * 2, [whole] * 8 + [smem], 10**6, 2 * block
    )(*raw, parity)
    got_odd = lax.ppermute(own_odd, "lon", lon_odd)
    got_even = lax.ppermute(own_even, "lon", lon_even)
    lat_own_odd, lat_own_even, partial = call(
        pack_lat,
        (shaped(LAT_ROWS, LANES), shaped(LAT_ROWS, LANES), shaped(ROWS, LANES)),
        [whole] * 8 + [smem], 4 * 10**6, block,
    )(*raw, parity)
    lat_got_odd = lax.ppermute(lat_own_odd, "lat", lat_odd)
    lat_got_even = lax.ppermute(lat_own_even, "lat", lat_even)

    own2d, odd2d, even2d = (x[4 * STRIP :] for x in (own_odd, got_odd, got_even))
    b_odd, b_even = call(
        forcing, (shaped(SOLVE_ROWS, LANES),) * 2,
        [smem, part(STRIP), part(STRIP), part(2 * STRIP, 1), part(2 * STRIP, 1)] + [whole] * 6,
        10**6, 10**6, grid=(1,),
    )(
        parity, own_odd, own_even, got_odd, got_even, own2d,
        lat_own_odd, lat_own_even, lat_got_odd, lat_got_even, partial,
    )
    b_got_odd = lax.ppermute(b_odd, "lon", lon_odd)
    b_got_even = lax.ppermute(b_even, "lon", lon_even)

    fresh = call(
        fields, (shaped(LEVELS, ROWS, LANES),) * 4, [smem] + [whole] * 10, 10**7, 3 * block
    )(parity, u, v, t, s, water, layers, got_odd, got_even, lat_got_odd, lat_got_even)

    height = call(solve, shaped(ROWS, LANES), [smem] + [whole] * 8, 10**6, 10**6)(
        parity, own2d, odd2d, even2d, lat_got_odd, lat_got_even, b_odd, b_got_odd, b_got_even
    )
    return (*fresh, height)


def solution(mesh):
    field, flat = P(None, "lon", "lat"), P("lon", "lat")
    return jax.shard_map(
        on_device,
        mesh=mesh,
        in_specs=(field,) * 4 + (flat,) * 4,
        out_specs=(field,) * 4 + (flat,),
        check_vma=False,
    )
```

```python
import jax
import jax.numpy as jnp
from jax import lax
from jax.experimental import pallas as pl
from jax.experimental.pallas import tpu as pltpu
from jax.sharding import PartitionSpec as P

ITERS = 8
LEVELS = 62
SPECTRUM_MID = 1.0
SPECTRUM_HALF = 0.995

ROWS = 8
LANES = 128
STRIP = 128
FLAT = 4 * STRIP
LON_ROWS = FLAT + 3 * ROWS
LAT_ROWS = 17 * ROWS
SOLVE_ROWS = 5 * ROWS + 32 + 8
VMEM = 12 * 1024 * 1024

F32 = jnp.float32
ADV = 0.1 / 12.0


def rows_of(shape=(ROWS, LANES)):
    return lax.broadcasted_iota(jnp.int32, shape, 0)


def lanes_of(shape=(ROWS, LANES)):
    return lax.broadcasted_iota(jnp.int32, shape, 1)


def by_rows(x, d):
    d %= ROWS
    return pltpu.roll(x, d, 0) if d else x


def by_lanes(x, d):
    d %= LANES
    return pltpu.roll(x, d, 1) if d else x


def scalar_mix(t, s):
    return 0.7 * t - 0.5 * s


def even(axis):
    return lax.axis_index(axis) % 2 == 0


def pack_lon(
    u, v, t, s, water, layers, diag, elev, parity, masked, up_first, low_first, held, held_int, held_flat, sems
):
    copies = [
        pltpu.make_async_copy(src, held.at[i], sems.at[i]) for i, src in enumerate((u, v, t, s))
    ]
    small = [
        pltpu.make_async_copy(water, held_int.at[0], sems.at[4]),
        pltpu.make_async_copy(layers, held_int.at[1], sems.at[5]),
        pltpu.make_async_copy(elev, held_flat.at[0], sems.at[6]),
        pltpu.make_async_copy(diag, held_flat.at[1], sems.at[7]),
    ]
    for copy in small + copies:
        copy.start()
    for copy in small:
        copy.wait()
    row = rows_of()
    group = row >> 1
    depth = held_int[0] * held_int[1]
    is_even = parity[0] == 0
    for ref in (up_first, low_first):
        ref[FLAT : FLAT + 8, :] = held_flat[0]
        ref[FLAT + 8 : FLAT + 16, :] = held_flat[1]
        ref[FLAT + 16 : FLAT + 24, :] = depth.astype(F32)

    for f in range(4):
        masked[f, 0] = jnp.zeros((ROWS, LANES), F32)
        masked[f, LEVELS + 3] = jnp.zeros((ROWS, LANES), F32)
        copies[f].wait()

        def body(g, carry, f=f):
            top = bottom = None
            for i in range(4):
                k = 4 * g + i
                m = jnp.where(k < depth, held[f, jnp.minimum(k, LEVELS - 1)], 0.0)
                masked[f, k + 1] = m
                a, b = by_rows(m, 2 * i), by_rows(m, 2 * i - 6)
                top = a if i == 0 else jnp.where(group == i, a, top)
                bottom = b if i == 0 else jnp.where(group == i, b, bottom)
            at = pl.ds(pl.multiple_of(f * STRIP + 8 * g, 8), 8)
            up_first[at, :] = jnp.where(is_even, top, bottom)
            low_first[at, :] = jnp.where(is_even, bottom, top)
            return carry

        lax.fori_loop(0, 16, body, 0, unroll=4)


def flat_of(ref):
    return [ref[FLAT + 8 * i : FLAT + 8 * i + 8, :] for i in range(3)]


def pack_lat(masked, own_lon, parity, odd_out, even_out, partial):
    row, lane = rows_of(), lanes_of()
    slot = lane >> 3
    elev, diag, depth = flat_of(own_lon)
    levels = depth.astype(jnp.int32)
    is_even = parity[1] == 0

    def body(a, acc):
        left = [None] * 4
        right = [None] * 4
        for i in range(16):
            k = 16 * a + i
            wet = k < levels
            m = [masked[f, k + 1] for f in range(4)]
            for f in range(4):
                x, y = by_lanes(m[f], 8 * i), by_lanes(m[f], 8 * i - 120)
                left[f] = x if i == 0 else jnp.where(slot == i, x, left[f])
                right[f] = y if i == 0 else jnp.where(slot == i, y, right[f])
            w = scalar_mix(m[2], m[3])
            n1 = jnp.where(row < 7, by_rows(w, -1), 0.0)
            p1 = jnp.where(row > 0, by_rows(w, 1), 0.0)
            n2 = jnp.where(row < 6, by_rows(w, -2), 0.0)
            p2 = jnp.where(row > 1, by_rows(w, 2), 0.0)
            e1 = jnp.where(lane < 127, by_lanes(w, -1), 0.0)
            q1 = jnp.where(lane > 0, by_lanes(w, 1), 0.0)
            e2 = jnp.where(lane < 126, by_lanes(w, -2), 0.0)
            q2 = jnp.where(lane > 1, by_lanes(w, 2), 0.0)
            gx = 8.0 * (n1 - p1) - (n2 - p2)
            gy = 8.0 * (e1 - q1) - (e2 - q2)
            around = jnp.where(wet, (n1 + p1) + (e1 + q1), 0.0)
            column = jnp.where(k > 0, w, 0.0) + jnp.where(k + 1 < levels, w, 0.0)
            acc = acc + (
                0.94 * w + 0.02 * column + 0.005 * around - ADV * (m[0] * gx + m[1] * gy)
            )
        for f in range(4):
            where = pl.ds(pl.multiple_of(f * 32 + 8 * a, 8), 8)
            odd_out[where, :] = jnp.where(is_even, left[f], right[f])
            even_out[where, :] = jnp.where(is_even, right[f], left[f])
        return acc

    acc = 0.1 * lax.fori_loop(0, 4, body, jnp.zeros((ROWS, LANES), F32))
    partial[...] = acc
    flat = (acc, elev, diag, depth)
    left = right = None
    for i, x in enumerate(flat):
        a, b = by_lanes(x, 8 * i), by_lanes(x, 8 * i - 120)
        left = a if i == 0 else jnp.where(slot == i, a, left)
        right = b if i == 0 else jnp.where(slot == i, b, right)
    odd_out[128:136, :] = jnp.where(is_even, left, right)
    even_out[128:136, :] = jnp.where(is_even, right, left)


def tile_lanes(x):
    x = jnp.where(lanes_of() < 8, x, 0.0)
    for d in (8, 16, 32, 64):
        x = x + by_lanes(x, d)
    return x


def sum_slots(x):
    for d in (8, 16, 32, 64):
        x = x + by_lanes(x, d)
    return x


def wet_pack(depth, a):
    return (16 * a + (lanes_of() >> 3)).astype(F32) < depth


def lat_rims(a_v, a_w, a_depth, b_v, b_w, b_depth):
    column = lanes_of() & 7
    a_sum = b_sum = jnp.zeros((ROWS, LANES), F32)
    for i in range(4):
        y1, y2 = by_lanes(b_w[i], 7), by_lanes(b_w[i], 6)
        y1 = jnp.where(column == 7, y1, 0.0)
        y2 = jnp.where(column >= 6, y2, 0.0)
        a_sum = a_sum - ADV * a_v[i] * (8.0 * y1 - y2)
        a_sum = a_sum + 0.005 * jnp.where(wet_pack(a_depth, i), y1, 0.0)
        z1, z2 = by_lanes(a_w[i], -7), by_lanes(a_w[i], -6)
        z1 = jnp.where(column == 0, z1, 0.0)
        z2 = jnp.where(column <= 1, z2, 0.0)
        b_sum = b_sum - ADV * b_v[i] * (z2 - 8.0 * z1)
        b_sum = b_sum + 0.005 * jnp.where(wet_pack(b_depth, i), z1, 0.0)
    return 0.1 * sum_slots(a_sum), 0.1 * sum_slots(b_sum)


def pick(flag, a, b):
    return jnp.where(flag, a, b)


def four(ref, base, flag, other):
    at = [slice(base + 8 * i, base + 8 * i + 8) for i in range(4)]
    return [jnp.where(flag, ref[x, :], other[x, :]) for x in at]


def forcing(
    parity, got_even, got_odd, own_odd, own_even,
    own_odd_lat, own_even_lat, got_odd_lat, got_even_lat, partial,
    odd_out, even_out,
):
    row, lane = rows_of(), lanes_of()
    lon_even, lat_even = parity[0] == 0, parity[1] == 0
    elev, diag, depth = flat_of(own_odd)
    total = elev + partial[...]

    r = row & 1
    for lower in (True, False):
        rim = row < 2 if lower else row >= 6
        tiled = jnp.where(rim, depth, 0.0)
        tiled = tiled + by_rows(tiled, 2)
        tiled = tiled + by_rows(tiled, 4)
        acc = jnp.zeros((ROWS, LANES), F32)
        own_first = lon_even if lower else jnp.logical_not(lon_even)
        for g in range(16):
            at = slice(8 * g, 8 * g + 8)
            at_t = slice(2 * STRIP + 8 * g, 2 * STRIP + 8 * g + 8)
            at_s = slice(3 * STRIP + 8 * g, 3 * STRIP + 8 * g + 8)
            vel = jnp.where(own_first, own_odd[at, :], own_even[at, :])
            w = scalar_mix(
                jnp.where(own_first, got_odd[at_t, :], got_even[at_t, :]),
                jnp.where(own_first, got_odd[at_s, :], got_even[at_s, :]),
            )
            wet = (4 * g + (row >> 1)).astype(F32) < tiled
            if lower:
                near = jnp.where(r == 0, by_rows(w, -1), 0.0)
                slope = w - 8.0 * near
            else:
                near = jnp.where(r == 1, by_rows(w, 1), 0.0)
                slope = 8.0 * near - w
            acc = acc + (0.005 * jnp.where(wet, near, 0.0) - ADV * vel * slope)
        acc = acc + by_rows(acc, 2)
        acc = acc + by_rows(acc, 4)
        total = total + jnp.where(rim, 0.1 * acc, 0.0)

    own_r = [four(own_even_lat, f * 32, lat_even, own_odd_lat) for f in range(1, 4)]
    own_l = [four(own_odd_lat, f * 32, lat_even, own_even_lat) for f in range(1, 4)]
    ext_r = [four(got_even_lat, f * 32, lat_even, got_odd_lat) for f in range(4)]
    ext_l = [four(got_odd_lat, f * 32, lat_even, got_even_lat) for f in range(4)]
    flat_r = jnp.where(lat_even, got_even_lat[128:136, :], got_odd_lat[128:136, :])
    flat_l = jnp.where(lat_even, got_odd_lat[128:136, :], got_even_lat[128:136, :])

    def mixed(pair):
        return [scalar_mix(x, y) for x, y in zip(*pair, strict=True)]

    w_r, w_l = mixed(ext_r[2:]), mixed(ext_l[2:])
    miss_own_r, miss_ext_r = lat_rims(
        own_r[0], mixed(own_r[1:]), tile_lanes(by_lanes(depth, 8)),
        ext_r[1], w_r, tile_lanes(by_lanes(flat_r, -24)),
    )
    miss_ext_l, miss_own_l = lat_rims(
        ext_l[1], w_l, tile_lanes(by_lanes(flat_l, -24)),
        own_l[0], mixed(own_l[1:]), tile_lanes(depth),
    )
    total = total + jnp.where(lane >= 126, miss_own_r, 0.0) + jnp.where(lane < 2, miss_own_l, 0.0)

    def side(i):
        return jnp.where(
            lane < 8,
            by_lanes(flat_r, -8 * i),
            jnp.where(lane >= 120, by_lanes(flat_l, 120 - 8 * i), 0.0),
        )

    elev_side = side(1)
    total_side = side(0) + elev_side
    total_side = total_side + jnp.where(lane < 2, miss_ext_r, 0.0)
    total_side = total_side + jnp.where(lane >= 126, miss_ext_l, 0.0)
    for ref in (odd_out, even_out):
        for i, x in enumerate((total, total_side, elev_side, side(2), side(3))):
            ref[8 * i : 8 * i + 8, :] = x
        ref[SOLVE_ROWS - 8 : SOLVE_ROWS, :] = jnp.zeros((8, LANES), F32)
    packs = ext_r[0] + ext_l[0] + w_r + w_l
    group = row >> 1
    for i in range(4):
        top = bottom = None
        for j in range(4):
            x = packs[4 * i + j]
            a, b = by_rows(x, 2 * j), by_rows(x, 2 * j - 6)
            top = a if j == 0 else jnp.where(group == j, a, top)
            bottom = b if j == 0 else jnp.where(group == j, b, bottom)
        at = slice(40 + 8 * i, 48 + 8 * i)
        odd_out[at, :] = jnp.where(lon_even, top, bottom)
        even_out[at, :] = jnp.where(lon_even, bottom, top)


CHUNKS = ((0, 5), (5, 10), (10, 15))


def fields(
    parity, masked, own_lon, odd_lon, even_lon, odd_lat, even_lat, o1, o2, o3, o4, rims, fresh, sems
):
    row, lane = rows_of(), lanes_of()
    levels = flat_of(own_lon)[2].astype(jnp.int32)
    lon_even, lat_even = parity[0] == 0, parity[1] == 0
    outs = (o1, o2, o3, o4)

    def unpack(a, carry):
        for f in range(4):
            at = pl.ds(pl.multiple_of(f * 32 + 8 * a, 8), 8)
            x, y = odd_lat[at, :], even_lat[at, :]
            west, east = jnp.where(lat_even, x, y), jnp.where(lat_even, y, x)
            for i in range(16):
                rims[f, 16 * a + i] = jnp.where(
                    lane < 64, by_lanes(east, -8 * i), by_lanes(west, 120 - 8 * i)
                )
        return carry

    lax.fori_loop(0, 4, unpack, 0)

    def group(g, count):
        strips = []
        for f in range(4):
            at = pl.ds(pl.multiple_of(f * STRIP + 8 * g, 8), 8)
            x, y = odd_lon[at, :], even_lon[at, :]
            strips.append((jnp.where(lon_even, y, x), jnp.where(lon_even, x, y)))
        for j in range(count):
            k = 4 * g + j
            wet = k < levels
            center = [masked[f, k + 1] for f in range(4)]
            zonal, merid = ADV * center[0], ADV * center[1]
            for f in range(4):
                m = center[f]
                upper, lower = strips[f]
                rim = jnp.where(row < 4, by_rows(upper, -2 * j), by_rows(lower, 6 - 2 * j))
                n1 = by_rows(jnp.where(row < 1, rim, m), -1)
                n2 = by_rows(jnp.where(row < 2, rim, m), -2)
                p1 = by_rows(jnp.where(row > 6, rim, m), 1)
                p2 = by_rows(jnp.where(row > 5, rim, m), 2)
                beside = rims[f, k]
                e1 = by_lanes(jnp.where(lane < 1, beside, m), -1)
                e2 = by_lanes(jnp.where(lane < 2, beside, m), -2)
                q1 = by_lanes(jnp.where(lane > 126, beside, m), 1)
                q2 = by_lanes(jnp.where(lane > 125, beside, m), 2)
                gx = 8.0 * (n1 - p1) - (n2 - p2)
                gy = 8.0 * (e1 - q1) - (e2 - q2)
                around = (n1 + p1) + (e1 + q1)
                column = masked[f, k] + masked[f, k + 2]
                value = 0.94 * m + 0.02 * column + 0.005 * around - (zonal * gx + merid * gy)
                fresh[f, k] = jnp.where(wet, value, 0.0)

    def body(g, carry):
        group(g, 4)
        return carry

    copies = []

    def send(first, last):
        for f in range(4):
            copies.append(
                pltpu.make_async_copy(
                    fresh.at[f, first:last], outs[f].at[first:last], sems.at[len(copies)]
                )
            )
            copies[-1].start()

    for first, last in CHUNKS:
        lax.fori_loop(first, last, body, 0)
        send(4 * first, 4 * last)
    group(15, LEVELS - 60)
    send(60, LEVELS)
    for copy in copies:
        copy.wait()


def solve(
    parity, odd_b, even_b, own_b, own_lon, odd_lon, even_lon, odd_lat, even_lat, height
):
    row, lane = rows_of(), lanes_of()
    lon_even, lat_even = parity[0] == 0, parity[1] == 0
    lower = [jnp.where(lon_even, odd_b[8 * i : 8 * i + 8, :], even_b[8 * i : 8 * i + 8, :]) for i in range(10)]
    upper = [jnp.where(lon_even, even_b[8 * i : 8 * i + 8, :], odd_b[8 * i : 8 * i + 8, :]) for i in range(10)]
    own = [own_b[8 * i : 8 * i + 8, :] for i in range(5)]

    ext_r = [four(even_lat, f * 32, lat_even, odd_lat) for f in (0, 2, 3)]
    ext_l = [four(odd_lat, f * 32, lat_even, even_lat) for f in (0, 2, 3)]

    def lon_part(vel, wet, x1, x2):
        slope = jnp.where(row == 0, -8.0 * x1, jnp.where(row == 7, 8.0 * x1, 0.0))
        slope = slope + jnp.where(row < 2, x2, jnp.where(row >= 6, -x2, 0.0))
        near = jnp.where((row == 0) | (row == 7), x1, 0.0)
        return 0.005 * jnp.where(wet, near, 0.0) - ADV * vel * slope

    def rim_rows(tile, q, first):
        return by_rows(tile[5 + q // 4], first - 2 * (q % 4))

    def side_parts(ext, base, own_depth, near_depth):
        mine = theirs = jnp.zeros((ROWS, LANES), F32)
        for i in range(4):
            vel, w = ext[0][i], scalar_mix(ext[1][i], ext[2][i])
            qu, qw = base + i, 8 + base + i
            x2 = jnp.where(row < 4, rim_rows(lower, qw, 0), rim_rows(upper, qw, 6))
            x1 = jnp.where(row < 4, rim_rows(lower, qw, -1), rim_rows(upper, qw, 7))
            mine = mine + lon_part(vel, wet_pack(own_depth, i), x1, x2)
            y2 = jnp.where(row < 4, by_rows(w, 2), by_rows(w, -2))
            y1 = jnp.where(row < 4, by_rows(w, 1), by_rows(w, -1))
            other = jnp.where(row < 4, rim_rows(upper, qu, 0), rim_rows(lower, qu, 6))
            theirs = theirs + lon_part(other, wet_pack(near_depth, i), y1, y2)
        return 0.1 * sum_slots(mine), 0.1 * sum_slots(theirs)

    near_side = jnp.where(row < 4, upper[4], lower[4])
    mine_r, theirs_r = side_parts(ext_r, 0, tile_lanes(own[4]), tile_lanes(near_side))
    mine_l, theirs_l = side_parts(
        ext_l, 4, tile_lanes(by_lanes(own[4], 8)), tile_lanes(by_lanes(near_side, 8))
    )
    in_r, in_l = lane < 8, lane >= 120
    mine = jnp.where(in_r, mine_r, jnp.where(in_l, mine_l, 0.0))
    theirs = jnp.where(in_r, theirs_r, jnp.where(in_l, theirs_l, 0.0))

    flat_own = flat_of(own_lon)
    flat_odd, flat_even = flat_of(odd_lon), flat_of(even_lon)
    flat_low = [jnp.where(lon_even, x, y) for x, y in zip(flat_odd, flat_even, strict=True)]
    flat_up = [jnp.where(lon_even, y, x) for x, y in zip(flat_odd, flat_even, strict=True)]

    rhs = [
        lower[0], own[0], upper[0],
        lower[1] + jnp.where(row >= 6, theirs, 0.0),
        own[1] + mine,
        upper[1] + jnp.where(row < 2, theirs, 0.0),
    ]
    elev = [flat_low[0], flat_own[0], flat_up[0], lower[2], own[2], upper[2]]
    diag = [flat_low[1], flat_own[1], flat_up[1], lower[3], own[3], upper[3]]
    wet = [x > 0.0 for x in (flat_low[2], flat_own[2], flat_up[2], lower[4], own[4], upper[4])]
    diag = [x + 4.0 for x in diag]
    inverse = [1.0 / x for x in diag]
    coupled = [jnp.where(a, x, 0.0) for a, x in zip(wet, inverse, strict=True)]

    def neighbours(x):
        out = []
        up = [by_rows(y, -1) for y in x]
        down = [by_rows(y, 1) for y in x]
        east = [by_lanes(y, -1) for y in x]
        west = [by_lanes(y, 1) for y in x]
        for i in range(6):
            h, c = divmod(i, 3)
            base = 3 * h
            other = 3 * (1 - h) + c
            n = jnp.where(row < 7, up[i], up[base + (c + 1) % 3])
            p = jnp.where(row > 0, down[i], down[base + (c + 2) % 3])
            e = jnp.where(lane < 127, east[i], east[other])
            w = jnp.where(lane > 0, west[i], west[other])
            out.append((n + p) + (e + w))
        return out

    sigma = SPECTRUM_MID / SPECTRUM_HALF
    ratio = 1.0 / sigma
    scaled = [x * y for x, y in zip(rhs, inverse, strict=True)]
    previous = elev
    iterate = elev[1]
    for step in range(ITERS):
        around = neighbours([jnp.where(a, x, 0.0) for a, x in zip(wet, previous, strict=True)])
        scaled = [
            (res - x) + c * n
            for res, x, c, n in zip(scaled, previous, coupled, around, strict=True)
        ]
        if step == 0:
            previous = [res / SPECTRUM_MID for res in scaled]
        else:
            following = 1.0 / (2.0 * sigma - ratio)
            keep, gain = following * ratio, 2.0 * following / SPECTRUM_HALF
            previous = [keep * x + gain * res for x, res in zip(previous, scaled, strict=True)]
            ratio = following
        iterate = iterate + previous[1]
    height[...] = iterate


def shaped(*shape):
    return jax.ShapeDtypeStruct(shape, F32)


def call(kernel, outs, ins, flops, moved, **kw):
    return pl.pallas_call(
        kernel,
        out_shape=outs,
        in_specs=ins,
        compiler_params=pltpu.CompilerParams(vmem_limit_bytes=VMEM),
        cost_estimate=pl.CostEstimate(flops=flops, bytes_accessed=moved, transcendentals=0),
        **kw,
    )


SMEM = pl.BlockSpec(memory_space=pltpu.SMEM)
WHOLE = pl.BlockSpec(memory_space=pltpu.VMEM)
HERE = pl.BlockSpec(memory_space=pltpu.HBM)
BLOCK = 4 * LEVELS * ROWS * LANES * 4


def call_pack_lon(*args):
    return call(
        pack_lon,
        (shaped(4, LEVELS + 4, ROWS, LANES), shaped(LON_ROWS, LANES), shaped(LON_ROWS, LANES)),
        [HERE] * 8 + [SMEM], 10**6, 2 * BLOCK,
        out_specs=(WHOLE,) * 3,
        scratch_shapes=[
            pltpu.VMEM((4, LEVELS, ROWS, LANES), F32),
            pltpu.VMEM((2, ROWS, LANES), jnp.int32),
            pltpu.VMEM((2, ROWS, LANES), F32),
            pltpu.SemaphoreType.DMA((8,)),
        ],
    )(*args)


def call_pack_lat(*args):
    return call(
        pack_lat, (shaped(LAT_ROWS, LANES), shaped(LAT_ROWS, LANES), shaped(ROWS, LANES)),
        [WHOLE] * 2 + [SMEM], 4 * 10**6, BLOCK,
    )(*args)


def call_forcing(*args):
    return call(
        forcing, (shaped(SOLVE_ROWS, LANES),) * 2, [SMEM] + [WHOLE] * 9, 10**6, 10**6
    )(*args)


def call_fields(*args):
    return call(
        fields, (shaped(LEVELS, ROWS, LANES),) * 4, [SMEM] + [WHOLE] * 6, 10**7, 3 * BLOCK,
        out_specs=(HERE,) * 4,
        scratch_shapes=[
            pltpu.VMEM((4, LEVELS + 2, ROWS, LANES), F32),
            pltpu.VMEM((4, LEVELS, ROWS, LANES), F32),
            pltpu.SemaphoreType.DMA((16,)),
        ],
    )(*args)


def call_solve(*args):
    return call(solve, shaped(ROWS, LANES), [SMEM] + [WHOLE] * 8, 10**6, 10**6)(*args)


def on_device(u, v, t, s, water, layers, diag, elev):
    lon, lat = lax.axis_size("lon"), lax.axis_size("lat")
    lon_even = [(i, i ^ 1) for i in range(lon)]
    lon_odd = [(i, (((i + 1) ^ 1) - 1) % lon) for i in range(lon)]
    lat_even = [(i, i ^ 1) for i in range(lat)]
    lat_odd = [(i, ((i + 1) ^ 1) - 1) for i in range(1, lat - 1)]
    parity = jnp.stack([lax.axis_index("lon") & 1, lax.axis_index("lat") & 1]).astype(jnp.int32)

    raw = [
        pltpu.with_memory_space_constraint(x, pltpu.HBM)
        for x in (u, v, t, s, water, layers, diag, elev)
    ]
    masked, own_odd, own_even = call_pack_lon(*raw, parity)
    got_even = lax.ppermute(own_even, "lon", lon_even)
    got_odd = lax.ppermute(own_odd, "lon", lon_odd)
    lat_own_odd, lat_own_even, partial = call_pack_lat(masked, own_odd, parity)
    lat_got_odd = lax.ppermute(lat_own_odd, "lat", lat_odd)
    lat_got_even = lax.ppermute(lat_own_even, "lat", lat_even)

    b_odd, b_even = call_forcing(
        parity, got_even, got_odd, own_odd, own_even,
        lat_own_odd, lat_own_even, lat_got_odd, lat_got_even, partial,
    )
    b_got_odd = lax.ppermute(b_odd, "lon", lon_odd)
    b_got_even = lax.ppermute(b_even, "lon", lon_even)

    fresh = call_fields(parity, masked, own_odd, got_odd, got_even, lat_got_odd, lat_got_even)
    height = call_solve(
        parity, b_got_odd, b_got_even, b_odd, own_odd, got_odd, got_even, lat_got_odd, lat_got_even
    )
    return (*fresh, height)


def solution(mesh):
    field, flat = P(None, "lon", "lat"), P("lon", "lat")
    return jax.shard_map(
        on_device,
        mesh=mesh,
        in_specs=(field,) * 4 + (flat,) * 4,
        out_specs=(field,) * 4 + (flat,),
        check_vma=False,
    )
```

```python
import jax
import jax.numpy as jnp
from jax import lax
from jax.experimental import pallas as pl
from jax.experimental.pallas import tpu as pltpu
from jax.sharding import PartitionSpec as P

ITERS = 8
LEVELS = 62
SPECTRUM_MID = 1.0
SPECTRUM_HALF = 0.995

ROWS = 8
LANES = 128
STRIP = 128
FLAT = 4 * STRIP
LON_ROWS = FLAT + 3 * ROWS
LAT_ROWS = 18 * ROWS
SOLVE_ROWS = 5 * ROWS + 5 * ROWS
VMEM = 12 * 1024 * 1024

F32 = jnp.float32
ADV = 0.1 / 12.0


def rows_of(shape=(ROWS, LANES)):
    return lax.broadcasted_iota(jnp.int32, shape, 0)


def lanes_of(shape=(ROWS, LANES)):
    return lax.broadcasted_iota(jnp.int32, shape, 1)


def by_rows(x, d):
    d %= ROWS
    return pltpu.roll(x, d, 0) if d else x


def by_lanes(x, d):
    d %= LANES
    return pltpu.roll(x, d, 1) if d else x


def scalar_mix(t, s):
    return 0.7 * t - 0.5 * s


def even(axis):
    return lax.axis_index(axis) % 2 == 0


def flat_of(ref, base=FLAT):
    return [ref[base + 8 * i : base + 8 * i + 8, :] for i in range(3)]


def prepare(
    u, v, t, s, water, layers, diag, elev, parity,
    masked, odd_out, even_out, partial, flat, held, held_int, sems,
):
    small = [
        pltpu.make_async_copy(water, held_int.at[0], sems.at[0]),
        pltpu.make_async_copy(layers, held_int.at[1], sems.at[1]),
        pltpu.make_async_copy(elev, flat.at[0:8], sems.at[2]),
        pltpu.make_async_copy(diag, flat.at[8:16], sems.at[3]),
    ]
    chunks = []
    for a in range(4):
        at = slice(16 * a, min(16 * a + 16, LEVELS))
        chunks.append(
            [
                pltpu.make_async_copy(src.at[at], held.at[f, at], sems.at[4 + 4 * a + f])
                for f, src in enumerate((u, v, t, s))
            ]
        )
    for copy in small[:2] + [x for chunk in chunks for x in chunk] + small[2:]:
        copy.start()
    for copy in small[:2]:
        copy.wait()
    row, lane = rows_of(), lanes_of()
    high, low = lane >> 4, ((lane - 8) & 127) >> 4
    in_even = (lane & 8) == 0
    depth = held_int[0] * held_int[1]
    flat[16:24, :] = depth.astype(F32)
    is_even = parity[1] == 0
    zero = jnp.zeros((ROWS, LANES), F32)
    for f in range(4):
        for i in (0, LEVELS + 1, LEVELS + 2):
            masked[f, i] = zero

    def tile(a, sums, count=16):
        whole, inner, sides, flux = sums
        first, second = [zero] * 4, [zero] * 4
        for i in range(count):
            k = 16 * a + i
            wet = k < depth
            m = [jnp.where(wet, held[f, k], 0.0) for f in range(4)]
            for f in range(4):
                masked[f, k + 1] = m[f]
                if i < 8:
                    first[f] = jnp.where(high == i, by_lanes(m[f], 16 * i - 120), first[f])
                else:
                    second[f] = jnp.where(low == i - 8, by_lanes(m[f], 16 * i - 240), second[f])
            w = scalar_mix(m[2], m[3])
            n1 = jnp.where(row < 7, by_rows(w, -1), 0.0)
            p1 = jnp.where(row > 0, by_rows(w, 1), 0.0)
            n2 = jnp.where(row < 6, by_rows(w, -2), 0.0)
            p2 = jnp.where(row > 1, by_rows(w, 2), 0.0)
            e1 = jnp.where(lane < 127, by_lanes(w, -1), 0.0)
            q1 = jnp.where(lane > 0, by_lanes(w, 1), 0.0)
            e2 = jnp.where(lane < 126, by_lanes(w, -2), 0.0)
            q2 = jnp.where(lane > 1, by_lanes(w, 2), 0.0)
            gx = 8.0 * (n1 - p1) - (n2 - p2)
            gy = 8.0 * (e1 - q1) - (e2 - q2)
            whole = whole + w
            inner = inner + jnp.where(k + 1 < depth, w, 0.0)
            sides = sides + jnp.where(wet, (n1 + p1) + (e1 + q1), 0.0)
            flux = flux + (m[0] * gx + m[1] * gy)
        for f in range(4):
            right = jnp.where(in_even, first[f], second[f])
            left = by_lanes(jnp.where(in_even, second[f], first[f]), -8)
            where = pl.ds(pl.multiple_of(f * 32 + 8 * a, 8), 8)
            odd_out[where, :] = jnp.where(is_even, left, right)
            even_out[where, :] = jnp.where(is_even, right, left)
        return whole, inner, sides, flux

    def body(a, sums):
        for f, src in enumerate((u, v, t, s)):
            at = pl.ds(16 * a, 16)
            pltpu.make_async_copy(src.at[at], held.at[f, at], sems.at[4 + 4 * a + f]).wait()
        return tile(a, sums)

    sums = lax.fori_loop(0, 3, body, (zero,) * 4)
    for copy in chunks[3]:
        copy.wait()
    whole, inner, sides, flux = tile(3, sums, LEVELS - 48)
    top = scalar_mix(masked[2, 1], masked[3, 1])
    acc = 0.1 * (0.94 * whole + 0.02 * (whole - top + inner) + 0.005 * sides - ADV * flux)
    partial[...] = acc
    for copy in small[2:]:
        copy.wait()
    slot = lane >> 3
    depth = depth.astype(F32)
    left = right = zero
    for i, x in enumerate((acc, flat[0:8, :], flat[8:16, :], depth)):
        left = jnp.where(slot == i, by_lanes(x, 8 * i), left)
        right = jnp.where(slot == i, by_lanes(x, 8 * i - 120), right)
    odd_out[128:136, :] = jnp.where(is_even, left, right)
    even_out[128:136, :] = jnp.where(is_even, right, left)
    left, right = tile_lanes(depth), tile_lanes(by_lanes(depth, 8))
    odd_out[136:144, :] = jnp.where(is_even, left, right)
    even_out[136:144, :] = jnp.where(is_even, right, left)


def pack_lon(masked, flat, after, parity, odd_out, even_out):
    group = rows_of() >> 1
    is_even = parity[0] == 0
    for ref in (odd_out, even_out):
        ref[FLAT : FLAT + 24, :] = flat[...]

    def body(g, carry):
        for f in range(4):
            top = bottom = None
            for i in range(4):
                m = masked[f, 4 * g + i + 1]
                a, b = by_rows(m, 2 * i), by_rows(m, 2 * i - 6)
                top = a if i == 0 else jnp.where(group == i, a, top)
                bottom = b if i == 0 else jnp.where(group == i, b, bottom)
            at = pl.ds(pl.multiple_of(f * STRIP + 8 * g, 8), 8)
            odd_out[at, :] = jnp.where(is_even, top, bottom)
            even_out[at, :] = jnp.where(is_even, bottom, top)
        return carry

    lax.fori_loop(0, 16, body, 0, unroll=2)


def tile_lanes(x):
    x = jnp.where(lanes_of() < 8, x, 0.0)
    for d in (8, 16, 32, 64):
        x = x + by_lanes(x, d)
    return x


def sum_slots(x):
    for d in (8, 16, 32, 64):
        x = x + by_lanes(x, d)
    return x


def wet_pack(depth, a):
    slot = lanes_of() >> 3
    return (16 * a + (slot >> 1) + 8 * (slot & 1)).astype(F32) < depth


def lat_rims(a_v, a_w, a_depth, b_v, b_w, b_depth):
    column = lanes_of() & 7
    a_sum = b_sum = jnp.zeros((ROWS, LANES), F32)
    for i in range(4):
        y1, y2 = by_lanes(b_w[i], 7), by_lanes(b_w[i], 6)
        y1 = jnp.where(column == 7, y1, 0.0)
        y2 = jnp.where(column >= 6, y2, 0.0)
        a_sum = a_sum - ADV * a_v[i] * (8.0 * y1 - y2)
        a_sum = a_sum + 0.005 * jnp.where(wet_pack(a_depth, i), y1, 0.0)
        z1, z2 = by_lanes(a_w[i], -7), by_lanes(a_w[i], -6)
        z1 = jnp.where(column == 0, z1, 0.0)
        z2 = jnp.where(column <= 1, z2, 0.0)
        b_sum = b_sum - ADV * b_v[i] * (z2 - 8.0 * z1)
        b_sum = b_sum + 0.005 * jnp.where(wet_pack(b_depth, i), z1, 0.0)
    return 0.1 * sum_slots(a_sum), 0.1 * sum_slots(b_sum)


def pick(flag, a, b):
    return jnp.where(flag, a, b)


def four(ref, base, flag, other):
    at = [slice(base + 8 * i, base + 8 * i + 8) for i in range(4)]
    return [jnp.where(flag, ref[x, :], other[x, :]) for x in at]


def forcing(
    parity, got_even, got_odd, own_odd, own_even,
    own_odd_lat, own_even_lat, got_odd_lat, got_even_lat, partial,
    odd_out, even_out,
):
    row, lane = rows_of(), lanes_of()
    lon_even, lat_even = parity[0] == 0, parity[1] == 0
    elev, diag, depth = flat_of(own_odd)
    total = elev + partial[...]

    r = row & 1
    for lower in (True, False):
        rim = row < 2 if lower else row >= 6
        tiled = jnp.where(rim, depth, 0.0)
        tiled = tiled + by_rows(tiled, 2)
        tiled = tiled + by_rows(tiled, 4)
        acc = jnp.zeros((ROWS, LANES), F32)
        own_first = lon_even if lower else jnp.logical_not(lon_even)
        for g in range(16):
            at = slice(8 * g, 8 * g + 8)
            at_t = slice(2 * STRIP + 8 * g, 2 * STRIP + 8 * g + 8)
            at_s = slice(3 * STRIP + 8 * g, 3 * STRIP + 8 * g + 8)
            vel = jnp.where(own_first, own_odd[at, :], own_even[at, :])
            w = scalar_mix(
                jnp.where(own_first, got_odd[at_t, :], got_even[at_t, :]),
                jnp.where(own_first, got_odd[at_s, :], got_even[at_s, :]),
            )
            wet = (4 * g + (row >> 1)).astype(F32) < tiled
            if lower:
                near = jnp.where(r == 0, by_rows(w, -1), 0.0)
                slope = w - 8.0 * near
            else:
                near = jnp.where(r == 1, by_rows(w, 1), 0.0)
                slope = 8.0 * near - w
            acc = acc + (0.005 * jnp.where(wet, near, 0.0) - ADV * vel * slope)
        acc = acc + by_rows(acc, 2)
        acc = acc + by_rows(acc, 4)
        total = total + jnp.where(rim, 0.1 * acc, 0.0)

    own_r = [four(own_even_lat, f * 32, lat_even, own_odd_lat) for f in range(1, 4)]
    own_l = [four(own_odd_lat, f * 32, lat_even, own_even_lat) for f in range(1, 4)]
    ext_r = [four(got_even_lat, f * 32, lat_even, got_odd_lat) for f in range(4)]
    ext_l = [four(got_odd_lat, f * 32, lat_even, got_even_lat) for f in range(4)]
    flat_r = jnp.where(lat_even, got_even_lat[128:136, :], got_odd_lat[128:136, :])
    flat_l = jnp.where(lat_even, got_odd_lat[128:136, :], got_even_lat[128:136, :])
    depth_r = jnp.where(lat_even, got_even_lat[136:144, :], got_odd_lat[136:144, :])
    depth_l = jnp.where(lat_even, got_odd_lat[136:144, :], got_even_lat[136:144, :])
    own_depth_r = jnp.where(lat_even, own_even_lat[136:144, :], own_odd_lat[136:144, :])
    own_depth_l = jnp.where(lat_even, own_odd_lat[136:144, :], own_even_lat[136:144, :])

    def mixed(pair):
        return [scalar_mix(x, y) for x, y in zip(*pair, strict=True)]

    w_r, w_l = mixed(ext_r[2:]), mixed(ext_l[2:])
    miss_own_r, miss_ext_r = lat_rims(
        own_r[0], mixed(own_r[1:]), own_depth_r, ext_r[1], w_r, depth_r
    )
    miss_ext_l, miss_own_l = lat_rims(
        ext_l[1], w_l, depth_l, own_l[0], mixed(own_l[1:]), own_depth_l
    )
    total = total + jnp.where(lane >= 126, miss_own_r, 0.0) + jnp.where(lane < 2, miss_own_l, 0.0)

    def side(i):
        return jnp.where(
            lane < 8,
            by_lanes(flat_r, -8 * i),
            jnp.where(lane >= 120, by_lanes(flat_l, 120 - 8 * i), 0.0),
        )

    elev_side = side(1)
    total_side = side(0) + elev_side
    total_side = total_side + jnp.where(lane < 2, miss_ext_r, 0.0)
    total_side = total_side + jnp.where(lane >= 126, miss_ext_l, 0.0)
    for ref in (odd_out, even_out):
        for i, x in enumerate((total, total_side, elev_side, side(2), side(3))):
            ref[8 * i : 8 * i + 8, :] = x
    packs = ext_r[0] + ext_l[0] + w_r + w_l + [depth_r, depth_l]
    group = row >> 1
    for i in range(5):
        top = bottom = jnp.zeros((ROWS, LANES), F32)
        for j, x in enumerate(packs[4 * i : 4 * i + 4]):
            top = jnp.where(group == j, by_rows(x, 2 * j), top)
            bottom = jnp.where(group == j, by_rows(x, 2 * j - 6), bottom)
        at = slice(40 + 8 * i, 48 + 8 * i)
        odd_out[at, :] = jnp.where(lon_even, top, bottom)
        even_out[at, :] = jnp.where(lon_even, bottom, top)


CHUNKS = ((0, 5), (5, 10), (10, 15))


def fields(
    parity, masked, own_lon, odd_lon, even_lon, odd_lat, even_lat, o1, o2, o3, o4, rims, fresh, sems
):
    row, lane = rows_of(), lanes_of()
    levels = flat_of(own_lon)[2].astype(jnp.int32)
    lon_even, lat_even = parity[0] == 0, parity[1] == 0
    outs = (o1, o2, o3, o4)

    in_even = (lane & 8) == 0

    def unpack(a, carry):
        for f in range(4):
            at = pl.ds(pl.multiple_of(f * 32 + 8 * a, 8), 8)
            x, y = odd_lat[at, :], even_lat[at, :]
            west = jnp.where(lat_even, x, y)
            east = by_lanes(jnp.where(lat_even, y, x), 8)
            first = jnp.where(in_even, west, east)
            second = jnp.where(in_even, east, west)
            for i in range(8):
                rims[f, 16 * a + i] = by_lanes(first, -16 * i - 8)
                rims[f, 16 * a + 8 + i] = by_lanes(second, -16 * i - 16)
        return carry

    lax.fori_loop(0, 4, unpack, 0)

    def group(g, count):
        strips = []
        for f in range(4):
            at = pl.ds(pl.multiple_of(f * STRIP + 8 * g, 8), 8)
            x, y = odd_lon[at, :], even_lon[at, :]
            strips.append((jnp.where(lon_even, y, x), jnp.where(lon_even, x, y)))
        for j in range(count):
            k = 4 * g + j
            wet = k < levels
            center = [masked[f, k + 1] for f in range(4)]
            zonal, merid = ADV * center[0], ADV * center[1]
            for f in range(4):
                m = center[f]
                upper, lower = strips[f]
                rim = jnp.where(row < 4, by_rows(upper, -2 * j), by_rows(lower, 6 - 2 * j))
                n1 = by_rows(jnp.where(row < 1, rim, m), -1)
                n2 = by_rows(jnp.where(row < 2, rim, m), -2)
                p1 = by_rows(jnp.where(row > 6, rim, m), 1)
                p2 = by_rows(jnp.where(row > 5, rim, m), 2)
                beside = rims[f, k]
                e1 = by_lanes(jnp.where(lane < 1, beside, m), -1)
                e2 = by_lanes(jnp.where(lane < 2, beside, m), -2)
                q1 = by_lanes(jnp.where(lane > 126, beside, m), 1)
                q2 = by_lanes(jnp.where(lane > 125, beside, m), 2)
                gx = 8.0 * (n1 - p1) - (n2 - p2)
                gy = 8.0 * (e1 - q1) - (e2 - q2)
                around = (n1 + p1) + (e1 + q1)
                column = masked[f, k] + masked[f, k + 2]
                value = 0.94 * m + 0.02 * column + 0.005 * around - (zonal * gx + merid * gy)
                fresh[f, k] = jnp.where(wet, value, 0.0)

    def body(g, carry):
        group(g, 4)
        return carry

    copies = []

    def send(first, last):
        for f in range(4):
            copies.append(
                pltpu.make_async_copy(
                    fresh.at[f, first:last], outs[f].at[first:last], sems.at[len(copies)]
                )
            )
            copies[-1].start()

    for first, last in CHUNKS:
        lax.fori_loop(first, last, body, 0)
        send(4 * first, 4 * last)
    group(15, LEVELS - 60)
    send(60, LEVELS)
    for copy in copies:
        copy.wait()


def solve(
    parity, odd_b, even_b, own_b, own_lon, odd_lon, even_lon, odd_lat, even_lat, height
):
    row, lane = rows_of(), lanes_of()
    lon_even, lat_even = parity[0] == 0, parity[1] == 0
    lower = [jnp.where(lon_even, odd_b[8 * i : 8 * i + 8, :], even_b[8 * i : 8 * i + 8, :]) for i in range(10)]
    upper = [jnp.where(lon_even, even_b[8 * i : 8 * i + 8, :], odd_b[8 * i : 8 * i + 8, :]) for i in range(10)]
    own = [own_b[8 * i : 8 * i + 8, :] for i in range(5)]

    ext_r = [four(even_lat, f * 32, lat_even, odd_lat) for f in (0, 2, 3)]
    ext_l = [four(odd_lat, f * 32, lat_even, even_lat) for f in (0, 2, 3)]

    def lon_part(vel, wet, x1, x2):
        slope = jnp.where(row == 0, -8.0 * x1, jnp.where(row == 7, 8.0 * x1, 0.0))
        slope = slope + jnp.where(row < 2, x2, jnp.where(row >= 6, -x2, 0.0))
        near = jnp.where((row == 0) | (row == 7), x1, 0.0)
        return 0.005 * jnp.where(wet, near, 0.0) - ADV * vel * slope

    def rim_rows(tile, q, first):
        return by_rows(tile[5 + q // 4], first - 2 * (q % 4))

    def near_rows(q):
        return jnp.where(row < 4, rim_rows(upper, q, 0), rim_rows(lower, q, 6))

    def side_parts(ext, base, own_depth, near_depth):
        mine = theirs = jnp.zeros((ROWS, LANES), F32)
        for i in range(4):
            vel, w = ext[0][i], scalar_mix(ext[1][i], ext[2][i])
            qu, qw = base + i, 8 + base + i
            x2 = jnp.where(row < 4, rim_rows(lower, qw, 0), rim_rows(upper, qw, 6))
            x1 = jnp.where(row < 4, rim_rows(lower, qw, -1), rim_rows(upper, qw, 7))
            mine = mine + lon_part(vel, wet_pack(own_depth, i), x1, x2)
            y2 = jnp.where(row < 4, by_rows(w, 2), by_rows(w, -2))
            y1 = jnp.where(row < 4, by_rows(w, 1), by_rows(w, -1))
            theirs = theirs + lon_part(near_rows(qu), wet_pack(near_depth, i), y1, y2)
        return 0.1 * sum_slots(mine), 0.1 * sum_slots(theirs)

    depth_r = jnp.where(lat_even, even_lat[136:144, :], odd_lat[136:144, :])
    depth_l = jnp.where(lat_even, odd_lat[136:144, :], even_lat[136:144, :])
    mine_r, theirs_r = side_parts(ext_r, 0, depth_r, near_rows(16))
    mine_l, theirs_l = side_parts(ext_l, 4, depth_l, near_rows(17))
    in_r, in_l = lane < 8, lane >= 120
    mine = jnp.where(in_r, mine_r, jnp.where(in_l, mine_l, 0.0))
    theirs = jnp.where(in_r, theirs_r, jnp.where(in_l, theirs_l, 0.0))

    flat_own = flat_of(own_lon)
    flat_odd, flat_even = flat_of(odd_lon), flat_of(even_lon)
    flat_low = [jnp.where(lon_even, x, y) for x, y in zip(flat_odd, flat_even, strict=True)]
    flat_up = [jnp.where(lon_even, y, x) for x, y in zip(flat_odd, flat_even, strict=True)]

    rhs = [
        lower[0], own[0], upper[0],
        lower[1] + jnp.where(row >= 6, theirs, 0.0),
        own[1] + mine,
        upper[1] + jnp.where(row < 2, theirs, 0.0),
    ]
    elev = [flat_low[0], flat_own[0], flat_up[0], lower[2], own[2], upper[2]]
    diag = [flat_low[1], flat_own[1], flat_up[1], lower[3], own[3], upper[3]]
    wet = [x > 0.0 for x in (flat_low[2], flat_own[2], flat_up[2], lower[4], own[4], upper[4])]
    diag = [x + 4.0 for x in diag]
    inverse = [1.0 / x for x in diag]
    coupled = [jnp.where(a, x, 0.0) for a, x in zip(wet, inverse, strict=True)]

    def neighbours(x):
        out = []
        up = [by_rows(y, -1) for y in x]
        down = [by_rows(y, 1) for y in x]
        east = [by_lanes(y, -1) for y in x]
        west = [by_lanes(y, 1) for y in x]
        for i in range(6):
            h, c = divmod(i, 3)
            base = 3 * h
            other = 3 * (1 - h) + c
            n = jnp.where(row < 7, up[i], up[base + (c + 1) % 3])
            p = jnp.where(row > 0, down[i], down[base + (c + 2) % 3])
            e = jnp.where(lane < 127, east[i], east[other])
            w = jnp.where(lane > 0, west[i], west[other])
            out.append((n + p) + (e + w))
        return out

    sigma = SPECTRUM_MID / SPECTRUM_HALF
    ratio = 1.0 / sigma
    scaled = [x * y for x, y in zip(rhs, inverse, strict=True)]
    previous = elev
    iterate = elev[1]
    for step in range(ITERS):
        around = neighbours([jnp.where(a, x, 0.0) for a, x in zip(wet, previous, strict=True)])
        scaled = [
            (res - x) + c * n
            for res, x, c, n in zip(scaled, previous, coupled, around, strict=True)
        ]
        if step == 0:
            previous = [res / SPECTRUM_MID for res in scaled]
        else:
            following = 1.0 / (2.0 * sigma - ratio)
            keep, gain = following * ratio, 2.0 * following / SPECTRUM_HALF
            previous = [keep * x + gain * res for x, res in zip(previous, scaled, strict=True)]
            ratio = following
        iterate = iterate + previous[1]
    height[...] = iterate


def shaped(*shape):
    return jax.ShapeDtypeStruct(shape, F32)


def call(kernel, outs, ins, flops, moved, **kw):
    return pl.pallas_call(
        kernel,
        out_shape=outs,
        in_specs=ins,
        compiler_params=pltpu.CompilerParams(vmem_limit_bytes=VMEM),
        cost_estimate=pl.CostEstimate(flops=flops, bytes_accessed=moved, transcendentals=0),
        **kw,
    )


SMEM = pl.BlockSpec(memory_space=pltpu.SMEM)
WHOLE = pl.BlockSpec(memory_space=pltpu.VMEM)
HERE = pl.BlockSpec(memory_space=pltpu.HBM)
BLOCK = 4 * LEVELS * ROWS * LANES * 4


def call_prepare(*args):
    return call(
        prepare,
        (
            shaped(4, LEVELS + 3, ROWS, LANES), shaped(LAT_ROWS, LANES), shaped(LAT_ROWS, LANES),
            shaped(ROWS, LANES), shaped(3 * ROWS, LANES),
        ),
        [HERE] * 8 + [SMEM], 10**7, BLOCK,
        out_specs=(WHOLE,) * 5,
        scratch_shapes=[
            pltpu.VMEM((4, LEVELS, ROWS, LANES), F32),
            pltpu.VMEM((2, ROWS, LANES), jnp.int32),
            pltpu.SemaphoreType.DMA((20,)),
        ],
    )(*args)


def call_pack_lon(*args):
    return call(
        pack_lon, (shaped(LON_ROWS, LANES),) * 2,
        [WHOLE, WHOLE, pl.BlockSpec(memory_space=pl.ANY), SMEM], 10**6, 10**6,
    )(*args)


def call_forcing(*args):
    return call(
        forcing, (shaped(SOLVE_ROWS, LANES),) * 2, [SMEM] + [WHOLE] * 9, 10**6, 10**6
    )(*args)


def call_fields(*args):
    return call(
        fields, (shaped(LEVELS, ROWS, LANES),) * 4, [SMEM] + [WHOLE] * 6, 10**7, 3 * BLOCK,
        out_specs=(HERE,) * 4,
        scratch_shapes=[
            pltpu.VMEM((4, LEVELS + 2, ROWS, LANES), F32),
            pltpu.VMEM((4, LEVELS, ROWS, LANES), F32),
            pltpu.SemaphoreType.DMA((16,)),
        ],
    )(*args)


def call_solve(*args):
    return call(solve, shaped(ROWS, LANES), [SMEM] + [WHOLE] * 8, 10**6, 10**6)(*args)


def exchanges(lon, lat):
    def pairs(size, first, around):
        last = size if around else size - 1
        return [(i, (i + 1) % size) for i in range(first, last, 2)]

    def over_lon(first):
        return [
            (x * lat + j, y * lat + j)
            for a, b in pairs(lon, first, True)
            for x, y in ((a, b), (b, a))
            for j in range(lat)
        ]

    def over_lat(first, rows):
        return [
            (i * lat + x, i * lat + y)
            for i in rows
            for a, b in pairs(lat, first, False)
            for x, y in ((a, b), (b, a))
        ]

    return over_lon, over_lat


RUN, EARLY = 8, 4


def on_device(u, v, t, s, water, layers, diag, elev):
    lon, lat = lax.axis_size("lon"), lax.axis_size("lat")
    over_lon, over_lat = exchanges(lon, lat)
    early = [i for i in range(lon) if i % RUN < EARLY]
    late = [i for i in range(lon) if i % RUN >= EARLY]
    both = ("lon", "lat")
    parity = jnp.stack([lax.axis_index("lon") & 1, lax.axis_index("lat") & 1]).astype(jnp.int32)

    raw = [
        pltpu.with_memory_space_constraint(x, pltpu.HBM)
        for x in (u, v, t, s, water, layers, diag, elev)
    ]
    masked, lat_own_odd, lat_own_even, partial, flat = call_prepare(*raw, parity)
    lat_early = lax.ppermute(lat_own_odd, both, over_lat(1, early))
    own_odd, own_even = call_pack_lon(masked, flat, lat_early, parity)
    got_even = lax.ppermute(own_even, both, over_lon(0))
    got_odd = lax.ppermute(own_odd, both, over_lon(1))
    lat_got_even = lax.ppermute(lat_own_even, both, over_lat(0, range(lon)))
    lat_late = lax.ppermute(lat_own_odd, both, over_lat(1, late))
    lat_got_odd = lat_early + lat_late

    b_odd, b_even = call_forcing(
        parity, got_even, got_odd, own_odd, own_even,
        lat_own_odd, lat_own_even, lat_got_odd, lat_got_even, partial,
    )
    b_got_odd = lax.ppermute(b_odd, both, over_lon(1))
    b_got_even = lax.ppermute(b_even, both, over_lon(0))

    fresh = call_fields(parity, masked, own_odd, got_odd, got_even, lat_got_odd, lat_got_even)
    height = call_solve(
        parity, b_got_odd, b_got_even, b_odd, own_odd, got_odd, got_even, lat_got_odd, lat_got_even
    )
    return (*fresh, height)


def solution(mesh):
    field, flat = P(None, "lon", "lat"), P("lon", "lat")
    return jax.shard_map(
        on_device,
        mesh=mesh,
        in_specs=(field,) * 4 + (flat,) * 4,
        out_specs=(field,) * 4 + (flat,),
        check_vma=False,
    )
```

```python
import jax
import jax.numpy as jnp
from jax import lax
from jax.experimental import pallas as pl
from jax.experimental.pallas import tpu as pltpu
from jax.sharding import PartitionSpec as P

ITERS = 8
LEVELS = 62
SPECTRUM_MID = 1.0
SPECTRUM_HALF = 0.995

ROWS = 8
LANES = 128
STRIP = 128
FLAT = 4 * STRIP
LON_ROWS = FLAT + 3 * ROWS
LAT_ROWS = 18 * ROWS
SOLVE_ROWS = 5 * ROWS + 5 * ROWS
VMEM = 12 * 1024 * 1024

F32 = jnp.float32
ADV = 0.1 / 12.0


def rows_of(shape=(ROWS, LANES)):
    return lax.broadcasted_iota(jnp.int32, shape, 0)


def lanes_of(shape=(ROWS, LANES)):
    return lax.broadcasted_iota(jnp.int32, shape, 1)


def by_rows(x, d):
    d %= ROWS
    return pltpu.roll(x, d, 0) if d else x


def by_lanes(x, d):
    d %= LANES
    return pltpu.roll(x, d, 1) if d else x


def scalar_mix(t, s):
    return 0.7 * t - 0.5 * s


def even(axis):
    return lax.axis_index(axis) % 2 == 0


def flat_of(ref, base=FLAT):
    return [ref[base + 8 * i : base + 8 * i + 8, :] for i in range(3)]


def pack_lon(
    u, v, t, s, water, layers, diag, elev, parity, masked, up_first, low_first, held, held_int, held_flat, sems
):
    copies = [
        pltpu.make_async_copy(src, held.at[i], sems.at[i]) for i, src in enumerate((u, v, t, s))
    ]
    small = [
        pltpu.make_async_copy(water, held_int.at[0], sems.at[4]),
        pltpu.make_async_copy(layers, held_int.at[1], sems.at[5]),
        pltpu.make_async_copy(elev, held_flat.at[0], sems.at[6]),
        pltpu.make_async_copy(diag, held_flat.at[1], sems.at[7]),
    ]
    for copy in small[:2] + copies + small[2:]:
        copy.start()
    for copy in small[:2]:
        copy.wait()
    row = rows_of()
    group = row >> 1
    depth = held_int[0] * held_int[1]
    is_even = parity[0] == 0

    for f in range(4):
        masked[f, 0] = jnp.zeros((ROWS, LANES), F32)
        masked[f, LEVELS + 3] = jnp.zeros((ROWS, LANES), F32)
        copies[f].wait()

        def body(g, carry, f=f):
            top = bottom = None
            for i in range(4):
                k = 4 * g + i
                m = jnp.where(k < depth, held[f, jnp.minimum(k, LEVELS - 1)], 0.0)
                masked[f, k + 1] = m
                a, b = by_rows(m, 2 * i), by_rows(m, 2 * i - 6)
                top = a if i == 0 else jnp.where(group == i, a, top)
                bottom = b if i == 0 else jnp.where(group == i, b, bottom)
            at = pl.ds(pl.multiple_of(f * STRIP + 8 * g, 8), 8)
            up_first[at, :] = jnp.where(is_even, top, bottom)
            low_first[at, :] = jnp.where(is_even, bottom, top)
            return carry

        lax.fori_loop(0, 16, body, 0, unroll=4)

    for copy in small[2:]:
        copy.wait()
    for ref in (up_first, low_first):
        ref[FLAT : FLAT + 8, :] = held_flat[0]
        ref[FLAT + 8 : FLAT + 16, :] = held_flat[1]
        ref[FLAT + 16 : FLAT + 24, :] = depth.astype(F32)


def pack_lat(masked, own_lon, parity, odd_out, even_out, partial):
    row, lane = rows_of(), lanes_of()
    high, low = lane >> 4, ((lane - 8) & 127) >> 4
    in_even = (lane & 8) == 0
    elev, diag, depth = flat_of(own_lon)
    levels = depth.astype(jnp.int32)
    is_even = parity[1] == 0
    zero = jnp.zeros((ROWS, LANES), F32)

    def tile(a, sums):
        whole, inner, sides, flux = sums
        first, second = [zero] * 4, [zero] * 4
        for i in range(16):
            k = 16 * a + i
            m = [masked[f, k + 1] for f in range(4)]
            for f in range(4):
                if i < 8:
                    first[f] = jnp.where(high == i, by_lanes(m[f], 16 * i - 120), first[f])
                else:
                    second[f] = jnp.where(low == i - 8, by_lanes(m[f], 16 * i - 240), second[f])
            w = scalar_mix(m[2], m[3])
            n1 = jnp.where(row < 7, by_rows(w, -1), 0.0)
            p1 = jnp.where(row > 0, by_rows(w, 1), 0.0)
            n2 = jnp.where(row < 6, by_rows(w, -2), 0.0)
            p2 = jnp.where(row > 1, by_rows(w, 2), 0.0)
            e1 = jnp.where(lane < 127, by_lanes(w, -1), 0.0)
            q1 = jnp.where(lane > 0, by_lanes(w, 1), 0.0)
            e2 = jnp.where(lane < 126, by_lanes(w, -2), 0.0)
            q2 = jnp.where(lane > 1, by_lanes(w, 2), 0.0)
            gx = 8.0 * (n1 - p1) - (n2 - p2)
            gy = 8.0 * (e1 - q1) - (e2 - q2)
            whole = whole + w
            inner = inner + jnp.where(k + 1 < levels, w, 0.0)
            sides = sides + jnp.where(k < levels, (n1 + p1) + (e1 + q1), 0.0)
            flux = flux + (m[0] * gx + m[1] * gy)
        for f in range(4):
            right = jnp.where(in_even, first[f], second[f])
            left = by_lanes(jnp.where(in_even, second[f], first[f]), -8)
            where = pl.ds(pl.multiple_of(f * 32 + 8 * a, 8), 8)
            odd_out[where, :] = jnp.where(is_even, left, right)
            even_out[where, :] = jnp.where(is_even, right, left)
        return whole, inner, sides, flux

    whole, inner, sides, flux = lax.fori_loop(0, 4, tile, (zero,) * 4)
    top = scalar_mix(masked[2, 1], masked[3, 1])
    acc = 0.1 * (0.94 * whole + 0.02 * (whole - top + inner) + 0.005 * sides - ADV * flux)
    partial[...] = acc
    slot = lane >> 3
    left = right = zero
    for i, x in enumerate((acc, elev, diag, depth)):
        left = jnp.where(slot == i, by_lanes(x, 8 * i), left)
        right = jnp.where(slot == i, by_lanes(x, 8 * i - 120), right)
    odd_out[128:136, :] = jnp.where(is_even, left, right)
    even_out[128:136, :] = jnp.where(is_even, right, left)
    left, right = tile_lanes(depth), tile_lanes(by_lanes(depth, 8))
    odd_out[136:144, :] = jnp.where(is_even, left, right)
    even_out[136:144, :] = jnp.where(is_even, right, left)


def tile_lanes(x):
    x = jnp.where(lanes_of() < 8, x, 0.0)
    for d in (8, 16, 32, 64):
        x = x + by_lanes(x, d)
    return x


def sum_slots(x):
    for d in (8, 16, 32, 64):
        x = x + by_lanes(x, d)
    return x


def wet_pack(depth, a):
    slot = lanes_of() >> 3
    return (16 * a + (slot >> 1) + 8 * (slot & 1)).astype(F32) < depth


def lat_rims(a_v, a_w, a_depth, b_v, b_w, b_depth):
    column = lanes_of() & 7
    a_sum = b_sum = jnp.zeros((ROWS, LANES), F32)
    for i in range(4):
        y1, y2 = by_lanes(b_w[i], 7), by_lanes(b_w[i], 6)
        y1 = jnp.where(column == 7, y1, 0.0)
        y2 = jnp.where(column >= 6, y2, 0.0)
        a_sum = a_sum - ADV * a_v[i] * (8.0 * y1 - y2)
        a_sum = a_sum + 0.005 * jnp.where(wet_pack(a_depth, i), y1, 0.0)
        z1, z2 = by_lanes(a_w[i], -7), by_lanes(a_w[i], -6)
        z1 = jnp.where(column == 0, z1, 0.0)
        z2 = jnp.where(column <= 1, z2, 0.0)
        b_sum = b_sum - ADV * b_v[i] * (z2 - 8.0 * z1)
        b_sum = b_sum + 0.005 * jnp.where(wet_pack(b_depth, i), z1, 0.0)
    return 0.1 * sum_slots(a_sum), 0.1 * sum_slots(b_sum)


def pick(flag, a, b):
    return jnp.where(flag, a, b)


def four(ref, base, flag, other):
    at = [slice(base + 8 * i, base + 8 * i + 8) for i in range(4)]
    return [jnp.where(flag, ref[x, :], other[x, :]) for x in at]


def forcing(
    parity, got_even, got_odd, own_odd, own_even,
    own_odd_lat, own_even_lat, got_odd_lat, got_even_lat, partial,
    odd_out, even_out,
):
    row, lane = rows_of(), lanes_of()
    lon_even, lat_even = parity[0] == 0, parity[1] == 0
    elev, diag, depth = flat_of(own_odd)
    total = elev + partial[...]

    r = row & 1
    for lower in (True, False):
        rim = row < 2 if lower else row >= 6
        tiled = jnp.where(rim, depth, 0.0)
        tiled = tiled + by_rows(tiled, 2)
        tiled = tiled + by_rows(tiled, 4)
        acc = jnp.zeros((ROWS, LANES), F32)
        own_first = lon_even if lower else jnp.logical_not(lon_even)
        for g in range(16):
            at = slice(8 * g, 8 * g + 8)
            at_t = slice(2 * STRIP + 8 * g, 2 * STRIP + 8 * g + 8)
            at_s = slice(3 * STRIP + 8 * g, 3 * STRIP + 8 * g + 8)
            vel = jnp.where(own_first, own_odd[at, :], own_even[at, :])
            w = scalar_mix(
                jnp.where(own_first, got_odd[at_t, :], got_even[at_t, :]),
                jnp.where(own_first, got_odd[at_s, :], got_even[at_s, :]),
            )
            wet = (4 * g + (row >> 1)).astype(F32) < tiled
            if lower:
                near = jnp.where(r == 0, by_rows(w, -1), 0.0)
                slope = w - 8.0 * near
            else:
                near = jnp.where(r == 1, by_rows(w, 1), 0.0)
                slope = 8.0 * near - w
            acc = acc + (0.005 * jnp.where(wet, near, 0.0) - ADV * vel * slope)
        acc = acc + by_rows(acc, 2)
        acc = acc + by_rows(acc, 4)
        total = total + jnp.where(rim, 0.1 * acc, 0.0)

    own_r = [four(own_even_lat, f * 32, lat_even, own_odd_lat) for f in range(1, 4)]
    own_l = [four(own_odd_lat, f * 32, lat_even, own_even_lat) for f in range(1, 4)]
    ext_r = [four(got_even_lat, f * 32, lat_even, got_odd_lat) for f in range(4)]
    ext_l = [four(got_odd_lat, f * 32, lat_even, got_even_lat) for f in range(4)]
    flat_r = jnp.where(lat_even, got_even_lat[128:136, :], got_odd_lat[128:136, :])
    flat_l = jnp.where(lat_even, got_odd_lat[128:136, :], got_even_lat[128:136, :])
    depth_r = jnp.where(lat_even, got_even_lat[136:144, :], got_odd_lat[136:144, :])
    depth_l = jnp.where(lat_even, got_odd_lat[136:144, :], got_even_lat[136:144, :])
    own_depth_r = jnp.where(lat_even, own_even_lat[136:144, :], own_odd_lat[136:144, :])
    own_depth_l = jnp.where(lat_even, own_odd_lat[136:144, :], own_even_lat[136:144, :])

    def mixed(pair):
        return [scalar_mix(x, y) for x, y in zip(*pair, strict=True)]

    w_r, w_l = mixed(ext_r[2:]), mixed(ext_l[2:])
    miss_own_r, miss_ext_r = lat_rims(
        own_r[0], mixed(own_r[1:]), own_depth_r, ext_r[1], w_r, depth_r
    )
    miss_ext_l, miss_own_l = lat_rims(
        ext_l[1], w_l, depth_l, own_l[0], mixed(own_l[1:]), own_depth_l
    )
    total = total + jnp.where(lane >= 126, miss_own_r, 0.0) + jnp.where(lane < 2, miss_own_l, 0.0)

    def side(i):
        return jnp.where(
            lane < 8,
            by_lanes(flat_r, -8 * i),
            jnp.where(lane >= 120, by_lanes(flat_l, 120 - 8 * i), 0.0),
        )

    elev_side = side(1)
    total_side = side(0) + elev_side
    total_side = total_side + jnp.where(lane < 2, miss_ext_r, 0.0)
    total_side = total_side + jnp.where(lane >= 126, miss_ext_l, 0.0)
    for ref in (odd_out, even_out):
        for i, x in enumerate((total, total_side, elev_side, side(2), side(3))):
            ref[8 * i : 8 * i + 8, :] = x
    packs = ext_r[0] + ext_l[0] + w_r + w_l + [depth_r, depth_l]
    group = row >> 1
    for i in range(5):
        top = bottom = jnp.zeros((ROWS, LANES), F32)
        for j, x in enumerate(packs[4 * i : 4 * i + 4]):
            top = jnp.where(group == j, by_rows(x, 2 * j), top)
            bottom = jnp.where(group == j, by_rows(x, 2 * j - 6), bottom)
        at = slice(40 + 8 * i, 48 + 8 * i)
        odd_out[at, :] = jnp.where(lon_even, top, bottom)
        even_out[at, :] = jnp.where(lon_even, bottom, top)


CHUNKS = ((0, 5), (5, 10), (10, 15))


def fields(
    parity, masked, own_lon, odd_lon, even_lon, odd_lat, even_lat, o1, o2, o3, o4, rims, fresh, sems
):
    row, lane = rows_of(), lanes_of()
    levels = flat_of(own_lon)[2].astype(jnp.int32)
    lon_even, lat_even = parity[0] == 0, parity[1] == 0
    outs = (o1, o2, o3, o4)

    in_even = (lane & 8) == 0

    def unpack(a, carry):
        for f in range(4):
            at = pl.ds(pl.multiple_of(f * 32 + 8 * a, 8), 8)
            x, y = odd_lat[at, :], even_lat[at, :]
            west = jnp.where(lat_even, x, y)
            east = by_lanes(jnp.where(lat_even, y, x), 8)
            first = jnp.where(in_even, west, east)
            second = jnp.where(in_even, east, west)
            for i in range(8):
                rims[f, 16 * a + i] = by_lanes(first, -16 * i - 8)
                rims[f, 16 * a + 8 + i] = by_lanes(second, -16 * i - 16)
        return carry

    lax.fori_loop(0, 4, unpack, 0)

    def group(g, count):
        strips = []
        for f in range(4):
            at = pl.ds(pl.multiple_of(f * STRIP + 8 * g, 8), 8)
            x, y = odd_lon[at, :], even_lon[at, :]
            strips.append((jnp.where(lon_even, y, x), jnp.where(lon_even, x, y)))
        for j in range(count):
            k = 4 * g + j
            wet = k < levels
            center = [masked[f, k + 1] for f in range(4)]
            zonal, merid = ADV * center[0], ADV * center[1]
            for f in range(4):
                m = center[f]
                upper, lower = strips[f]
                rim = jnp.where(row < 4, by_rows(upper, -2 * j), by_rows(lower, 6 - 2 * j))
                n1 = by_rows(jnp.where(row < 1, rim, m), -1)
                n2 = by_rows(jnp.where(row < 2, rim, m), -2)
                p1 = by_rows(jnp.where(row > 6, rim, m), 1)
                p2 = by_rows(jnp.where(row > 5, rim, m), 2)
                beside = rims[f, k]
                e1 = by_lanes(jnp.where(lane < 1, beside, m), -1)
                e2 = by_lanes(jnp.where(lane < 2, beside, m), -2)
                q1 = by_lanes(jnp.where(lane > 126, beside, m), 1)
                q2 = by_lanes(jnp.where(lane > 125, beside, m), 2)
                gx = 8.0 * (n1 - p1) - (n2 - p2)
                gy = 8.0 * (e1 - q1) - (e2 - q2)
                around = (n1 + p1) + (e1 + q1)
                column = masked[f, k] + masked[f, k + 2]
                value = 0.94 * m + 0.02 * column + 0.005 * around - (zonal * gx + merid * gy)
                fresh[f, k] = jnp.where(wet, value, 0.0)

    def body(g, carry):
        group(g, 4)
        return carry

    copies = []

    def send(first, last):
        for f in range(4):
            copies.append(
                pltpu.make_async_copy(
                    fresh.at[f, first:last], outs[f].at[first:last], sems.at[len(copies)]
                )
            )
            copies[-1].start()

    for first, last in CHUNKS:
        lax.fori_loop(first, last, body, 0)
        send(4 * first, 4 * last)
    group(15, LEVELS - 60)
    send(60, LEVELS)
    for copy in copies:
        copy.wait()


def solve(
    parity, odd_b, even_b, own_b, own_lon, odd_lon, even_lon, odd_lat, even_lat, height
):
    row, lane = rows_of(), lanes_of()
    lon_even, lat_even = parity[0] == 0, parity[1] == 0
    lower = [jnp.where(lon_even, odd_b[8 * i : 8 * i + 8, :], even_b[8 * i : 8 * i + 8, :]) for i in range(10)]
    upper = [jnp.where(lon_even, even_b[8 * i : 8 * i + 8, :], odd_b[8 * i : 8 * i + 8, :]) for i in range(10)]
    own = [own_b[8 * i : 8 * i + 8, :] for i in range(5)]

    ext_r = [four(even_lat, f * 32, lat_even, odd_lat) for f in (0, 2, 3)]
    ext_l = [four(odd_lat, f * 32, lat_even, even_lat) for f in (0, 2, 3)]

    def lon_part(vel, wet, x1, x2):
        slope = jnp.where(row == 0, -8.0 * x1, jnp.where(row == 7, 8.0 * x1, 0.0))
        slope = slope + jnp.where(row < 2, x2, jnp.where(row >= 6, -x2, 0.0))
        near = jnp.where((row == 0) | (row == 7), x1, 0.0)
        return 0.005 * jnp.where(wet, near, 0.0) - ADV * vel * slope

    def rim_rows(tile, q, first):
        return by_rows(tile[5 + q // 4], first - 2 * (q % 4))

    def near_rows(q):
        return jnp.where(row < 4, rim_rows(upper, q, 0), rim_rows(lower, q, 6))

    def side_parts(ext, base, own_depth, near_depth):
        mine = theirs = jnp.zeros((ROWS, LANES), F32)
        for i in range(4):
            vel, w = ext[0][i], scalar_mix(ext[1][i], ext[2][i])
            qu, qw = base + i, 8 + base + i
            x2 = jnp.where(row < 4, rim_rows(lower, qw, 0), rim_rows(upper, qw, 6))
            x1 = jnp.where(row < 4, rim_rows(lower, qw, -1), rim_rows(upper, qw, 7))
            mine = mine + lon_part(vel, wet_pack(own_depth, i), x1, x2)
            y2 = jnp.where(row < 4, by_rows(w, 2), by_rows(w, -2))
            y1 = jnp.where(row < 4, by_rows(w, 1), by_rows(w, -1))
            theirs = theirs + lon_part(near_rows(qu), wet_pack(near_depth, i), y1, y2)
        return 0.1 * sum_slots(mine), 0.1 * sum_slots(theirs)

    depth_r = jnp.where(lat_even, even_lat[136:144, :], odd_lat[136:144, :])
    depth_l = jnp.where(lat_even, odd_lat[136:144, :], even_lat[136:144, :])
    mine_r, theirs_r = side_parts(ext_r, 0, depth_r, near_rows(16))
    mine_l, theirs_l = side_parts(ext_l, 4, depth_l, near_rows(17))
    in_r, in_l = lane < 8, lane >= 120
    mine = jnp.where(in_r, mine_r, jnp.where(in_l, mine_l, 0.0))
    theirs = jnp.where(in_r, theirs_r, jnp.where(in_l, theirs_l, 0.0))

    flat_own = flat_of(own_lon)
    flat_odd, flat_even = flat_of(odd_lon), flat_of(even_lon)
    flat_low = [jnp.where(lon_even, x, y) for x, y in zip(flat_odd, flat_even, strict=True)]
    flat_up = [jnp.where(lon_even, y, x) for x, y in zip(flat_odd, flat_even, strict=True)]

    rhs = [
        lower[0], own[0], upper[0],
        lower[1] + jnp.where(row >= 6, theirs, 0.0),
        own[1] + mine,
        upper[1] + jnp.where(row < 2, theirs, 0.0),
    ]
    elev = [flat_low[0], flat_own[0], flat_up[0], lower[2], own[2], upper[2]]
    diag = [flat_low[1], flat_own[1], flat_up[1], lower[3], own[3], upper[3]]
    wet = [x > 0.0 for x in (flat_low[2], flat_own[2], flat_up[2], lower[4], own[4], upper[4])]
    diag = [x + 4.0 for x in diag]
    inverse = [1.0 / x for x in diag]
    coupled = [jnp.where(a, x, 0.0) for a, x in zip(wet, inverse, strict=True)]

    def neighbours(x):
        out = []
        up = [by_rows(y, -1) for y in x]
        down = [by_rows(y, 1) for y in x]
        east = [by_lanes(y, -1) for y in x]
        west = [by_lanes(y, 1) for y in x]
        for i in range(6):
            h, c = divmod(i, 3)
            base = 3 * h
            other = 3 * (1 - h) + c
            n = jnp.where(row < 7, up[i], up[base + (c + 1) % 3])
            p = jnp.where(row > 0, down[i], down[base + (c + 2) % 3])
            e = jnp.where(lane < 127, east[i], east[other])
            w = jnp.where(lane > 0, west[i], west[other])
            out.append((n + p) + (e + w))
        return out

    sigma = SPECTRUM_MID / SPECTRUM_HALF
    ratio = 1.0 / sigma
    scaled = [x * y for x, y in zip(rhs, inverse, strict=True)]
    previous = elev
    iterate = elev[1]
    for step in range(ITERS):
        around = neighbours([jnp.where(a, x, 0.0) for a, x in zip(wet, previous, strict=True)])
        scaled = [
            (res - x) + c * n
            for res, x, c, n in zip(scaled, previous, coupled, around, strict=True)
        ]
        if step == 0:
            previous = [res / SPECTRUM_MID for res in scaled]
        else:
            following = 1.0 / (2.0 * sigma - ratio)
            keep, gain = following * ratio, 2.0 * following / SPECTRUM_HALF
            previous = [keep * x + gain * res for x, res in zip(previous, scaled, strict=True)]
            ratio = following
        iterate = iterate + previous[1]
    height[...] = iterate


def shaped(*shape):
    return jax.ShapeDtypeStruct(shape, F32)


def call(kernel, outs, ins, flops, moved, **kw):
    return pl.pallas_call(
        kernel,
        out_shape=outs,
        in_specs=ins,
        compiler_params=pltpu.CompilerParams(vmem_limit_bytes=VMEM),
        cost_estimate=pl.CostEstimate(flops=flops, bytes_accessed=moved, transcendentals=0),
        **kw,
    )


SMEM = pl.BlockSpec(memory_space=pltpu.SMEM)
WHOLE = pl.BlockSpec(memory_space=pltpu.VMEM)
HERE = pl.BlockSpec(memory_space=pltpu.HBM)
BLOCK = 4 * LEVELS * ROWS * LANES * 4


def call_pack_lon(*args):
    return call(
        pack_lon,
        (shaped(4, LEVELS + 4, ROWS, LANES), shaped(LON_ROWS, LANES), shaped(LON_ROWS, LANES)),
        [HERE] * 8 + [SMEM], 10**6, 2 * BLOCK,
        out_specs=(WHOLE,) * 3,
        scratch_shapes=[
            pltpu.VMEM((4, LEVELS, ROWS, LANES), F32),
            pltpu.VMEM((2, ROWS, LANES), jnp.int32),
            pltpu.VMEM((2, ROWS, LANES), F32),
            pltpu.SemaphoreType.DMA((8,)),
        ],
    )(*args)


def call_pack_lat(*args):
    return call(
        pack_lat, (shaped(LAT_ROWS, LANES), shaped(LAT_ROWS, LANES), shaped(ROWS, LANES)),
        [WHOLE] * 2 + [SMEM], 4 * 10**6, BLOCK,
    )(*args)


def call_forcing(*args):
    return call(
        forcing, (shaped(SOLVE_ROWS, LANES),) * 2, [SMEM] + [WHOLE] * 9, 10**6, 10**6
    )(*args)


def call_fields(*args):
    return call(
        fields, (shaped(LEVELS, ROWS, LANES),) * 4, [SMEM] + [WHOLE] * 6, 10**7, 3 * BLOCK,
        out_specs=(HERE,) * 4,
        scratch_shapes=[
            pltpu.VMEM((4, LEVELS + 2, ROWS, LANES), F32),
            pltpu.VMEM((4, LEVELS, ROWS, LANES), F32),
            pltpu.SemaphoreType.DMA((16,)),
        ],
    )(*args)


def call_solve(*args):
    return call(solve, shaped(ROWS, LANES), [SMEM] + [WHOLE] * 8, 10**6, 10**6)(*args)


def on_device(u, v, t, s, water, layers, diag, elev):
    lon, lat = lax.axis_size("lon"), lax.axis_size("lat")
    lon_even = [(i, i ^ 1) for i in range(lon)]
    lon_odd = [(i, (((i + 1) ^ 1) - 1) % lon) for i in range(lon)]
    lat_even = [(i, i ^ 1) for i in range(lat)]
    lat_odd = [(i, ((i + 1) ^ 1) - 1) for i in range(1, lat - 1)]
    parity = jnp.stack([lax.axis_index("lon") & 1, lax.axis_index("lat") & 1]).astype(jnp.int32)

    raw = [
        pltpu.with_memory_space_constraint(x, pltpu.HBM)
        for x in (u, v, t, s, water, layers, diag, elev)
    ]
    masked, own_odd, own_even = call_pack_lon(*raw, parity)
    got_even = lax.ppermute(own_even, "lon", lon_even)
    got_odd = lax.ppermute(own_odd, "lon", lon_odd)
    lat_own_odd, lat_own_even, partial = call_pack_lat(masked, own_odd, parity)
    lat_got_odd = lax.ppermute(lat_own_odd, "lat", lat_odd)
    lat_got_even = lax.ppermute(lat_own_even, "lat", lat_even)

    b_odd, b_even = call_forcing(
        parity, got_even, got_odd, own_odd, own_even,
        lat_own_odd, lat_own_even, lat_got_odd, lat_got_even, partial,
    )
    b_got_odd = lax.ppermute(b_odd, "lon", lon_odd)
    b_got_even = lax.ppermute(b_even, "lon", lon_even)

    fresh = call_fields(parity, masked, own_odd, got_odd, got_even, lat_got_odd, lat_got_even)
    height = call_solve(
        parity, b_got_odd, b_got_even, b_odd, own_odd, got_odd, got_even, lat_got_odd, lat_got_even
    )
    return (*fresh, height)


def solution(mesh):
    field, flat = P(None, "lon", "lat"), P("lon", "lat")
    return jax.shard_map(
        on_device,
        mesh=mesh,
        in_specs=(field,) * 4 + (flat,) * 4,
        out_specs=(field,) * 4 + (flat,),
        check_vma=False,
    )
```

```python
import jax
import jax.numpy as jnp
from jax import lax
from jax.experimental import pallas as pl
from jax.experimental.pallas import tpu as pltpu
from jax.sharding import PartitionSpec as P

ITERS = 8
LEVELS = 62
SPECTRUM_MID = 1.0
SPECTRUM_HALF = 0.995

ROWS = 8
LANES = 128
STRIP = 128
FLAT = 4 * STRIP
LON_ROWS = FLAT + 3 * ROWS
LAT_ROWS = 18 * ROWS
SOLVE_ROWS = 5 * ROWS + 5 * ROWS
VMEM = 12 * 1024 * 1024

F32 = jnp.float32
ADV = 0.1 / 12.0


def rows_of(shape=(ROWS, LANES)):
    return lax.broadcasted_iota(jnp.int32, shape, 0)


def lanes_of(shape=(ROWS, LANES)):
    return lax.broadcasted_iota(jnp.int32, shape, 1)


def by_rows(x, d):
    d %= ROWS
    return pltpu.roll(x, d, 0) if d else x


def by_lanes(x, d):
    d %= LANES
    return pltpu.roll(x, d, 1) if d else x


def scalar_mix(t, s):
    return 0.7 * t - 0.5 * s


def even(axis):
    return lax.axis_index(axis) % 2 == 0


def flat_of(ref, base=FLAT):
    return [ref[base + 8 * i : base + 8 * i + 8, :] for i in range(3)]


def pack_lon(
    u, v, t, s, water, layers, diag, elev, parity, masked, up_first, low_first, held, held_int, held_flat, sems
):
    copies = [
        pltpu.make_async_copy(src, held.at[i], sems.at[i]) for i, src in enumerate((u, v, t, s))
    ]
    small = [
        pltpu.make_async_copy(water, held_int.at[0], sems.at[4]),
        pltpu.make_async_copy(layers, held_int.at[1], sems.at[5]),
        pltpu.make_async_copy(elev, held_flat.at[0], sems.at[6]),
        pltpu.make_async_copy(diag, held_flat.at[1], sems.at[7]),
    ]
    for copy in small[:2] + copies + small[2:]:
        copy.start()
    for copy in small[:2]:
        copy.wait()
    row = rows_of()
    group = row >> 1
    depth = held_int[0] * held_int[1]
    is_even = parity[0] == 0

    for f in range(4):
        masked[f, 0] = jnp.zeros((ROWS, LANES), F32)
        masked[f, LEVELS + 3] = jnp.zeros((ROWS, LANES), F32)
        copies[f].wait()

        def body(g, carry, f=f):
            top = bottom = None
            for i in range(4):
                k = 4 * g + i
                m = jnp.where(k < depth, held[f, jnp.minimum(k, LEVELS - 1)], 0.0)
                masked[f, k + 1] = m
                a, b = by_rows(m, 2 * i), by_rows(m, 2 * i - 6)
                top = a if i == 0 else jnp.where(group == i, a, top)
                bottom = b if i == 0 else jnp.where(group == i, b, bottom)
            at = pl.ds(pl.multiple_of(f * STRIP + 8 * g, 8), 8)
            up_first[at, :] = jnp.where(is_even, top, bottom)
            low_first[at, :] = jnp.where(is_even, bottom, top)
            return carry

        lax.fori_loop(0, 16, body, 0, unroll=True)

    for copy in small[2:]:
        copy.wait()
    for ref in (up_first, low_first):
        ref[FLAT : FLAT + 8, :] = held_flat[0]
        ref[FLAT + 8 : FLAT + 16, :] = held_flat[1]
        ref[FLAT + 16 : FLAT + 24, :] = depth.astype(F32)


BF16 = jnp.bfloat16


def lat_matrix():
    shape = (2 * LANES, 2 * LANES)
    source = rows_of(shape) & 127
    target = lanes_of(shape)
    d = source - (target & 127)
    slope = jnp.where(d == 1, 8.0, jnp.where(d == -1, -8.0, 0.0))
    slope = slope + jnp.where(d == 2, -1.0, jnp.where(d == -2, 1.0, 0.0))
    near = jnp.where(jnp.abs(d) == 1, 1.0, 0.0)
    return jnp.where(target < LANES, slope, near).astype(BF16)


def lat_terms(x, matrix):
    high = x.astype(BF16)
    rest = (x - high.astype(F32)).astype(BF16)
    return jnp.dot(jnp.concatenate([high, rest], axis=1), matrix, preferred_element_type=F32)


def pack_lat(masked, own_lon, parity, odd_out, even_out, partial):
    row, lane = rows_of(), lanes_of()
    high, low = lane >> 4, ((lane - 8) & 127) >> 4
    in_even = (lane & 8) == 0
    elev, diag, depth = flat_of(own_lon)
    levels = depth.astype(jnp.int32)
    is_even = parity[1] == 0
    zero = jnp.zeros((ROWS, LANES), F32)
    matrix = lat_matrix()
    left, right = tile_lanes(depth), tile_lanes(by_lanes(depth, 8))
    odd_out[136:144, :] = jnp.where(is_even, left, right)
    even_out[136:144, :] = jnp.where(is_even, right, left)

    def tile(a, sums):
        whole, inner, sides, flux = sums
        first, second = [zero] * 4, [zero] * 4
        tracer = [
            scalar_mix(masked[2, 16 * a + i + 1], masked[3, 16 * a + i + 1]) for i in range(16)
        ]
        terms = lat_terms(jnp.concatenate(tracer, axis=0), matrix)
        for i in range(16):
            k = 16 * a + i
            m = [masked[f, k + 1] for f in range(4)]
            for f in range(4):
                if i < 8:
                    first[f] = jnp.where(high == i, by_lanes(m[f], 16 * i - 120), first[f])
                else:
                    second[f] = jnp.where(low == i - 8, by_lanes(m[f], 16 * i - 240), second[f])
            w = tracer[i]
            n1 = jnp.where(row < 7, by_rows(w, -1), 0.0)
            p1 = jnp.where(row > 0, by_rows(w, 1), 0.0)
            n2 = jnp.where(row < 6, by_rows(w, -2), 0.0)
            p2 = jnp.where(row > 1, by_rows(w, 2), 0.0)
            gx = 8.0 * (n1 - p1) - (n2 - p2)
            gy = terms[8 * i : 8 * i + 8, :LANES]
            around = (n1 + p1) + terms[8 * i : 8 * i + 8, LANES:]
            whole = whole + w
            inner = inner + jnp.where(k + 1 < levels, w, 0.0)
            sides = sides + jnp.where(k < levels, around, 0.0)
            flux = flux + (m[0] * gx + m[1] * gy)
        for f in range(4):
            right = jnp.where(in_even, first[f], second[f])
            left = by_lanes(jnp.where(in_even, second[f], first[f]), -8)
            where = pl.ds(pl.multiple_of(f * 32 + 8 * a, 8), 8)
            odd_out[where, :] = jnp.where(is_even, left, right)
            even_out[where, :] = jnp.where(is_even, right, left)
        return whole, inner, sides, flux

    whole, inner, sides, flux = lax.fori_loop(0, 4, tile, (zero,) * 4, unroll=True)
    top = scalar_mix(masked[2, 1], masked[3, 1])
    acc = 0.1 * (0.94 * whole + 0.02 * (whole - top + inner) + 0.005 * sides - ADV * flux)
    partial[...] = acc
    slot = lane >> 3
    left = right = zero
    for i, x in enumerate((acc, elev, diag, depth)):
        left = jnp.where(slot == i, by_lanes(x, 8 * i), left)
        right = jnp.where(slot == i, by_lanes(x, 8 * i - 120), right)
    odd_out[128:136, :] = jnp.where(is_even, left, right)
    even_out[128:136, :] = jnp.where(is_even, right, left)


def tile_lanes(x):
    return sum_slots(jnp.where(lanes_of() < 8, x, 0.0))


def sum_slots(x):
    for d in (8, 32):
        x = (x + by_lanes(x, d)) + (by_lanes(x, 2 * d) + by_lanes(x, 3 * d))
    return x


def wet_pack(depth, a):
    slot = lanes_of() >> 3
    return (16 * a + (slot >> 1) + 8 * (slot & 1)).astype(F32) < depth


def west_part(vel, depth, east, i):
    column = lanes_of() & 7
    y1 = jnp.where(column == 7, by_lanes(east, 7), 0.0)
    y2 = jnp.where(column >= 6, by_lanes(east, 6), 0.0)
    return 0.005 * jnp.where(wet_pack(depth, i), y1, 0.0) - ADV * vel * (8.0 * y1 - y2)


def east_part(vel, depth, west, i):
    column = lanes_of() & 7
    z1 = jnp.where(column == 0, by_lanes(west, -7), 0.0)
    z2 = jnp.where(column <= 1, by_lanes(west, -6), 0.0)
    return 0.005 * jnp.where(wet_pack(depth, i), z1, 0.0) - ADV * vel * (z2 - 8.0 * z1)


def lat_rims(a_v, a_w, a_depth, b_v, b_w, b_depth):
    a_sum = b_sum = jnp.zeros((ROWS, LANES), F32)
    for i in range(4):
        a_sum = a_sum + west_part(a_v[i], a_depth, b_w[i], i)
        b_sum = b_sum + east_part(b_v[i], b_depth, a_w[i], i)
    return 0.1 * sum_slots(a_sum), 0.1 * sum_slots(b_sum)


def four(ref, base, flag, other):
    at = [slice(base + 8 * i, base + 8 * i + 8) for i in range(4)]
    return [jnp.where(flag, ref[x, :], other[x, :]) for x in at]


def forcing(
    parity, got_even, got_odd, own_odd, own_even,
    own_odd_lat, own_even_lat, got_odd_lat, got_even_lat, partial,
    odd_out, even_out,
):
    row, lane = rows_of(), lanes_of()
    lon_even, lat_even = parity[0] == 0, parity[1] == 0
    elev, diag, depth = flat_of(own_odd)
    total = elev + partial[...]

    r = row & 1
    for lower in (True, False):
        rim = row < 2 if lower else row >= 6
        tiled = jnp.where(rim, depth, 0.0)
        tiled = tiled + by_rows(tiled, 2)
        tiled = tiled + by_rows(tiled, 4)
        acc = jnp.zeros((ROWS, LANES), F32)
        own_first = lon_even if lower else jnp.logical_not(lon_even)
        for g in range(16):
            at = slice(8 * g, 8 * g + 8)
            at_t = slice(2 * STRIP + 8 * g, 2 * STRIP + 8 * g + 8)
            at_s = slice(3 * STRIP + 8 * g, 3 * STRIP + 8 * g + 8)
            vel = jnp.where(own_first, own_odd[at, :], own_even[at, :])
            w = scalar_mix(
                jnp.where(own_first, got_odd[at_t, :], got_even[at_t, :]),
                jnp.where(own_first, got_odd[at_s, :], got_even[at_s, :]),
            )
            wet = (4 * g + (row >> 1)).astype(F32) < tiled
            if lower:
                near = jnp.where(r == 0, by_rows(w, -1), 0.0)
                slope = w - 8.0 * near
            else:
                near = jnp.where(r == 1, by_rows(w, 1), 0.0)
                slope = 8.0 * near - w
            acc = acc + (0.005 * jnp.where(wet, near, 0.0) - ADV * vel * slope)
        acc = acc + by_rows(acc, 2)
        acc = acc + by_rows(acc, 4)
        total = total + jnp.where(rim, 0.1 * acc, 0.0)

    own_r = [four(own_even_lat, f * 32, lat_even, own_odd_lat) for f in range(1, 4)]
    own_l = [four(own_odd_lat, f * 32, lat_even, own_even_lat) for f in range(1, 4)]
    ext_r = [four(got_even_lat, f * 32, lat_even, got_odd_lat) for f in range(4)]
    ext_l = [four(got_odd_lat, f * 32, lat_even, got_even_lat) for f in range(4)]
    flat_r = jnp.where(lat_even, got_even_lat[128:136, :], got_odd_lat[128:136, :])
    flat_l = jnp.where(lat_even, got_odd_lat[128:136, :], got_even_lat[128:136, :])
    depth_r = jnp.where(lat_even, got_even_lat[136:144, :], got_odd_lat[136:144, :])
    depth_l = jnp.where(lat_even, got_odd_lat[136:144, :], got_even_lat[136:144, :])
    own_depth_r = jnp.where(lat_even, own_even_lat[136:144, :], own_odd_lat[136:144, :])
    own_depth_l = jnp.where(lat_even, own_odd_lat[136:144, :], own_even_lat[136:144, :])

    def mixed(pair):
        return [scalar_mix(x, y) for x, y in zip(*pair, strict=True)]

    w_r, w_l = mixed(ext_r[2:]), mixed(ext_l[2:])
    miss_own_r, miss_ext_r = lat_rims(
        own_r[0], mixed(own_r[1:]), own_depth_r, ext_r[1], w_r, depth_r
    )
    miss_ext_l, miss_own_l = lat_rims(
        ext_l[1], w_l, depth_l, own_l[0], mixed(own_l[1:]), own_depth_l
    )
    total = total + jnp.where(lane >= 126, miss_own_r, 0.0) + jnp.where(lane < 2, miss_own_l, 0.0)

    def side(i):
        return jnp.where(
            lane < 8,
            by_lanes(flat_r, -8 * i),
            jnp.where(lane >= 120, by_lanes(flat_l, 120 - 8 * i), 0.0),
        )

    elev_side = side(1)
    total_side = side(0) + elev_side
    total_side = total_side + jnp.where(lane < 2, miss_ext_r, 0.0)
    total_side = total_side + jnp.where(lane >= 126, miss_ext_l, 0.0)
    for ref in (odd_out, even_out):
        for i, x in enumerate((total, total_side, elev_side, side(2), side(3))):
            ref[8 * i : 8 * i + 8, :] = x
    packs = ext_r[0] + ext_l[0] + w_r + w_l + [depth_r, depth_l]
    group = row >> 1
    for i in range(5):
        top = bottom = jnp.zeros((ROWS, LANES), F32)
        for j, x in enumerate(packs[4 * i : 4 * i + 4]):
            top = jnp.where(group == j, by_rows(x, 2 * j), top)
            bottom = jnp.where(group == j, by_rows(x, 2 * j - 6), bottom)
        at = slice(40 + 8 * i, 48 + 8 * i)
        odd_out[at, :] = jnp.where(lon_even, top, bottom)
        even_out[at, :] = jnp.where(lon_even, bottom, top)


CHUNKS = ((0, 5), (5, 10), (10, 15))


def fields(
    parity, masked, own_lon, own_odd_lat, own_even_lat, odd_lon, even_lon, odd_lat, even_lat,
    o1, o2, o3, o4, terms, rims, fresh, sems,
):
    row, lane = rows_of(), lanes_of()
    levels = flat_of(own_lon)[2].astype(jnp.int32)
    lon_even, lat_even = parity[0] == 0, parity[1] == 0
    outs = (o1, o2, o3, o4)
    at_edge = (lane < 2) | (lane >= 126)

    matrix = lat_matrix()
    for f in range(4):
        for first in range(0, LEVELS, 16):
            count = min(16, LEVELS - first)
            x = masked[f, first + 1 : first + 1 + count].reshape(count * ROWS, LANES)
            terms[f, ROWS * first : ROWS * (first + count), :] = lat_terms(x, matrix)

    in_even = (lane & 8) == 0

    def west_east(odd, even, base):
        x, y = odd[base : base + 8, :], even[base : base + 8, :]
        return jnp.where(lat_even, x, y), jnp.where(lat_even, y, x)

    depth_west, depth_east = west_east(own_odd_lat, own_even_lat, 136)
    for a in range(4):
        vel_west, vel_east = west_east(own_odd_lat, own_even_lat, 32 + 8 * a)
        for f in range(4):
            west, east = west_east(odd_lat, even_lat, f * 32 + 8 * a)
            right = west_part(vel_east, depth_east, east, a)
            left = by_lanes(east_part(vel_west, depth_west, west, a), 8)
            first = jnp.where(in_even, right, left)
            second = jnp.where(in_even, left, right)
            for i in range(8):
                rims[f, 16 * a + i] = by_lanes(first, -16 * i - 8)
                rims[f, 16 * a + 8 + i] = by_lanes(second, -16 * i - 16)

    def group(g, count):
        strips = []
        for f in range(4):
            at = pl.ds(pl.multiple_of(f * STRIP + 8 * g, 8), 8)
            x, y = odd_lon[at, :], even_lon[at, :]
            strips.append((jnp.where(lon_even, y, x), jnp.where(lon_even, x, y)))
        for j in range(count):
            k = 4 * g + j
            wet = k < levels
            center = [masked[f, k + 1] for f in range(4)]
            zonal, merid = ADV * center[0], ADV * center[1]
            at = pl.ds(pl.multiple_of(ROWS * k, ROWS), ROWS)
            for f in range(4):
                m = center[f]
                upper, lower = strips[f]
                rim = jnp.where(row < 4, by_rows(upper, -2 * j), by_rows(lower, 6 - 2 * j))
                n1 = by_rows(jnp.where(row < 1, rim, m), -1)
                n2 = by_rows(jnp.where(row < 2, rim, m), -2)
                p1 = by_rows(jnp.where(row > 6, rim, m), 1)
                p2 = by_rows(jnp.where(row > 5, rim, m), 2)
                gx = 8.0 * (n1 - p1) - (n2 - p2)
                gy = terms[f, at, :LANES]
                around = (n1 + p1) + terms[f, at, LANES:]
                column = masked[f, k] + masked[f, k + 2]
                value = 0.94 * m + 0.02 * column + 0.005 * around - (zonal * gx + merid * gy)
                fresh[f, k] = jnp.where(wet, value, 0.0) + jnp.where(at_edge, rims[f, k], 0.0)

    def body(g, carry):
        group(g, 4)
        return carry

    copies = []

    def send(first, last):
        for f in range(4):
            copies.append(
                pltpu.make_async_copy(
                    fresh.at[f, first:last], outs[f].at[first:last], sems.at[len(copies)]
                )
            )
            copies[-1].start()

    for first, last in CHUNKS:
        lax.fori_loop(first, last, body, 0, unroll=True)
        send(4 * first, 4 * last)
    group(15, LEVELS - 60)
    send(60, LEVELS)
    for copy in copies:
        copy.wait()


def solve(
    parity, odd_b, even_b, own_b, own_lon, odd_lon, even_lon, odd_lat, even_lat, height
):
    row, lane = rows_of(), lanes_of()
    lon_even, lat_even = parity[0] == 0, parity[1] == 0
    lower = [jnp.where(lon_even, odd_b[8 * i : 8 * i + 8, :], even_b[8 * i : 8 * i + 8, :]) for i in range(10)]
    upper = [jnp.where(lon_even, even_b[8 * i : 8 * i + 8, :], odd_b[8 * i : 8 * i + 8, :]) for i in range(10)]
    own = [own_b[8 * i : 8 * i + 8, :] for i in range(5)]

    ext_r = [four(even_lat, f * 32, lat_even, odd_lat) for f in (0, 2, 3)]
    ext_l = [four(odd_lat, f * 32, lat_even, even_lat) for f in (0, 2, 3)]

    def lon_part(vel, wet, x1, x2):
        slope = jnp.where(row == 0, -8.0 * x1, jnp.where(row == 7, 8.0 * x1, 0.0))
        slope = slope + jnp.where(row < 2, x2, jnp.where(row >= 6, -x2, 0.0))
        near = jnp.where((row == 0) | (row == 7), x1, 0.0)
        return 0.005 * jnp.where(wet, near, 0.0) - ADV * vel * slope

    def rim_rows(tile, q, first):
        return by_rows(tile[5 + q // 4], first - 2 * (q % 4))

    def near_rows(q):
        return jnp.where(row < 4, rim_rows(upper, q, 0), rim_rows(lower, q, 6))

    def side_parts(ext, base, own_depth, near_depth):
        mine = theirs = jnp.zeros((ROWS, LANES), F32)
        for i in range(4):
            vel, w = ext[0][i], scalar_mix(ext[1][i], ext[2][i])
            qu, qw = base + i, 8 + base + i
            x2 = jnp.where(row < 4, rim_rows(lower, qw, 0), rim_rows(upper, qw, 6))
            x1 = jnp.where(row < 4, rim_rows(lower, qw, -1), rim_rows(upper, qw, 7))
            mine = mine + lon_part(vel, wet_pack(own_depth, i), x1, x2)
            y2 = jnp.where(row < 4, by_rows(w, 2), by_rows(w, -2))
            y1 = jnp.where(row < 4, by_rows(w, 1), by_rows(w, -1))
            theirs = theirs + lon_part(near_rows(qu), wet_pack(near_depth, i), y1, y2)
        return 0.1 * sum_slots(mine), 0.1 * sum_slots(theirs)

    depth_r = jnp.where(lat_even, even_lat[136:144, :], odd_lat[136:144, :])
    depth_l = jnp.where(lat_even, odd_lat[136:144, :], even_lat[136:144, :])
    mine_r, theirs_r = side_parts(ext_r, 0, depth_r, near_rows(16))
    mine_l, theirs_l = side_parts(ext_l, 4, depth_l, near_rows(17))
    in_r, in_l = lane < 8, lane >= 120
    mine = jnp.where(in_r, mine_r, jnp.where(in_l, mine_l, 0.0))
    theirs = jnp.where(in_r, theirs_r, jnp.where(in_l, theirs_l, 0.0))

    flat_own = flat_of(own_lon)
    flat_odd, flat_even = flat_of(odd_lon), flat_of(even_lon)
    flat_low = [jnp.where(lon_even, x, y) for x, y in zip(flat_odd, flat_even, strict=True)]
    flat_up = [jnp.where(lon_even, y, x) for x, y in zip(flat_odd, flat_even, strict=True)]

    rhs = [
        lower[0], own[0], upper[0],
        lower[1] + jnp.where(row >= 6, theirs, 0.0),
        own[1] + mine,
        upper[1] + jnp.where(row < 2, theirs, 0.0),
    ]
    elev = [flat_low[0], flat_own[0], flat_up[0], lower[2], own[2], upper[2]]
    diag = [flat_low[1], flat_own[1], flat_up[1], lower[3], own[3], upper[3]]
    wet = [x > 0.0 for x in (flat_low[2], flat_own[2], flat_up[2], lower[4], own[4], upper[4])]
    diag = [x + 4.0 for x in diag]
    inverse = [1.0 / x for x in diag]
    coupled = [jnp.where(a, x, 0.0) for a, x in zip(wet, inverse, strict=True)]

    def neighbours(x):
        out = []
        up = [by_rows(y, -1) for y in x]
        down = [by_rows(y, 1) for y in x]
        east = [by_lanes(y, -1) for y in x]
        west = [by_lanes(y, 1) for y in x]
        for i in range(6):
            h, c = divmod(i, 3)
            base = 3 * h
            other = 3 * (1 - h) + c
            n = jnp.where(row < 7, up[i], up[base + (c + 1) % 3])
            p = jnp.where(row > 0, down[i], down[base + (c + 2) % 3])
            e = jnp.where(lane < 127, east[i], east[other])
            w = jnp.where(lane > 0, west[i], west[other])
            out.append((n + p) + (e + w))
        return out

    sigma = SPECTRUM_MID / SPECTRUM_HALF
    ratio = 1.0 / sigma
    scaled = [x * y for x, y in zip(rhs, inverse, strict=True)]
    previous = elev
    iterate = elev[1]
    for step in range(ITERS):
        around = neighbours([jnp.where(a, x, 0.0) for a, x in zip(wet, previous, strict=True)])
        scaled = [
            (res - x) + c * n
            for res, x, c, n in zip(scaled, previous, coupled, around, strict=True)
        ]
        if step == 0:
            previous = [res / SPECTRUM_MID for res in scaled]
        else:
            following = 1.0 / (2.0 * sigma - ratio)
            keep, gain = following * ratio, 2.0 * following / SPECTRUM_HALF
            previous = [keep * x + gain * res for x, res in zip(previous, scaled, strict=True)]
            ratio = following
        iterate = iterate + previous[1]
    height[...] = iterate


def shaped(*shape):
    return jax.ShapeDtypeStruct(shape, F32)


def call(kernel, outs, ins, flops, moved, **kw):
    return pl.pallas_call(
        kernel,
        out_shape=outs,
        in_specs=ins,
        compiler_params=pltpu.CompilerParams(vmem_limit_bytes=VMEM),
        cost_estimate=pl.CostEstimate(flops=flops, bytes_accessed=moved, transcendentals=0),
        **kw,
    )


SMEM = pl.BlockSpec(memory_space=pltpu.SMEM)
WHOLE = pl.BlockSpec(memory_space=pltpu.VMEM)
HERE = pl.BlockSpec(memory_space=pltpu.HBM)
BLOCK = 4 * LEVELS * ROWS * LANES * 4


def call_pack_lon(*args):
    return call(
        pack_lon,
        (shaped(4, LEVELS + 4, ROWS, LANES), shaped(LON_ROWS, LANES), shaped(LON_ROWS, LANES)),
        [HERE] * 8 + [SMEM], 10**6, 2 * BLOCK,
        out_specs=(WHOLE,) * 3,
        scratch_shapes=[
            pltpu.VMEM((4, LEVELS, ROWS, LANES), F32),
            pltpu.VMEM((2, ROWS, LANES), jnp.int32),
            pltpu.VMEM((2, ROWS, LANES), F32),
            pltpu.SemaphoreType.DMA((8,)),
        ],
    )(*args)


def call_pack_lat(*args):
    return call(
        pack_lat, (shaped(LAT_ROWS, LANES), shaped(LAT_ROWS, LANES), shaped(ROWS, LANES)),
        [WHOLE] * 2 + [SMEM], 4 * 10**6, BLOCK,
    )(*args)


def call_forcing(*args):
    return call(
        forcing, (shaped(SOLVE_ROWS, LANES),) * 2, [SMEM] + [WHOLE] * 9, 10**6, 10**6
    )(*args)


def call_fields(*args):
    return call(
        fields, (shaped(LEVELS, ROWS, LANES),) * 4, [SMEM] + [WHOLE] * 8, 10**7, 3 * BLOCK,
        out_specs=(HERE,) * 4,
        scratch_shapes=[
            pltpu.VMEM((4, LEVELS * ROWS, 2 * LANES), F32),
            pltpu.VMEM((4, LEVELS + 2, ROWS, LANES), F32),
            pltpu.VMEM((4, LEVELS, ROWS, LANES), F32),
            pltpu.SemaphoreType.DMA((16,)),
        ],
    )(*args)


def call_solve(*args):
    return call(solve, shaped(ROWS, LANES), [SMEM] + [WHOLE] * 8, 10**6, 10**6)(*args)


def on_device(u, v, t, s, water, layers, diag, elev):
    lon, lat = lax.axis_size("lon"), lax.axis_size("lat")
    lon_even = [(i, i ^ 1) for i in range(lon)]
    lon_odd = [(i, (((i + 1) ^ 1) - 1) % lon) for i in range(lon)]
    lat_even = [(i, i ^ 1) for i in range(lat)]
    lat_odd = [(i, ((i + 1) ^ 1) - 1) for i in range(1, lat - 1)]
    parity = jnp.stack([lax.axis_index("lon") & 1, lax.axis_index("lat") & 1]).astype(jnp.int32)

    raw = [
        pltpu.with_memory_space_constraint(x, pltpu.HBM)
        for x in (u, v, t, s, water, layers, diag, elev)
    ]
    masked, own_odd, own_even = call_pack_lon(*raw, parity)
    got_even = lax.ppermute(own_even, "lon", lon_even)
    got_odd = lax.ppermute(own_odd, "lon", lon_odd)
    lat_own_odd, lat_own_even, partial = call_pack_lat(masked, own_odd, parity)
    lat_got_odd = lax.ppermute(lat_own_odd, "lat", lat_odd)
    lat_got_even = lax.ppermute(lat_own_even, "lat", lat_even)

    b_odd, b_even = call_forcing(
        parity, got_even, got_odd, own_odd, own_even,
        lat_own_odd, lat_own_even, lat_got_odd, lat_got_even, partial,
    )
    b_got_odd = lax.ppermute(b_odd, "lon", lon_odd)
    b_got_even = lax.ppermute(b_even, "lon", lon_even)

    fresh = call_fields(
        parity, masked, own_odd, lat_own_odd, lat_own_even, got_odd, got_even, lat_got_odd, lat_got_even
    )
    height = call_solve(
        parity, b_got_odd, b_got_even, b_odd, own_odd, got_odd, got_even, lat_got_odd, lat_got_even
    )
    return (*fresh, height)


def solution(mesh):
    field, flat = P(None, "lon", "lat"), P("lon", "lat")
    return jax.shard_map(
        on_device,
        mesh=mesh,
        in_specs=(field,) * 4 + (flat,) * 4,
        out_specs=(field,) * 4 + (flat,),
        check_vma=False,
    )
```

```python
import jax
import jax.numpy as jnp
from jax import lax
from jax.experimental import pallas as pl
from jax.experimental.pallas import tpu as pltpu
from jax.sharding import PartitionSpec as P

ITERS = 8
LEVELS = 62
SPECTRUM_MID = 1.0
SPECTRUM_HALF = 0.995

ROWS = 8
LANES = 128
STRIP = 128
FLAT = 4 * STRIP
LON_ROWS = FLAT + 3 * ROWS
LAT_ROWS = 18 * ROWS
SOLVE_ROWS = 5 * ROWS + 5 * ROWS
VMEM = 12 * 1024 * 1024

F32 = jnp.float32
ADV = 0.1 / 12.0


def rows_of(shape=(ROWS, LANES)):
    return lax.broadcasted_iota(jnp.int32, shape, 0)


def lanes_of(shape=(ROWS, LANES)):
    return lax.broadcasted_iota(jnp.int32, shape, 1)


def by_rows(x, d):
    d %= ROWS
    return pltpu.roll(x, d, 0) if d else x


def by_lanes(x, d):
    d %= LANES
    return pltpu.roll(x, d, 1) if d else x


def scalar_mix(t, s):
    return 0.7 * t - 0.5 * s


def even(axis):
    return lax.axis_index(axis) % 2 == 0


def flat_of(ref, base=FLAT):
    return [ref[base + 8 * i : base + 8 * i + 8, :] for i in range(3)]


def pack_lon(
    u, v, t, s, water, layers, diag, elev, after, parity, masked, up_first, low_first, held, held_int, held_flat, sems
):
    copies = [
        pltpu.make_async_copy(src, held.at[i], sems.at[i]) for i, src in enumerate((u, v, t, s))
    ]
    small = [
        pltpu.make_async_copy(water, held_int.at[0], sems.at[4]),
        pltpu.make_async_copy(layers, held_int.at[1], sems.at[5]),
        pltpu.make_async_copy(elev, held_flat.at[0], sems.at[6]),
        pltpu.make_async_copy(diag, held_flat.at[1], sems.at[7]),
    ]
    for copy in small[:2] + copies + small[2:]:
        copy.start()
    for copy in small[:2]:
        copy.wait()
    row = rows_of()
    group = row >> 1
    depth = held_int[0] * held_int[1]
    is_even = parity[0] == 0

    for f in range(4):
        masked[f, 0] = jnp.zeros((ROWS, LANES), F32)
        masked[f, LEVELS + 3] = jnp.zeros((ROWS, LANES), F32)
        copies[f].wait()

        def body(g, carry, f=f):
            top = bottom = None
            for i in range(4):
                k = 4 * g + i
                m = jnp.where(k < depth, held[f, jnp.minimum(k, LEVELS - 1)], 0.0)
                masked[f, k + 1] = m
                a, b = by_rows(m, 2 * i), by_rows(m, 2 * i - 6)
                top = a if i == 0 else jnp.where(group == i, a, top)
                bottom = b if i == 0 else jnp.where(group == i, b, bottom)
            at = pl.ds(pl.multiple_of(f * STRIP + 8 * g, 8), 8)
            up_first[at, :] = jnp.where(is_even, top, bottom)
            low_first[at, :] = jnp.where(is_even, bottom, top)
            return carry

        lax.fori_loop(0, 16, body, 0, unroll=True)

    for copy in small[2:]:
        copy.wait()
    for ref in (up_first, low_first):
        ref[FLAT : FLAT + 8, :] = held_flat[0]
        ref[FLAT + 8 : FLAT + 16, :] = held_flat[1]
        ref[FLAT + 16 : FLAT + 24, :] = depth.astype(F32)


BF16 = jnp.bfloat16


def lat_matrix():
    shape = (2 * LANES, 2 * LANES)
    source = rows_of(shape) & 127
    target = lanes_of(shape)
    d = source - (target & 127)
    slope = jnp.where(d == 1, 8.0, jnp.where(d == -1, -8.0, 0.0))
    slope = slope + jnp.where(d == 2, -1.0, jnp.where(d == -2, 1.0, 0.0))
    near = jnp.where(jnp.abs(d) == 1, 1.0, 0.0)
    return jnp.where(target < LANES, slope, near).astype(BF16)


def lat_terms(x, matrix):
    high = x.astype(BF16)
    rest = (x - high.astype(F32)).astype(BF16)
    return jnp.dot(jnp.concatenate([high, rest], axis=1), matrix, preferred_element_type=F32)


def lat_packs(masked, flat, parity, odd_out, even_out, partial):
    row, lane = rows_of(), lanes_of()
    high, low = lane >> 4, ((lane - 8) & 127) >> 4
    in_even = (lane & 8) == 0
    elev, diag, depth = flat
    levels = depth.astype(jnp.int32)
    is_even = parity[1] == 0
    zero = jnp.zeros((ROWS, LANES), F32)
    matrix = lat_matrix()
    left, right = tile_lanes(depth), tile_lanes(by_lanes(depth, 8))
    odd_out[136:144, :] = jnp.where(is_even, left, right)
    even_out[136:144, :] = jnp.where(is_even, right, left)

    def tile(a, sums):
        whole, inner, sides, flux = sums
        first, second = [zero] * 4, [zero] * 4
        tracer = [
            scalar_mix(masked[2, 16 * a + i + 1], masked[3, 16 * a + i + 1]) for i in range(16)
        ]
        terms = lat_terms(jnp.concatenate(tracer, axis=0), matrix)
        for i in range(16):
            k = 16 * a + i
            m = [masked[f, k + 1] for f in range(4)]
            for f in range(4):
                if i < 8:
                    first[f] = jnp.where(high == i, by_lanes(m[f], 16 * i - 120), first[f])
                else:
                    second[f] = jnp.where(low == i - 8, by_lanes(m[f], 16 * i - 240), second[f])
            w = tracer[i]
            n1 = jnp.where(row < 7, by_rows(w, -1), 0.0)
            p1 = jnp.where(row > 0, by_rows(w, 1), 0.0)
            n2 = jnp.where(row < 6, by_rows(w, -2), 0.0)
            p2 = jnp.where(row > 1, by_rows(w, 2), 0.0)
            gx = 8.0 * (n1 - p1) - (n2 - p2)
            gy = terms[8 * i : 8 * i + 8, :LANES]
            around = (n1 + p1) + terms[8 * i : 8 * i + 8, LANES:]
            whole = whole + w
            inner = inner + jnp.where(k + 1 < levels, w, 0.0)
            sides = sides + jnp.where(k < levels, around, 0.0)
            flux = flux + (m[0] * gx + m[1] * gy)
        for f in range(4):
            right = jnp.where(in_even, first[f], second[f])
            left = by_lanes(jnp.where(in_even, second[f], first[f]), -8)
            where = pl.ds(pl.multiple_of(f * 32 + 8 * a, 8), 8)
            odd_out[where, :] = jnp.where(is_even, left, right)
            even_out[where, :] = jnp.where(is_even, right, left)
        return whole, inner, sides, flux

    whole, inner, sides, flux = lax.fori_loop(0, 4, tile, (zero,) * 4, unroll=True)
    top = scalar_mix(masked[2, 1], masked[3, 1])
    acc = 0.1 * (0.94 * whole + 0.02 * (whole - top + inner) + 0.005 * sides - ADV * flux)
    partial[...] = acc
    slot = lane >> 3
    left = right = zero
    for i, x in enumerate((acc, elev, diag, depth)):
        left = jnp.where(slot == i, by_lanes(x, 8 * i), left)
        right = jnp.where(slot == i, by_lanes(x, 8 * i - 120), right)
    odd_out[128:136, :] = jnp.where(is_even, left, right)
    even_out[128:136, :] = jnp.where(is_even, right, left)


def pack_lat_early(
    u, v, t, s, water, layers, diag, elev, parity, odd_out, even_out, partial, masked, held, held_int, held_flat, sems
):
    @pl.when(parity[2] == 1)
    def _():
        copies = [
            pltpu.make_async_copy(src, dst, sems.at[i])
            for i, (src, dst) in enumerate(
                [(x, held.at[f]) for f, x in enumerate((u, v, t, s))]
                + [(water, held_int.at[0]), (layers, held_int.at[1])]
                + [(elev, held_flat.at[0]), (diag, held_flat.at[1])]
            )
        ]
        for copy in copies:
            copy.start()
        for copy in copies:
            copy.wait()
        depth = held_int[0] * held_int[1]
        for f in range(4):
            for i in (0, LEVELS + 1, LEVELS + 2, LEVELS + 3):
                masked[f, i] = jnp.zeros((ROWS, LANES), F32)

        def body(k, carry):
            for f in range(4):
                masked[f, k + 1] = jnp.where(k < depth, held[f, k], 0.0)
            return carry

        lax.fori_loop(0, LEVELS, body, 0)
        flat = (held_flat[0], held_flat[1], depth.astype(F32))
        lat_packs(masked, flat, parity, odd_out, even_out, partial)


def pack_lat_late(masked, own_lon, odd, even, before, parity, odd_out, even_out, partial):
    @pl.when(parity[2] == 1)
    def _():
        odd_out[...] = odd[...]
        even_out[...] = even[...]
        partial[...] = before[...]

    @pl.when(parity[2] == 0)
    def _():
        lat_packs(masked, flat_of(own_lon), parity, odd_out, even_out, partial)


def tile_lanes(x):
    return sum_slots(jnp.where(lanes_of() < 8, x, 0.0))


def sum_slots(x):
    for d in (8, 32):
        x = (x + by_lanes(x, d)) + (by_lanes(x, 2 * d) + by_lanes(x, 3 * d))
    return x


def wet_pack(depth, a):
    slot = lanes_of() >> 3
    return (16 * a + (slot >> 1) + 8 * (slot & 1)).astype(F32) < depth


def west_part(vel, depth, east, i):
    column = lanes_of() & 7
    y1 = jnp.where(column == 7, by_lanes(east, 7), 0.0)
    y2 = jnp.where(column >= 6, by_lanes(east, 6), 0.0)
    return 0.005 * jnp.where(wet_pack(depth, i), y1, 0.0) - ADV * vel * (8.0 * y1 - y2)


def east_part(vel, depth, west, i):
    column = lanes_of() & 7
    z1 = jnp.where(column == 0, by_lanes(west, -7), 0.0)
    z2 = jnp.where(column <= 1, by_lanes(west, -6), 0.0)
    return 0.005 * jnp.where(wet_pack(depth, i), z1, 0.0) - ADV * vel * (z2 - 8.0 * z1)


def lat_rims(a_v, a_w, a_depth, b_v, b_w, b_depth):
    a_sum = b_sum = jnp.zeros((ROWS, LANES), F32)
    for i in range(4):
        a_sum = a_sum + west_part(a_v[i], a_depth, b_w[i], i)
        b_sum = b_sum + east_part(b_v[i], b_depth, a_w[i], i)
    return 0.1 * sum_slots(a_sum), 0.1 * sum_slots(b_sum)


def four(ref, base, flag, other):
    at = [slice(base + 8 * i, base + 8 * i + 8) for i in range(4)]
    return [jnp.where(flag, ref[x, :], other[x, :]) for x in at]


def forcing(
    parity, got_even, got_odd, own_odd, own_even,
    own_odd_lat, own_even_lat, got_odd_lat, got_even_lat, partial,
    odd_out, even_out,
):
    row, lane = rows_of(), lanes_of()
    lon_even, lat_even = parity[0] == 0, parity[1] == 0
    elev, diag, depth = flat_of(own_odd)
    total = elev + partial[...]

    r = row & 1
    for lower in (True, False):
        rim = row < 2 if lower else row >= 6
        tiled = jnp.where(rim, depth, 0.0)
        tiled = tiled + by_rows(tiled, 2)
        tiled = tiled + by_rows(tiled, 4)
        acc = jnp.zeros((ROWS, LANES), F32)
        own_first = lon_even if lower else jnp.logical_not(lon_even)
        for g in range(16):
            at = slice(8 * g, 8 * g + 8)
            at_t = slice(2 * STRIP + 8 * g, 2 * STRIP + 8 * g + 8)
            at_s = slice(3 * STRIP + 8 * g, 3 * STRIP + 8 * g + 8)
            vel = jnp.where(own_first, own_odd[at, :], own_even[at, :])
            w = scalar_mix(
                jnp.where(own_first, got_odd[at_t, :], got_even[at_t, :]),
                jnp.where(own_first, got_odd[at_s, :], got_even[at_s, :]),
            )
            wet = (4 * g + (row >> 1)).astype(F32) < tiled
            if lower:
                near = jnp.where(r == 0, by_rows(w, -1), 0.0)
                slope = w - 8.0 * near
            else:
                near = jnp.where(r == 1, by_rows(w, 1), 0.0)
                slope = 8.0 * near - w
            acc = acc + (0.005 * jnp.where(wet, near, 0.0) - ADV * vel * slope)
        acc = acc + by_rows(acc, 2)
        acc = acc + by_rows(acc, 4)
        total = total + jnp.where(rim, 0.1 * acc, 0.0)

    own_r = [four(own_even_lat, f * 32, lat_even, own_odd_lat) for f in range(1, 4)]
    own_l = [four(own_odd_lat, f * 32, lat_even, own_even_lat) for f in range(1, 4)]
    ext_r = [four(got_even_lat, f * 32, lat_even, got_odd_lat) for f in range(4)]
    ext_l = [four(got_odd_lat, f * 32, lat_even, got_even_lat) for f in range(4)]
    flat_r = jnp.where(lat_even, got_even_lat[128:136, :], got_odd_lat[128:136, :])
    flat_l = jnp.where(lat_even, got_odd_lat[128:136, :], got_even_lat[128:136, :])
    depth_r = jnp.where(lat_even, got_even_lat[136:144, :], got_odd_lat[136:144, :])
    depth_l = jnp.where(lat_even, got_odd_lat[136:144, :], got_even_lat[136:144, :])
    own_depth_r = jnp.where(lat_even, own_even_lat[136:144, :], own_odd_lat[136:144, :])
    own_depth_l = jnp.where(lat_even, own_odd_lat[136:144, :], own_even_lat[136:144, :])

    def mixed(pair):
        return [scalar_mix(x, y) for x, y in zip(*pair, strict=True)]

    w_r, w_l = mixed(ext_r[2:]), mixed(ext_l[2:])
    miss_own_r, miss_ext_r = lat_rims(
        own_r[0], mixed(own_r[1:]), own_depth_r, ext_r[1], w_r, depth_r
    )
    miss_ext_l, miss_own_l = lat_rims(
        ext_l[1], w_l, depth_l, own_l[0], mixed(own_l[1:]), own_depth_l
    )
    total = total + jnp.where(lane >= 126, miss_own_r, 0.0) + jnp.where(lane < 2, miss_own_l, 0.0)

    def side(i):
        return jnp.where(
            lane < 8,
            by_lanes(flat_r, -8 * i),
            jnp.where(lane >= 120, by_lanes(flat_l, 120 - 8 * i), 0.0),
        )

    elev_side = side(1)
    total_side = side(0) + elev_side
    total_side = total_side + jnp.where(lane < 2, miss_ext_r, 0.0)
    total_side = total_side + jnp.where(lane >= 126, miss_ext_l, 0.0)
    for ref in (odd_out, even_out):
        for i, x in enumerate((total, total_side, elev_side, side(2), side(3))):
            ref[8 * i : 8 * i + 8, :] = x
    packs = ext_r[0] + ext_l[0] + w_r + w_l + [depth_r, depth_l]
    group = row >> 1
    for i in range(5):
        top = bottom = jnp.zeros((ROWS, LANES), F32)
        for j, x in enumerate(packs[4 * i : 4 * i + 4]):
            top = jnp.where(group == j, by_rows(x, 2 * j), top)
            bottom = jnp.where(group == j, by_rows(x, 2 * j - 6), bottom)
        at = slice(40 + 8 * i, 48 + 8 * i)
        odd_out[at, :] = jnp.where(lon_even, top, bottom)
        even_out[at, :] = jnp.where(lon_even, bottom, top)


CHUNKS = ((0, 5), (5, 10), (10, 15))


def fields(
    parity, masked, own_lon, own_odd_lat, own_even_lat, odd_lon, even_lon, odd_lat, even_lat,
    o1, o2, o3, o4, terms, rims, fresh, sems,
):
    row, lane = rows_of(), lanes_of()
    levels = flat_of(own_lon)[2].astype(jnp.int32)
    lon_even, lat_even = parity[0] == 0, parity[1] == 0
    outs = (o1, o2, o3, o4)
    at_edge = (lane < 2) | (lane >= 126)

    matrix = lat_matrix()
    for f in range(4):
        for first in range(0, LEVELS, 16):
            count = min(16, LEVELS - first)
            x = masked[f, first + 1 : first + 1 + count].reshape(count * ROWS, LANES)
            terms[f, ROWS * first : ROWS * (first + count), :] = lat_terms(x, matrix)

    in_even = (lane & 8) == 0

    def west_east(odd, even, base):
        x, y = odd[base : base + 8, :], even[base : base + 8, :]
        return jnp.where(lat_even, x, y), jnp.where(lat_even, y, x)

    depth_west, depth_east = west_east(own_odd_lat, own_even_lat, 136)
    for a in range(4):
        vel_west, vel_east = west_east(own_odd_lat, own_even_lat, 32 + 8 * a)
        for f in range(4):
            west, east = west_east(odd_lat, even_lat, f * 32 + 8 * a)
            right = west_part(vel_east, depth_east, east, a)
            left = by_lanes(east_part(vel_west, depth_west, west, a), 8)
            first = jnp.where(in_even, right, left)
            second = jnp.where(in_even, left, right)
            for i in range(8):
                rims[f, 16 * a + i] = by_lanes(first, -16 * i - 8)
                rims[f, 16 * a + 8 + i] = by_lanes(second, -16 * i - 16)

    def group(g, count):
        strips = []
        for f in range(4):
            at = pl.ds(pl.multiple_of(f * STRIP + 8 * g, 8), 8)
            x, y = odd_lon[at, :], even_lon[at, :]
            strips.append((jnp.where(lon_even, y, x), jnp.where(lon_even, x, y)))
        for j in range(count):
            k = 4 * g + j
            wet = k < levels
            center = [masked[f, k + 1] for f in range(4)]
            zonal, merid = ADV * center[0], ADV * center[1]
            at = pl.ds(pl.multiple_of(ROWS * k, ROWS), ROWS)
            for f in range(4):
                m = center[f]
                upper, lower = strips[f]
                rim = jnp.where(row < 4, by_rows(upper, -2 * j), by_rows(lower, 6 - 2 * j))
                n1 = by_rows(jnp.where(row < 1, rim, m), -1)
                n2 = by_rows(jnp.where(row < 2, rim, m), -2)
                p1 = by_rows(jnp.where(row > 6, rim, m), 1)
                p2 = by_rows(jnp.where(row > 5, rim, m), 2)
                gx = 8.0 * (n1 - p1) - (n2 - p2)
                gy = terms[f, at, :LANES]
                around = (n1 + p1) + terms[f, at, LANES:]
                column = masked[f, k] + masked[f, k + 2]
                value = 0.94 * m + 0.02 * column + 0.005 * around - (zonal * gx + merid * gy)
                fresh[f, k] = jnp.where(wet, value, 0.0) + jnp.where(at_edge, rims[f, k], 0.0)

    def body(g, carry):
        group(g, 4)
        return carry

    copies = []

    def send(first, last):
        for f in range(4):
            copies.append(
                pltpu.make_async_copy(
                    fresh.at[f, first:last], outs[f].at[first:last], sems.at[len(copies)]
                )
            )
            copies[-1].start()

    for first, last in CHUNKS:
        lax.fori_loop(first, last, body, 0, unroll=True)
        send(4 * first, 4 * last)
    group(15, LEVELS - 60)
    send(60, LEVELS)
    for copy in copies:
        copy.wait()


def solve(
    parity, odd_b, even_b, own_b, own_lon, odd_lon, even_lon, odd_lat, even_lat, height
):
    row, lane = rows_of(), lanes_of()
    lon_even, lat_even = parity[0] == 0, parity[1] == 0
    lower = [jnp.where(lon_even, odd_b[8 * i : 8 * i + 8, :], even_b[8 * i : 8 * i + 8, :]) for i in range(10)]
    upper = [jnp.where(lon_even, even_b[8 * i : 8 * i + 8, :], odd_b[8 * i : 8 * i + 8, :]) for i in range(10)]
    own = [own_b[8 * i : 8 * i + 8, :] for i in range(5)]

    ext_r = [four(even_lat, f * 32, lat_even, odd_lat) for f in (0, 2, 3)]
    ext_l = [four(odd_lat, f * 32, lat_even, even_lat) for f in (0, 2, 3)]

    def lon_part(vel, wet, x1, x2):
        slope = jnp.where(row == 0, -8.0 * x1, jnp.where(row == 7, 8.0 * x1, 0.0))
        slope = slope + jnp.where(row < 2, x2, jnp.where(row >= 6, -x2, 0.0))
        near = jnp.where((row == 0) | (row == 7), x1, 0.0)
        return 0.005 * jnp.where(wet, near, 0.0) - ADV * vel * slope

    def rim_rows(tile, q, first):
        return by_rows(tile[5 + q // 4], first - 2 * (q % 4))

    def near_rows(q):
        return jnp.where(row < 4, rim_rows(upper, q, 0), rim_rows(lower, q, 6))

    def side_parts(ext, base, own_depth, near_depth):
        mine = theirs = jnp.zeros((ROWS, LANES), F32)
        for i in range(4):
            vel, w = ext[0][i], scalar_mix(ext[1][i], ext[2][i])
            qu, qw = base + i, 8 + base + i
            x2 = jnp.where(row < 4, rim_rows(lower, qw, 0), rim_rows(upper, qw, 6))
            x1 = jnp.where(row < 4, rim_rows(lower, qw, -1), rim_rows(upper, qw, 7))
            mine = mine + lon_part(vel, wet_pack(own_depth, i), x1, x2)
            y2 = jnp.where(row < 4, by_rows(w, 2), by_rows(w, -2))
            y1 = jnp.where(row < 4, by_rows(w, 1), by_rows(w, -1))
            theirs = theirs + lon_part(near_rows(qu), wet_pack(near_depth, i), y1, y2)
        return 0.1 * sum_slots(mine), 0.1 * sum_slots(theirs)

    depth_r = jnp.where(lat_even, even_lat[136:144, :], odd_lat[136:144, :])
    depth_l = jnp.where(lat_even, odd_lat[136:144, :], even_lat[136:144, :])
    mine_r, theirs_r = side_parts(ext_r, 0, depth_r, near_rows(16))
    mine_l, theirs_l = side_parts(ext_l, 4, depth_l, near_rows(17))
    in_r, in_l = lane < 8, lane >= 120
    mine = jnp.where(in_r, mine_r, jnp.where(in_l, mine_l, 0.0))
    theirs = jnp.where(in_r, theirs_r, jnp.where(in_l, theirs_l, 0.0))

    flat_own = flat_of(own_lon)
    flat_odd, flat_even = flat_of(odd_lon), flat_of(even_lon)
    flat_low = [jnp.where(lon_even, x, y) for x, y in zip(flat_odd, flat_even, strict=True)]
    flat_up = [jnp.where(lon_even, y, x) for x, y in zip(flat_odd, flat_even, strict=True)]

    rhs = [
        lower[0], own[0], upper[0],
        lower[1] + jnp.where(row >= 6, theirs, 0.0),
        own[1] + mine,
        upper[1] + jnp.where(row < 2, theirs, 0.0),
    ]
    elev = [flat_low[0], flat_own[0], flat_up[0], lower[2], own[2], upper[2]]
    diag = [flat_low[1], flat_own[1], flat_up[1], lower[3], own[3], upper[3]]
    wet = [x > 0.0 for x in (flat_low[2], flat_own[2], flat_up[2], lower[4], own[4], upper[4])]
    diag = [x + 4.0 for x in diag]
    inverse = [1.0 / x for x in diag]
    coupled = [jnp.where(a, x, 0.0) for a, x in zip(wet, inverse, strict=True)]

    def neighbours(x):
        out = []
        up = [by_rows(y, -1) for y in x]
        down = [by_rows(y, 1) for y in x]
        east = [by_lanes(y, -1) for y in x]
        west = [by_lanes(y, 1) for y in x]
        for i in range(6):
            h, c = divmod(i, 3)
            base = 3 * h
            other = 3 * (1 - h) + c
            n = jnp.where(row < 7, up[i], up[base + (c + 1) % 3])
            p = jnp.where(row > 0, down[i], down[base + (c + 2) % 3])
            e = jnp.where(lane < 127, east[i], east[other])
            w = jnp.where(lane > 0, west[i], west[other])
            out.append((n + p) + (e + w))
        return out

    sigma = SPECTRUM_MID / SPECTRUM_HALF
    ratio = 1.0 / sigma
    scaled = [x * y for x, y in zip(rhs, inverse, strict=True)]
    previous = elev
    iterate = elev[1]
    for step in range(ITERS):
        around = neighbours([jnp.where(a, x, 0.0) for a, x in zip(wet, previous, strict=True)])
        scaled = [
            (res - x) + c * n
            for res, x, c, n in zip(scaled, previous, coupled, around, strict=True)
        ]
        if step == 0:
            previous = [res / SPECTRUM_MID for res in scaled]
        else:
            following = 1.0 / (2.0 * sigma - ratio)
            keep, gain = following * ratio, 2.0 * following / SPECTRUM_HALF
            previous = [keep * x + gain * res for x, res in zip(previous, scaled, strict=True)]
            ratio = following
        iterate = iterate + previous[1]
    height[...] = iterate


def shaped(*shape):
    return jax.ShapeDtypeStruct(shape, F32)


def call(kernel, outs, ins, flops, moved, **kw):
    return pl.pallas_call(
        kernel,
        out_shape=outs,
        in_specs=ins,
        compiler_params=pltpu.CompilerParams(vmem_limit_bytes=VMEM),
        cost_estimate=pl.CostEstimate(flops=flops, bytes_accessed=moved, transcendentals=0),
        **kw,
    )


SMEM = pl.BlockSpec(memory_space=pltpu.SMEM)
WHOLE = pl.BlockSpec(memory_space=pltpu.VMEM)
HERE = pl.BlockSpec(memory_space=pltpu.HBM)
BLOCK = 4 * LEVELS * ROWS * LANES * 4


def call_pack_lon(*args):
    return call(
        pack_lon,
        (shaped(4, LEVELS + 4, ROWS, LANES), shaped(LON_ROWS, LANES), shaped(LON_ROWS, LANES)),
        [HERE] * 8 + [pl.BlockSpec(memory_space=pl.ANY), SMEM], 10**6, 2 * BLOCK,
        out_specs=(WHOLE,) * 3,
        scratch_shapes=[
            pltpu.VMEM((4, LEVELS, ROWS, LANES), F32),
            pltpu.VMEM((2, ROWS, LANES), jnp.int32),
            pltpu.VMEM((2, ROWS, LANES), F32),
            pltpu.SemaphoreType.DMA((8,)),
        ],
    )(*args)


LAT_OUT = (shaped(LAT_ROWS, LANES), shaped(LAT_ROWS, LANES), shaped(ROWS, LANES))


def call_pack_lat_early(*args):
    return call(
        pack_lat_early, LAT_OUT, [HERE] * 8 + [SMEM], 4 * 10**6, BLOCK,
        scratch_shapes=[
            pltpu.VMEM((4, LEVELS + 4, ROWS, LANES), F32),
            pltpu.VMEM((4, LEVELS, ROWS, LANES), F32),
            pltpu.VMEM((2, ROWS, LANES), jnp.int32),
            pltpu.VMEM((2, ROWS, LANES), F32),
            pltpu.SemaphoreType.DMA((8,)),
        ],
    )(*args)


def call_pack_lat_late(*args):
    return call(pack_lat_late, LAT_OUT, [WHOLE] * 5 + [SMEM], 4 * 10**6, BLOCK)(*args)


def call_forcing(*args):
    return call(
        forcing, (shaped(SOLVE_ROWS, LANES),) * 2, [SMEM] + [WHOLE] * 9, 10**6, 10**6
    )(*args)


def call_fields(*args):
    return call(
        fields, (shaped(LEVELS, ROWS, LANES),) * 4, [SMEM] + [WHOLE] * 8, 10**7, 3 * BLOCK,
        out_specs=(HERE,) * 4,
        scratch_shapes=[
            pltpu.VMEM((4, LEVELS * ROWS, 2 * LANES), F32),
            pltpu.VMEM((4, LEVELS + 2, ROWS, LANES), F32),
            pltpu.VMEM((4, LEVELS, ROWS, LANES), F32),
            pltpu.SemaphoreType.DMA((16,)),
        ],
    )(*args)


def call_solve(*args):
    return call(solve, shaped(ROWS, LANES), [SMEM] + [WHOLE] * 8, 10**6, 10**6)(*args)


RUN, EARLY = 8, 4


def on_device(u, v, t, s, water, layers, diag, elev):
    lon, lat = lax.axis_size("lon"), lax.axis_size("lat")
    lon_even = [(i, i ^ 1) for i in range(lon)]
    lon_odd = [(i, (((i + 1) ^ 1) - 1) % lon) for i in range(lon)]
    lat_even = [(i, i ^ 1) for i in range(lat)]
    lat_odd = [(i, ((i + 1) ^ 1) - 1) for i in range(1, lat - 1)]

    def odd_of(early):
        rows = [i for i in range(lon) if (i % RUN < EARLY) == early]
        return [(i * lat + a, i * lat + b) for i in rows for a, b in lat_odd]

    at = lax.axis_index("lon")
    parity = jnp.stack([at & 1, lax.axis_index("lat") & 1, at % RUN < EARLY]).astype(jnp.int32)

    raw = [
        pltpu.with_memory_space_constraint(x, pltpu.HBM)
        for x in (u, v, t, s, water, layers, diag, elev)
    ]
    first_odd, first_even, first_partial = call_pack_lat_early(*raw, parity)
    lat_early = lax.ppermute(first_odd, ("lon", "lat"), odd_of(True))
    masked, own_odd, own_even = call_pack_lon(*raw, lat_early, parity)
    got_even = lax.ppermute(own_even, "lon", lon_even)
    got_odd = lax.ppermute(own_odd, "lon", lon_odd)
    lat_own_odd, lat_own_even, partial = call_pack_lat_late(
        masked, own_odd, first_odd, first_even, first_partial, parity
    )
    lat_got_even = lax.ppermute(lat_own_even, "lat", lat_even)
    lat_got_odd = lat_early + lax.ppermute(lat_own_odd, ("lon", "lat"), odd_of(False))

    b_odd, b_even = call_forcing(
        parity, got_even, got_odd, own_odd, own_even,
        lat_own_odd, lat_own_even, lat_got_odd, lat_got_even, partial,
    )
    b_got_odd = lax.ppermute(b_odd, "lon", lon_odd)
    b_got_even = lax.ppermute(b_even, "lon", lon_even)

    fresh = call_fields(
        parity, masked, own_odd, lat_own_odd, lat_own_even, got_odd, got_even, lat_got_odd, lat_got_even
    )
    height = call_solve(
        parity, b_got_odd, b_got_even, b_odd, own_odd, got_odd, got_even, lat_got_odd, lat_got_even
    )
    return (*fresh, height)


def solution(mesh):
    field, flat = P(None, "lon", "lat"), P("lon", "lat")
    return jax.shard_map(
        on_device,
        mesh=mesh,
        in_specs=(field,) * 4 + (flat,) * 4,
        out_specs=(field,) * 4 + (flat,),
        check_vma=False,
    )
```

```python
import jax
import jax.numpy as jnp
from jax import lax
from jax.experimental import pallas as pl
from jax.experimental.pallas import tpu as pltpu
from jax.sharding import PartitionSpec as P

ITERS = 8
LEVELS = 62
SPECTRUM_MID = 1.0
SPECTRUM_HALF = 0.995

ROWS = 8
LANES = 128
STRIP = 128
FLAT = 4 * STRIP
TIED = FLAT + 3 * ROWS
LON_ROWS = TIED + ROWS
LAT_ROWS = 18 * ROWS
SOLVE_ROWS = 5 * ROWS + 5 * ROWS
VMEM = 12 * 1024 * 1024

F32 = jnp.float32
ADV = 0.1 / 12.0


def rows_of(shape=(ROWS, LANES)):
    return lax.broadcasted_iota(jnp.int32, shape, 0)


def lanes_of(shape=(ROWS, LANES)):
    return lax.broadcasted_iota(jnp.int32, shape, 1)


def by_rows(x, d):
    d %= ROWS
    return pltpu.roll(x, d, 0) if d else x


def by_lanes(x, d):
    d %= LANES
    return pltpu.roll(x, d, 1) if d else x


def scalar_mix(t, s):
    return 0.7 * t - 0.5 * s


def even(axis):
    return lax.axis_index(axis) % 2 == 0


def flat_of(ref, base=FLAT):
    return [ref[base + 8 * i : base + 8 * i + 8, :] for i in range(3)]


def pack_lon(
    u, v, t, s, water, layers, diag, elev, parity, masked, up_first, low_first, held, held_int, held_flat, sems
):
    copies = [
        pltpu.make_async_copy(src, held.at[i], sems.at[i]) for i, src in enumerate((u, v, t, s))
    ]
    small = [
        pltpu.make_async_copy(water, held_int.at[0], sems.at[4]),
        pltpu.make_async_copy(layers, held_int.at[1], sems.at[5]),
        pltpu.make_async_copy(elev, held_flat.at[0], sems.at[6]),
        pltpu.make_async_copy(diag, held_flat.at[1], sems.at[7]),
    ]
    for copy in small[:2] + copies + small[2:]:
        copy.start()
    for copy in small[:2]:
        copy.wait()
    row = rows_of()
    group = row >> 1
    depth = held_int[0] * held_int[1]
    is_even = parity[0] == 0

    for f in range(4):
        masked[f, 0] = jnp.zeros((ROWS, LANES), F32)
        masked[f, LEVELS + 3] = jnp.zeros((ROWS, LANES), F32)
        copies[f].wait()

        def body(g, carry, f=f):
            top = bottom = None
            for i in range(4):
                k = 4 * g + i
                m = jnp.where(k < depth, held[f, jnp.minimum(k, LEVELS - 1)], 0.0)
                masked[f, k + 1] = m
                a, b = by_rows(m, 2 * i), by_rows(m, 2 * i - 6)
                top = a if i == 0 else jnp.where(group == i, a, top)
                bottom = b if i == 0 else jnp.where(group == i, b, bottom)
            at = pl.ds(pl.multiple_of(f * STRIP + 8 * g, 8), 8)
            up_first[at, :] = jnp.where(is_even, top, bottom)
            low_first[at, :] = jnp.where(is_even, bottom, top)
            return carry

        lax.fori_loop(0, 16, body, 0, unroll=True)

    for copy in small[2:]:
        copy.wait()
    for ref in (up_first, low_first):
        ref[FLAT : FLAT + 8, :] = held_flat[0]
        ref[FLAT + 8 : FLAT + 16, :] = held_flat[1]
        ref[FLAT + 16 : FLAT + 24, :] = depth.astype(F32)
        ref[TIED:LON_ROWS, :] = jnp.zeros((ROWS, LANES), F32)


BF16 = jnp.bfloat16


def lat_matrix():
    shape = (2 * LANES, 2 * LANES)
    source = rows_of(shape) & 127
    target = lanes_of(shape)
    d = source - (target & 127)
    slope = jnp.where(d == 1, 8.0, jnp.where(d == -1, -8.0, 0.0))
    slope = slope + jnp.where(d == 2, -1.0, jnp.where(d == -2, 1.0, 0.0))
    near = jnp.where(jnp.abs(d) == 1, 1.0, 0.0)
    return jnp.where(target < LANES, slope, near).astype(BF16)


def lat_terms(x, matrix):
    high = x.astype(BF16)
    rest = (x - high.astype(F32)).astype(BF16)
    return jnp.dot(jnp.concatenate([high, rest], axis=1), matrix, preferred_element_type=F32)


def pack_lat(masked, own_lon, parity, odd_out, even_out, partial):
    row, lane = rows_of(), lanes_of()
    high, low = lane >> 4, ((lane - 8) & 127) >> 4
    in_even = (lane & 8) == 0
    elev, diag, depth = flat_of(own_lon)
    levels = depth.astype(jnp.int32)
    is_even = parity[1] == 0
    zero = jnp.zeros((ROWS, LANES), F32)
    matrix = lat_matrix()
    left, right = tile_lanes(depth), tile_lanes(by_lanes(depth, 8))
    odd_out[136:144, :] = jnp.where(is_even, left, right)
    even_out[136:144, :] = jnp.where(is_even, right, left)

    def tile(a, sums):
        whole, inner, sides, flux = sums
        first, second = [zero] * 4, [zero] * 4
        tracer = [
            scalar_mix(masked[2, 16 * a + i + 1], masked[3, 16 * a + i + 1]) for i in range(16)
        ]
        terms = lat_terms(jnp.concatenate(tracer, axis=0), matrix)
        for i in range(16):
            k = 16 * a + i
            m = [masked[f, k + 1] for f in range(4)]
            for f in range(4):
                if i < 8:
                    first[f] = jnp.where(high == i, by_lanes(m[f], 16 * i - 120), first[f])
                else:
                    second[f] = jnp.where(low == i - 8, by_lanes(m[f], 16 * i - 240), second[f])
            w = tracer[i]
            n1 = jnp.where(row < 7, by_rows(w, -1), 0.0)
            p1 = jnp.where(row > 0, by_rows(w, 1), 0.0)
            n2 = jnp.where(row < 6, by_rows(w, -2), 0.0)
            p2 = jnp.where(row > 1, by_rows(w, 2), 0.0)
            gx = 8.0 * (n1 - p1) - (n2 - p2)
            gy = terms[8 * i : 8 * i + 8, :LANES]
            around = (n1 + p1) + terms[8 * i : 8 * i + 8, LANES:]
            whole = whole + w
            inner = inner + jnp.where(k + 1 < levels, w, 0.0)
            sides = sides + jnp.where(k < levels, around, 0.0)
            flux = flux + (m[0] * gx + m[1] * gy)
        for f in range(4):
            right = jnp.where(in_even, first[f], second[f])
            left = by_lanes(jnp.where(in_even, second[f], first[f]), -8)
            where = pl.ds(pl.multiple_of(f * 32 + 8 * a, 8), 8)
            odd_out[where, :] = jnp.where(is_even, left, right)
            even_out[where, :] = jnp.where(is_even, right, left)
        return whole, inner, sides, flux

    whole, inner, sides, flux = lax.fori_loop(0, 4, tile, (zero,) * 4, unroll=True)
    top = scalar_mix(masked[2, 1], masked[3, 1])
    acc = 0.1 * (0.94 * whole + 0.02 * (whole - top + inner) + 0.005 * sides - ADV * flux)
    partial[...] = acc
    slot = lane >> 3
    left = right = zero
    for i, x in enumerate((acc, elev, diag, depth)):
        left = jnp.where(slot == i, by_lanes(x, 8 * i), left)
        right = jnp.where(slot == i, by_lanes(x, 8 * i - 120), right)
    odd_out[128:136, :] = jnp.where(is_even, left, right)
    even_out[128:136, :] = jnp.where(is_even, right, left)


def tile_lanes(x):
    return sum_slots(jnp.where(lanes_of() < 8, x, 0.0))


def sum_slots(x):
    for d in (8, 32):
        x = (x + by_lanes(x, d)) + (by_lanes(x, 2 * d) + by_lanes(x, 3 * d))
    return x


def wet_pack(depth, a):
    slot = lanes_of() >> 3
    return (16 * a + (slot >> 1) + 8 * (slot & 1)).astype(F32) < depth


def west_part(vel, depth, east, i):
    column = lanes_of() & 7
    y1 = jnp.where(column == 7, by_lanes(east, 7), 0.0)
    y2 = jnp.where(column >= 6, by_lanes(east, 6), 0.0)
    return 0.005 * jnp.where(wet_pack(depth, i), y1, 0.0) - ADV * vel * (8.0 * y1 - y2)


def east_part(vel, depth, west, i):
    column = lanes_of() & 7
    z1 = jnp.where(column == 0, by_lanes(west, -7), 0.0)
    z2 = jnp.where(column <= 1, by_lanes(west, -6), 0.0)
    return 0.005 * jnp.where(wet_pack(depth, i), z1, 0.0) - ADV * vel * (z2 - 8.0 * z1)


def lat_rims(a_v, a_w, a_depth, b_v, b_w, b_depth):
    a_sum = b_sum = jnp.zeros((ROWS, LANES), F32)
    for i in range(4):
        a_sum = a_sum + west_part(a_v[i], a_depth, b_w[i], i)
        b_sum = b_sum + east_part(b_v[i], b_depth, a_w[i], i)
    return 0.1 * sum_slots(a_sum), 0.1 * sum_slots(b_sum)


class Either:
    def __init__(self, first, second):
        self.refs = (first, second)

    def __getitem__(self, at):
        first, second = self.refs
        return first[at] + second[at]


def four(ref, base, flag, other):
    at = [slice(base + 8 * i, base + 8 * i + 8) for i in range(4)]
    return [jnp.where(flag, ref[x, :], other[x, :]) for x in at]


def forcing(
    parity, got_late, got_odd, got_early, own_odd, own_even,
    own_odd_lat, own_even_lat, got_odd_lat, got_even_lat, partial,
    odd_out, even_out,
):
    got_even = Either(got_early, got_late)
    row, lane = rows_of(), lanes_of()
    lon_even, lat_even = parity[0] == 0, parity[1] == 0
    elev, diag, depth = flat_of(own_odd)
    total = elev + partial[...]

    r = row & 1
    for lower in (True, False):
        rim = row < 2 if lower else row >= 6
        tiled = jnp.where(rim, depth, 0.0)
        tiled = tiled + by_rows(tiled, 2)
        tiled = tiled + by_rows(tiled, 4)
        acc = jnp.zeros((ROWS, LANES), F32)
        own_first = lon_even if lower else jnp.logical_not(lon_even)
        for g in range(16):
            at = slice(8 * g, 8 * g + 8)
            at_t = slice(2 * STRIP + 8 * g, 2 * STRIP + 8 * g + 8)
            at_s = slice(3 * STRIP + 8 * g, 3 * STRIP + 8 * g + 8)
            vel = jnp.where(own_first, own_odd[at, :], own_even[at, :])
            w = scalar_mix(
                jnp.where(own_first, got_odd[at_t, :], got_even[at_t, :]),
                jnp.where(own_first, got_odd[at_s, :], got_even[at_s, :]),
            )
            wet = (4 * g + (row >> 1)).astype(F32) < tiled
            if lower:
                near = jnp.where(r == 0, by_rows(w, -1), 0.0)
                slope = w - 8.0 * near
            else:
                near = jnp.where(r == 1, by_rows(w, 1), 0.0)
                slope = 8.0 * near - w
            acc = acc + (0.005 * jnp.where(wet, near, 0.0) - ADV * vel * slope)
        acc = acc + by_rows(acc, 2)
        acc = acc + by_rows(acc, 4)
        total = total + jnp.where(rim, 0.1 * acc, 0.0)

    own_r = [four(own_even_lat, f * 32, lat_even, own_odd_lat) for f in range(1, 4)]
    own_l = [four(own_odd_lat, f * 32, lat_even, own_even_lat) for f in range(1, 4)]
    ext_r = [four(got_even_lat, f * 32, lat_even, got_odd_lat) for f in range(4)]
    ext_l = [four(got_odd_lat, f * 32, lat_even, got_even_lat) for f in range(4)]
    flat_r = jnp.where(lat_even, got_even_lat[128:136, :], got_odd_lat[128:136, :])
    flat_l = jnp.where(lat_even, got_odd_lat[128:136, :], got_even_lat[128:136, :])
    depth_r = jnp.where(lat_even, got_even_lat[136:144, :], got_odd_lat[136:144, :])
    depth_l = jnp.where(lat_even, got_odd_lat[136:144, :], got_even_lat[136:144, :])
    own_depth_r = jnp.where(lat_even, own_even_lat[136:144, :], own_odd_lat[136:144, :])
    own_depth_l = jnp.where(lat_even, own_odd_lat[136:144, :], own_even_lat[136:144, :])

    def mixed(pair):
        return [scalar_mix(x, y) for x, y in zip(*pair, strict=True)]

    w_r, w_l = mixed(ext_r[2:]), mixed(ext_l[2:])
    miss_own_r, miss_ext_r = lat_rims(
        own_r[0], mixed(own_r[1:]), own_depth_r, ext_r[1], w_r, depth_r
    )
    miss_ext_l, miss_own_l = lat_rims(
        ext_l[1], w_l, depth_l, own_l[0], mixed(own_l[1:]), own_depth_l
    )
    total = total + jnp.where(lane >= 126, miss_own_r, 0.0) + jnp.where(lane < 2, miss_own_l, 0.0)

    def side(i):
        return jnp.where(
            lane < 8,
            by_lanes(flat_r, -8 * i),
            jnp.where(lane >= 120, by_lanes(flat_l, 120 - 8 * i), 0.0),
        )

    elev_side = side(1)
    total_side = side(0) + elev_side
    total_side = total_side + jnp.where(lane < 2, miss_ext_r, 0.0)
    total_side = total_side + jnp.where(lane >= 126, miss_ext_l, 0.0)
    for ref in (odd_out, even_out):
        for i, x in enumerate((total, total_side, elev_side, side(2), side(3))):
            ref[8 * i : 8 * i + 8, :] = x
    packs = ext_r[0] + ext_l[0] + w_r + w_l + [depth_r, depth_l]
    group = row >> 1
    for i in range(5):
        top = bottom = jnp.zeros((ROWS, LANES), F32)
        for j, x in enumerate(packs[4 * i : 4 * i + 4]):
            top = jnp.where(group == j, by_rows(x, 2 * j), top)
            bottom = jnp.where(group == j, by_rows(x, 2 * j - 6), bottom)
        at = slice(40 + 8 * i, 48 + 8 * i)
        odd_out[at, :] = jnp.where(lon_even, top, bottom)
        even_out[at, :] = jnp.where(lon_even, bottom, top)


CHUNKS = ((0, 5), (5, 10), (10, 15))


def fields(
    parity, masked, own_lon, own_odd_lat, own_even_lat, late_lon, odd_lon, early_lon, odd_lat, even_lat,
    o1, o2, o3, o4, terms, rims, fresh, sems,
):
    even_lon = Either(early_lon, late_lon)
    row, lane = rows_of(), lanes_of()
    levels = flat_of(own_lon)[2].astype(jnp.int32)
    lon_even, lat_even = parity[0] == 0, parity[1] == 0
    outs = (o1, o2, o3, o4)
    at_edge = (lane < 2) | (lane >= 126)

    matrix = lat_matrix()
    for f in range(4):
        for first in range(0, LEVELS, 16):
            count = min(16, LEVELS - first)
            x = masked[f, first + 1 : first + 1 + count].reshape(count * ROWS, LANES)
            terms[f, ROWS * first : ROWS * (first + count), :] = lat_terms(x, matrix)

    in_even = (lane & 8) == 0

    def west_east(odd, even, base):
        x, y = odd[base : base + 8, :], even[base : base + 8, :]
        return jnp.where(lat_even, x, y), jnp.where(lat_even, y, x)

    depth_west, depth_east = west_east(own_odd_lat, own_even_lat, 136)
    for a in range(4):
        vel_west, vel_east = west_east(own_odd_lat, own_even_lat, 32 + 8 * a)
        for f in range(4):
            west, east = west_east(odd_lat, even_lat, f * 32 + 8 * a)
            right = west_part(vel_east, depth_east, east, a)
            left = by_lanes(east_part(vel_west, depth_west, west, a), 8)
            first = jnp.where(in_even, right, left)
            second = jnp.where(in_even, left, right)
            for i in range(8):
                rims[f, 16 * a + i] = by_lanes(first, -16 * i - 8)
                rims[f, 16 * a + 8 + i] = by_lanes(second, -16 * i - 16)

    def group(g, count):
        strips = []
        for f in range(4):
            at = pl.ds(pl.multiple_of(f * STRIP + 8 * g, 8), 8)
            x, y = odd_lon[at, :], even_lon[at, :]
            strips.append((jnp.where(lon_even, y, x), jnp.where(lon_even, x, y)))
        for j in range(count):
            k = 4 * g + j
            wet = k < levels
            center = [masked[f, k + 1] for f in range(4)]
            zonal, merid = ADV * center[0], ADV * center[1]
            at = pl.ds(pl.multiple_of(ROWS * k, ROWS), ROWS)
            for f in range(4):
                m = center[f]
                upper, lower = strips[f]
                rim = jnp.where(row < 4, by_rows(upper, -2 * j), by_rows(lower, 6 - 2 * j))
                n1 = by_rows(jnp.where(row < 1, rim, m), -1)
                n2 = by_rows(jnp.where(row < 2, rim, m), -2)
                p1 = by_rows(jnp.where(row > 6, rim, m), 1)
                p2 = by_rows(jnp.where(row > 5, rim, m), 2)
                gx = 8.0 * (n1 - p1) - (n2 - p2)
                gy = terms[f, at, :LANES]
                around = (n1 + p1) + terms[f, at, LANES:]
                column = masked[f, k] + masked[f, k + 2]
                value = 0.94 * m + 0.02 * column + 0.005 * around - (zonal * gx + merid * gy)
                fresh[f, k] = jnp.where(wet, value, 0.0) + jnp.where(at_edge, rims[f, k], 0.0)

    def body(g, carry):
        group(g, 4)
        return carry

    copies = []

    def send(first, last):
        for f in range(4):
            copies.append(
                pltpu.make_async_copy(
                    fresh.at[f, first:last], outs[f].at[first:last], sems.at[len(copies)]
                )
            )
            copies[-1].start()

    for first, last in CHUNKS:
        lax.fori_loop(first, last, body, 0, unroll=True)
        send(4 * first, 4 * last)
    group(15, LEVELS - 60)
    send(60, LEVELS)
    for copy in copies:
        copy.wait()


def solve(
    parity, odd_b, even_b, own_b, own_lon, late_lon, odd_lon, early_lon, odd_lat, even_lat, height
):
    even_lon = Either(early_lon, late_lon)
    row, lane = rows_of(), lanes_of()
    lon_even, lat_even = parity[0] == 0, parity[1] == 0
    lower = [jnp.where(lon_even, odd_b[8 * i : 8 * i + 8, :], even_b[8 * i : 8 * i + 8, :]) for i in range(10)]
    upper = [jnp.where(lon_even, even_b[8 * i : 8 * i + 8, :], odd_b[8 * i : 8 * i + 8, :]) for i in range(10)]
    own = [own_b[8 * i : 8 * i + 8, :] for i in range(5)]

    ext_r = [four(even_lat, f * 32, lat_even, odd_lat) for f in (0, 2, 3)]
    ext_l = [four(odd_lat, f * 32, lat_even, even_lat) for f in (0, 2, 3)]

    def lon_part(vel, wet, x1, x2):
        slope = jnp.where(row == 0, -8.0 * x1, jnp.where(row == 7, 8.0 * x1, 0.0))
        slope = slope + jnp.where(row < 2, x2, jnp.where(row >= 6, -x2, 0.0))
        near = jnp.where((row == 0) | (row == 7), x1, 0.0)
        return 0.005 * jnp.where(wet, near, 0.0) - ADV * vel * slope

    def rim_rows(tile, q, first):
        return by_rows(tile[5 + q // 4], first - 2 * (q % 4))

    def near_rows(q):
        return jnp.where(row < 4, rim_rows(upper, q, 0), rim_rows(lower, q, 6))

    def side_parts(ext, base, own_depth, near_depth):
        mine = theirs = jnp.zeros((ROWS, LANES), F32)
        for i in range(4):
            vel, w = ext[0][i], scalar_mix(ext[1][i], ext[2][i])
            qu, qw = base + i, 8 + base + i
            x2 = jnp.where(row < 4, rim_rows(lower, qw, 0), rim_rows(upper, qw, 6))
            x1 = jnp.where(row < 4, rim_rows(lower, qw, -1), rim_rows(upper, qw, 7))
            mine = mine + lon_part(vel, wet_pack(own_depth, i), x1, x2)
            y2 = jnp.where(row < 4, by_rows(w, 2), by_rows(w, -2))
            y1 = jnp.where(row < 4, by_rows(w, 1), by_rows(w, -1))
            theirs = theirs + lon_part(near_rows(qu), wet_pack(near_depth, i), y1, y2)
        return 0.1 * sum_slots(mine), 0.1 * sum_slots(theirs)

    depth_r = jnp.where(lat_even, even_lat[136:144, :], odd_lat[136:144, :])
    depth_l = jnp.where(lat_even, odd_lat[136:144, :], even_lat[136:144, :])
    mine_r, theirs_r = side_parts(ext_r, 0, depth_r, near_rows(16))
    mine_l, theirs_l = side_parts(ext_l, 4, depth_l, near_rows(17))
    in_r, in_l = lane < 8, lane >= 120
    mine = jnp.where(in_r, mine_r, jnp.where(in_l, mine_l, 0.0))
    theirs = jnp.where(in_r, theirs_r, jnp.where(in_l, theirs_l, 0.0))

    flat_own = flat_of(own_lon)
    flat_odd, flat_even = flat_of(odd_lon), flat_of(even_lon)
    flat_low = [jnp.where(lon_even, x, y) for x, y in zip(flat_odd, flat_even, strict=True)]
    flat_up = [jnp.where(lon_even, y, x) for x, y in zip(flat_odd, flat_even, strict=True)]

    rhs = [
        lower[0], own[0], upper[0],
        lower[1] + jnp.where(row >= 6, theirs, 0.0),
        own[1] + mine,
        upper[1] + jnp.where(row < 2, theirs, 0.0),
    ]
    elev = [flat_low[0], flat_own[0], flat_up[0], lower[2], own[2], upper[2]]
    diag = [flat_low[1], flat_own[1], flat_up[1], lower[3], own[3], upper[3]]
    wet = [x > 0.0 for x in (flat_low[2], flat_own[2], flat_up[2], lower[4], own[4], upper[4])]
    diag = [x + 4.0 for x in diag]
    inverse = [1.0 / x for x in diag]
    coupled = [jnp.where(a, x, 0.0) for a, x in zip(wet, inverse, strict=True)]

    def neighbours(x):
        out = []
        up = [by_rows(y, -1) for y in x]
        down = [by_rows(y, 1) for y in x]
        east = [by_lanes(y, -1) for y in x]
        west = [by_lanes(y, 1) for y in x]
        for i in range(6):
            h, c = divmod(i, 3)
            base = 3 * h
            other = 3 * (1 - h) + c
            n = jnp.where(row < 7, up[i], up[base + (c + 1) % 3])
            p = jnp.where(row > 0, down[i], down[base + (c + 2) % 3])
            e = jnp.where(lane < 127, east[i], east[other])
            w = jnp.where(lane > 0, west[i], west[other])
            out.append((n + p) + (e + w))
        return out

    sigma = SPECTRUM_MID / SPECTRUM_HALF
    ratio = 1.0 / sigma
    scaled = [x * y for x, y in zip(rhs, inverse, strict=True)]
    previous = elev
    iterate = elev[1]
    for step in range(ITERS):
        around = neighbours([jnp.where(a, x, 0.0) for a, x in zip(wet, previous, strict=True)])
        scaled = [
            (res - x) + c * n
            for res, x, c, n in zip(scaled, previous, coupled, around, strict=True)
        ]
        if step == 0:
            previous = [res / SPECTRUM_MID for res in scaled]
        else:
            following = 1.0 / (2.0 * sigma - ratio)
            keep, gain = following * ratio, 2.0 * following / SPECTRUM_HALF
            previous = [keep * x + gain * res for x, res in zip(previous, scaled, strict=True)]
            ratio = following
        iterate = iterate + previous[1]
    height[...] = iterate


def shaped(*shape):
    return jax.ShapeDtypeStruct(shape, F32)


def call(kernel, outs, ins, flops, moved, **kw):
    return pl.pallas_call(
        kernel,
        out_shape=outs,
        in_specs=ins,
        compiler_params=pltpu.CompilerParams(vmem_limit_bytes=VMEM),
        cost_estimate=pl.CostEstimate(flops=flops, bytes_accessed=moved, transcendentals=0),
        **kw,
    )


SMEM = pl.BlockSpec(memory_space=pltpu.SMEM)
WHOLE = pl.BlockSpec(memory_space=pltpu.VMEM)
HERE = pl.BlockSpec(memory_space=pltpu.HBM)
BLOCK = 4 * LEVELS * ROWS * LANES * 4


def call_pack_lon(*args):
    return call(
        pack_lon,
        (shaped(4, LEVELS + 4, ROWS, LANES), shaped(LON_ROWS, LANES), shaped(LON_ROWS, LANES)),
        [HERE] * 8 + [SMEM], 10**6, 2 * BLOCK,
        out_specs=(WHOLE,) * 3,
        scratch_shapes=[
            pltpu.VMEM((4, LEVELS, ROWS, LANES), F32),
            pltpu.VMEM((2, ROWS, LANES), jnp.int32),
            pltpu.VMEM((2, ROWS, LANES), F32),
            pltpu.SemaphoreType.DMA((8,)),
        ],
    )(*args)


def call_pack_lat(*args):
    return call(
        pack_lat, (shaped(LAT_ROWS, LANES), shaped(LAT_ROWS, LANES), shaped(ROWS, LANES)),
        [WHOLE] * 2 + [SMEM], 4 * 10**6, BLOCK,
    )(*args)


def call_forcing(*args):
    return call(
        forcing, (shaped(SOLVE_ROWS, LANES),) * 2, [SMEM] + [WHOLE] * 10, 10**6, 10**6
    )(*args)


def call_fields(*args):
    return call(
        fields, (shaped(LEVELS, ROWS, LANES),) * 4, [SMEM] + [WHOLE] * 9, 10**7, 3 * BLOCK,
        out_specs=(HERE,) * 4,
        scratch_shapes=[
            pltpu.VMEM((4, LEVELS * ROWS, 2 * LANES), F32),
            pltpu.VMEM((4, LEVELS + 2, ROWS, LANES), F32),
            pltpu.VMEM((4, LEVELS, ROWS, LANES), F32),
            pltpu.SemaphoreType.DMA((16,)),
        ],
    )(*args)


def call_solve(*args):
    return call(solve, shaped(ROWS, LANES), [SMEM] + [WHOLE] * 9, 10**6, 10**6)(*args)


RUN, EARLY = 8, 2


def on_device(u, v, t, s, water, layers, diag, elev):
    lon, lat = lax.axis_size("lon"), lax.axis_size("lat")
    lon_even = [(i, i ^ 1) for i in range(lon)]
    lon_odd = [(i, (((i + 1) ^ 1) - 1) % lon) for i in range(lon)]
    lat_even = [(i, i ^ 1) for i in range(lat)]
    lat_odd = [(i, ((i + 1) ^ 1) - 1) for i in range(1, lat - 1)]
    early = [(a, b) for a, b in lon_even if a % RUN < EARLY]
    late = [(a, b) for a, b in lon_even if a % RUN >= EARLY]
    parity = jnp.stack([lax.axis_index("lon") & 1, lax.axis_index("lat") & 1]).astype(jnp.int32)

    raw = [
        pltpu.with_memory_space_constraint(x, pltpu.HBM)
        for x in (u, v, t, s, water, layers, diag, elev)
    ]
    masked, own_odd, own_even = call_pack_lon(*raw, parity)
    got_early = lax.ppermute(own_even, "lon", early)
    own_odd = own_odd.at[TIED:].set(got_early[TIED:])
    own_even = own_even.at[TIED:].set(got_early[TIED:])
    got_odd = lax.ppermute(own_odd, "lon", lon_odd)
    got_late = lax.ppermute(own_even, "lon", late)
    lat_own_odd, lat_own_even, partial = call_pack_lat(masked, own_odd, parity)
    lat_got_odd = lax.ppermute(lat_own_odd, "lat", lat_odd)
    lat_got_even = lax.ppermute(lat_own_even, "lat", lat_even)

    b_odd, b_even = call_forcing(
        parity, got_late, got_odd, got_early, own_odd, own_even,
        lat_own_odd, lat_own_even, lat_got_odd, lat_got_even, partial,
    )
    b_got_odd = lax.ppermute(b_odd, "lon", lon_odd)
    b_got_even = lax.ppermute(b_even, "lon", lon_even)

    fresh = call_fields(
        parity, masked, own_odd, lat_own_odd, lat_own_even, got_late, got_odd, got_early,
        lat_got_odd, lat_got_even,
    )
    height = call_solve(
        parity, b_got_odd, b_got_even, b_odd, own_odd, got_late, got_odd, got_early,
        lat_got_odd, lat_got_even,
    )
    return (*fresh, height)


def solution(mesh):
    field, flat = P(None, "lon", "lat"), P("lon", "lat")
    return jax.shard_map(
        on_device,
        mesh=mesh,
        in_specs=(field,) * 4 + (flat,) * 4,
        out_specs=(field,) * 4 + (flat,),
        check_vma=False,
    )
```

```python
import jax
import jax.numpy as jnp
from jax import lax
from jax.experimental import pallas as pl
from jax.experimental.pallas import tpu as pltpu
from jax.sharding import PartitionSpec as P

ITERS = 8
LEVELS = 62
SPECTRUM_MID = 1.0
SPECTRUM_HALF = 0.995

ROWS = 8
LANES = 128
STRIP = 128
FLAT = 4 * STRIP
LON_ROWS = FLAT + 3 * ROWS
LAT_ROWS = 18 * ROWS
SOLVE_ROWS = 5 * ROWS + 5 * ROWS
VMEM = 12 * 1024 * 1024

F32 = jnp.float32
ADV = 0.1 / 12.0


def rows_of(shape=(ROWS, LANES)):
    return lax.broadcasted_iota(jnp.int32, shape, 0)


def lanes_of(shape=(ROWS, LANES)):
    return lax.broadcasted_iota(jnp.int32, shape, 1)


def by_rows(x, d):
    d %= ROWS
    return pltpu.roll(x, d, 0) if d else x


def by_lanes(x, d):
    d %= LANES
    return pltpu.roll(x, d, 1) if d else x


def scalar_mix(t, s):
    return 0.7 * t - 0.5 * s


def even(axis):
    return lax.axis_index(axis) % 2 == 0


def flat_of(ref, base=FLAT):
    return [ref[base + 8 * i : base + 8 * i + 8, :] for i in range(3)]


def pack_lon(
    u, v, t, s, water, layers, diag, elev, parity, masked, up_first, low_first, held, held_int, held_flat, sems
):
    copies = [
        pltpu.make_async_copy(src, held.at[i], sems.at[i]) for i, src in enumerate((u, v, t, s))
    ]
    small = [
        pltpu.make_async_copy(water, held_int.at[0], sems.at[4]),
        pltpu.make_async_copy(layers, held_int.at[1], sems.at[5]),
        pltpu.make_async_copy(elev, held_flat.at[0], sems.at[6]),
        pltpu.make_async_copy(diag, held_flat.at[1], sems.at[7]),
    ]
    for copy in small[:2] + copies + small[2:]:
        copy.start()
    for copy in small[:2]:
        copy.wait()
    row = rows_of()
    group = row >> 1
    depth = held_int[0] * held_int[1]
    is_even = parity[0] == 0

    for f in range(4):
        masked[f, 0] = jnp.zeros((ROWS, LANES), F32)
        masked[f, LEVELS + 3] = jnp.zeros((ROWS, LANES), F32)
        copies[f].wait()

        def body(g, carry, f=f):
            top = bottom = None
            for i in range(4):
                k = 4 * g + i
                m = jnp.where(k < depth, held[f, jnp.minimum(k, LEVELS - 1)], 0.0)
                masked[f, k + 1] = m
                a, b = by_rows(m, 2 * i), by_rows(m, 2 * i - 6)
                top = a if i == 0 else jnp.where(group == i, a, top)
                bottom = b if i == 0 else jnp.where(group == i, b, bottom)
            at = pl.ds(pl.multiple_of(f * STRIP + 8 * g, 8), 8)
            up_first[at, :] = jnp.where(is_even, top, bottom)
            low_first[at, :] = jnp.where(is_even, bottom, top)
            return carry

        lax.fori_loop(0, 16, body, 0, unroll=True)

    for copy in small[2:]:
        copy.wait()
    for ref in (up_first, low_first):
        ref[FLAT : FLAT + 8, :] = held_flat[0]
        ref[FLAT + 8 : FLAT + 16, :] = held_flat[1]
        ref[FLAT + 16 : FLAT + 24, :] = depth.astype(F32)


BF16 = jnp.bfloat16


def lat_matrix():
    shape = (2 * LANES, 2 * LANES)
    source = rows_of(shape) & 127
    target = lanes_of(shape)
    d = source - (target & 127)
    slope = jnp.where(d == 1, 8.0, jnp.where(d == -1, -8.0, 0.0))
    slope = slope + jnp.where(d == 2, -1.0, jnp.where(d == -2, 1.0, 0.0))
    near = jnp.where(jnp.abs(d) == 1, 1.0, 0.0)
    return jnp.where(target < LANES, slope, near).astype(BF16)


def lat_terms(x, matrix):
    high = x.astype(BF16)
    rest = (x - high.astype(F32)).astype(BF16)
    return jnp.dot(jnp.concatenate([high, rest], axis=1), matrix, preferred_element_type=F32)


def pack_lat(masked, own_lon, parity, odd_out, even_out, partial):
    row, lane = rows_of(), lanes_of()
    high, low = lane >> 4, ((lane - 8) & 127) >> 4
    in_even = (lane & 8) == 0
    elev, diag, depth = flat_of(own_lon)
    levels = depth.astype(jnp.int32)
    is_even = parity[1] == 0
    zero = jnp.zeros((ROWS, LANES), F32)
    matrix = lat_matrix()
    left, right = tile_lanes(depth), tile_lanes(by_lanes(depth, 8))
    odd_out[136:144, :] = jnp.where(is_even, left, right)
    even_out[136:144, :] = jnp.where(is_even, right, left)

    def tile(a, sums):
        whole, inner, sides, flux = sums
        first, second = [zero] * 4, [zero] * 4
        tracer = [
            scalar_mix(masked[2, 16 * a + i + 1], masked[3, 16 * a + i + 1]) for i in range(16)
        ]
        terms = lat_terms(jnp.concatenate(tracer, axis=0), matrix)
        for i in range(16):
            k = 16 * a + i
            m = [masked[f, k + 1] for f in range(4)]
            for f in range(4):
                if i < 8:
                    first[f] = jnp.where(high == i, by_lanes(m[f], 16 * i - 120), first[f])
                else:
                    second[f] = jnp.where(low == i - 8, by_lanes(m[f], 16 * i - 240), second[f])
            w = tracer[i]
            n1 = jnp.where(row < 7, by_rows(w, -1), 0.0)
            p1 = jnp.where(row > 0, by_rows(w, 1), 0.0)
            n2 = jnp.where(row < 6, by_rows(w, -2), 0.0)
            p2 = jnp.where(row > 1, by_rows(w, 2), 0.0)
            gx = 8.0 * (n1 - p1) - (n2 - p2)
            gy = terms[8 * i : 8 * i + 8, :LANES]
            around = (n1 + p1) + terms[8 * i : 8 * i + 8, LANES:]
            whole = whole + w
            inner = inner + jnp.where(k + 1 < levels, w, 0.0)
            sides = sides + jnp.where(k < levels, around, 0.0)
            flux = flux + (m[0] * gx + m[1] * gy)
        for f in range(4):
            right = jnp.where(in_even, first[f], second[f])
            left = by_lanes(jnp.where(in_even, second[f], first[f]), -8)
            where = pl.ds(pl.multiple_of(f * 32 + 8 * a, 8), 8)
            odd_out[where, :] = jnp.where(is_even, left, right)
            even_out[where, :] = jnp.where(is_even, right, left)
        return whole, inner, sides, flux

    whole, inner, sides, flux = lax.fori_loop(0, 4, tile, (zero,) * 4, unroll=True)
    top = scalar_mix(masked[2, 1], masked[3, 1])
    acc = 0.1 * (0.94 * whole + 0.02 * (whole - top + inner) + 0.005 * sides - ADV * flux)
    partial[...] = acc
    slot = lane >> 3
    left = right = zero
    for i, x in enumerate((acc, elev, diag, depth)):
        left = jnp.where(slot == i, by_lanes(x, 8 * i), left)
        right = jnp.where(slot == i, by_lanes(x, 8 * i - 120), right)
    odd_out[128:136, :] = jnp.where(is_even, left, right)
    even_out[128:136, :] = jnp.where(is_even, right, left)


def tile_lanes(x):
    return sum_slots(jnp.where(lanes_of() < 8, x, 0.0))


def sum_slots(x):
    for d in (8, 32):
        x = (x + by_lanes(x, d)) + (by_lanes(x, 2 * d) + by_lanes(x, 3 * d))
    return x


def wet_pack(depth, a):
    slot = lanes_of() >> 3
    return (16 * a + (slot >> 1) + 8 * (slot & 1)).astype(F32) < depth


def west_part(vel, depth, east, i):
    column = lanes_of() & 7
    y1 = jnp.where(column == 7, by_lanes(east, 7), 0.0)
    y2 = jnp.where(column >= 6, by_lanes(east, 6), 0.0)
    return 0.005 * jnp.where(wet_pack(depth, i), y1, 0.0) - ADV * vel * (8.0 * y1 - y2)


def east_part(vel, depth, west, i):
    column = lanes_of() & 7
    z1 = jnp.where(column == 0, by_lanes(west, -7), 0.0)
    z2 = jnp.where(column <= 1, by_lanes(west, -6), 0.0)
    return 0.005 * jnp.where(wet_pack(depth, i), z1, 0.0) - ADV * vel * (z2 - 8.0 * z1)


def lat_rims(a_v, a_w, a_depth, b_v, b_w, b_depth):
    a_sum = b_sum = jnp.zeros((ROWS, LANES), F32)
    for i in range(4):
        a_sum = a_sum + west_part(a_v[i], a_depth, b_w[i], i)
        b_sum = b_sum + east_part(b_v[i], b_depth, a_w[i], i)
    return 0.1 * sum_slots(a_sum), 0.1 * sum_slots(b_sum)


def four(ref, base, flag, other):
    at = [slice(base + 8 * i, base + 8 * i + 8) for i in range(4)]
    return [jnp.where(flag, ref[x, :], other[x, :]) for x in at]


def forcing(
    parity, got_even, got_odd, own_odd, own_even,
    own_odd_lat, own_even_lat, got_odd_lat, got_even_lat, partial,
    odd_out, even_out,
):
    row, lane = rows_of(), lanes_of()
    lon_even, lat_even = parity[0] == 0, parity[1] == 0
    elev, diag, depth = flat_of(own_odd)
    total = elev + partial[...]

    r = row & 1
    for lower in (True, False):
        rim = row < 2 if lower else row >= 6
        tiled = jnp.where(rim, depth, 0.0)
        tiled = tiled + by_rows(tiled, 2)
        tiled = tiled + by_rows(tiled, 4)
        acc = jnp.zeros((ROWS, LANES), F32)
        own_first = lon_even if lower else jnp.logical_not(lon_even)
        for g in range(16):
            at = slice(8 * g, 8 * g + 8)
            at_t = slice(2 * STRIP + 8 * g, 2 * STRIP + 8 * g + 8)
            at_s = slice(3 * STRIP + 8 * g, 3 * STRIP + 8 * g + 8)
            vel = jnp.where(own_first, own_odd[at, :], own_even[at, :])
            w = scalar_mix(
                jnp.where(own_first, got_odd[at_t, :], got_even[at_t, :]),
                jnp.where(own_first, got_odd[at_s, :], got_even[at_s, :]),
            )
            wet = (4 * g + (row >> 1)).astype(F32) < tiled
            if lower:
                near = jnp.where(r == 0, by_rows(w, -1), 0.0)
                slope = w - 8.0 * near
            else:
                near = jnp.where(r == 1, by_rows(w, 1), 0.0)
                slope = 8.0 * near - w
            acc = acc + (0.005 * jnp.where(wet, near, 0.0) - ADV * vel * slope)
        acc = acc + by_rows(acc, 2)
        acc = acc + by_rows(acc, 4)
        total = total + jnp.where(rim, 0.1 * acc, 0.0)

    own_r = [four(own_even_lat, f * 32, lat_even, own_odd_lat) for f in range(1, 4)]
    own_l = [four(own_odd_lat, f * 32, lat_even, own_even_lat) for f in range(1, 4)]
    ext_r = [four(got_even_lat, f * 32, lat_even, got_odd_lat) for f in range(4)]
    ext_l = [four(got_odd_lat, f * 32, lat_even, got_even_lat) for f in range(4)]
    flat_r = jnp.where(lat_even, got_even_lat[128:136, :], got_odd_lat[128:136, :])
    flat_l = jnp.where(lat_even, got_odd_lat[128:136, :], got_even_lat[128:136, :])
    depth_r = jnp.where(lat_even, got_even_lat[136:144, :], got_odd_lat[136:144, :])
    depth_l = jnp.where(lat_even, got_odd_lat[136:144, :], got_even_lat[136:144, :])
    own_depth_r = jnp.where(lat_even, own_even_lat[136:144, :], own_odd_lat[136:144, :])
    own_depth_l = jnp.where(lat_even, own_odd_lat[136:144, :], own_even_lat[136:144, :])

    def mixed(pair):
        return [scalar_mix(x, y) for x, y in zip(*pair, strict=True)]

    w_r, w_l = mixed(ext_r[2:]), mixed(ext_l[2:])
    miss_own_r, miss_ext_r = lat_rims(
        own_r[0], mixed(own_r[1:]), own_depth_r, ext_r[1], w_r, depth_r
    )
    miss_ext_l, miss_own_l = lat_rims(
        ext_l[1], w_l, depth_l, own_l[0], mixed(own_l[1:]), own_depth_l
    )
    total = total + jnp.where(lane >= 126, miss_own_r, 0.0) + jnp.where(lane < 2, miss_own_l, 0.0)

    def side(i):
        return jnp.where(
            lane < 8,
            by_lanes(flat_r, -8 * i),
            jnp.where(lane >= 120, by_lanes(flat_l, 120 - 8 * i), 0.0),
        )

    elev_side = side(1)
    total_side = side(0) + elev_side
    total_side = total_side + jnp.where(lane < 2, miss_ext_r, 0.0)
    total_side = total_side + jnp.where(lane >= 126, miss_ext_l, 0.0)
    for ref in (odd_out, even_out):
        for i, x in enumerate((total, total_side, elev_side, side(2), side(3))):
            ref[8 * i : 8 * i + 8, :] = x
    packs = ext_r[0] + ext_l[0] + w_r + w_l + [depth_r, depth_l]
    group = row >> 1
    for i in range(5):
        top = bottom = jnp.zeros((ROWS, LANES), F32)
        for j, x in enumerate(packs[4 * i : 4 * i + 4]):
            top = jnp.where(group == j, by_rows(x, 2 * j), top)
            bottom = jnp.where(group == j, by_rows(x, 2 * j - 6), bottom)
        at = slice(40 + 8 * i, 48 + 8 * i)
        odd_out[at, :] = jnp.where(lon_even, top, bottom)
        even_out[at, :] = jnp.where(lon_even, bottom, top)


CHUNKS = ((0, 5), (5, 10), (10, 15))


def fields(
    parity, masked, own_lon, own_odd_lat, own_even_lat, odd_lon, even_lon, odd_lat, even_lat,
    o1, o2, o3, o4, terms, rims, fresh, sems,
):
    row, lane = rows_of(), lanes_of()
    levels = flat_of(own_lon)[2].astype(jnp.int32)
    lon_even, lat_even = parity[0] == 0, parity[1] == 0
    outs = (o1, o2, o3, o4)
    at_edge = (lane < 2) | (lane >= 126)

    matrix = lat_matrix()
    for f in range(4):
        for first in range(0, LEVELS, 16):
            count = min(16, LEVELS - first)
            x = masked[f, first + 1 : first + 1 + count].reshape(count * ROWS, LANES)
            terms[f, ROWS * first : ROWS * (first + count), :] = lat_terms(x, matrix)

    in_even = (lane & 8) == 0

    def west_east(odd, even, base):
        x, y = odd[base : base + 8, :], even[base : base + 8, :]
        return jnp.where(lat_even, x, y), jnp.where(lat_even, y, x)

    depth_west, depth_east = west_east(own_odd_lat, own_even_lat, 136)
    for a in range(4):
        vel_west, vel_east = west_east(own_odd_lat, own_even_lat, 32 + 8 * a)
        for f in range(4):
            west, east = west_east(odd_lat, even_lat, f * 32 + 8 * a)
            right = west_part(vel_east, depth_east, east, a)
            left = by_lanes(east_part(vel_west, depth_west, west, a), 8)
            first = jnp.where(in_even, right, left)
            second = jnp.where(in_even, left, right)
            for i in range(8):
                rims[f, 16 * a + i] = by_lanes(first, -16 * i - 8)
                rims[f, 16 * a + 8 + i] = by_lanes(second, -16 * i - 16)

    def group(g, count):
        strips = []
        for f in range(4):
            at = pl.ds(pl.multiple_of(f * STRIP + 8 * g, 8), 8)
            x, y = odd_lon[at, :], even_lon[at, :]
            strips.append((jnp.where(lon_even, y, x), jnp.where(lon_even, x, y)))
        for j in range(count):
            k = 4 * g + j
            wet = k < levels
            center = [masked[f, k + 1] for f in range(4)]
            zonal, merid = ADV * center[0], ADV * center[1]
            at = pl.ds(pl.multiple_of(ROWS * k, ROWS), ROWS)
            for f in range(4):
                m = center[f]
                upper, lower = strips[f]
                rim = jnp.where(row < 4, by_rows(upper, -2 * j), by_rows(lower, 6 - 2 * j))
                n1 = by_rows(jnp.where(row < 1, rim, m), -1)
                n2 = by_rows(jnp.where(row < 2, rim, m), -2)
                p1 = by_rows(jnp.where(row > 6, rim, m), 1)
                p2 = by_rows(jnp.where(row > 5, rim, m), 2)
                gx = 8.0 * (n1 - p1) - (n2 - p2)
                gy = terms[f, at, :LANES]
                around = (n1 + p1) + terms[f, at, LANES:]
                column = masked[f, k] + masked[f, k + 2]
                value = 0.94 * m + 0.02 * column + 0.005 * around - (zonal * gx + merid * gy)
                fresh[f, k] = jnp.where(wet, value, 0.0) + jnp.where(at_edge, rims[f, k], 0.0)

    def body(g, carry):
        group(g, 4)
        return carry

    copies = []

    def send(first, last):
        for f in range(4):
            copies.append(
                pltpu.make_async_copy(
                    fresh.at[f, first:last], outs[f].at[first:last], sems.at[len(copies)]
                )
            )
            copies[-1].start()

    for first, last in CHUNKS:
        lax.fori_loop(first, last, body, 0, unroll=True)
        send(4 * first, 4 * last)
    group(15, LEVELS - 60)
    send(60, LEVELS)
    for copy in copies:
        copy.wait()


def solve(
    parity, odd_b, even_b, own_b, own_lon, odd_lon, even_lon, odd_lat, even_lat, height
):
    row, lane = rows_of(), lanes_of()
    lon_even, lat_even = parity[0] == 0, parity[1] == 0
    lower = [jnp.where(lon_even, odd_b[8 * i : 8 * i + 8, :], even_b[8 * i : 8 * i + 8, :]) for i in range(10)]
    upper = [jnp.where(lon_even, even_b[8 * i : 8 * i + 8, :], odd_b[8 * i : 8 * i + 8, :]) for i in range(10)]
    own = [own_b[8 * i : 8 * i + 8, :] for i in range(5)]

    ext_r = [four(even_lat, f * 32, lat_even, odd_lat) for f in (0, 2, 3)]
    ext_l = [four(odd_lat, f * 32, lat_even, even_lat) for f in (0, 2, 3)]

    def lon_part(vel, wet, x1, x2):
        slope = jnp.where(row == 0, -8.0 * x1, jnp.where(row == 7, 8.0 * x1, 0.0))
        slope = slope + jnp.where(row < 2, x2, jnp.where(row >= 6, -x2, 0.0))
        near = jnp.where((row == 0) | (row == 7), x1, 0.0)
        return 0.005 * jnp.where(wet, near, 0.0) - ADV * vel * slope

    def rim_rows(tile, q, first):
        return by_rows(tile[5 + q // 4], first - 2 * (q % 4))

    def near_rows(q):
        return jnp.where(row < 4, rim_rows(upper, q, 0), rim_rows(lower, q, 6))

    def side_parts(ext, base, own_depth, near_depth):
        mine = theirs = jnp.zeros((ROWS, LANES), F32)
        for i in range(4):
            vel, w = ext[0][i], scalar_mix(ext[1][i], ext[2][i])
            qu, qw = base + i, 8 + base + i
            x2 = jnp.where(row < 4, rim_rows(lower, qw, 0), rim_rows(upper, qw, 6))
            x1 = jnp.where(row < 4, rim_rows(lower, qw, -1), rim_rows(upper, qw, 7))
            mine = mine + lon_part(vel, wet_pack(own_depth, i), x1, x2)
            y2 = jnp.where(row < 4, by_rows(w, 2), by_rows(w, -2))
            y1 = jnp.where(row < 4, by_rows(w, 1), by_rows(w, -1))
            theirs = theirs + lon_part(near_rows(qu), wet_pack(near_depth, i), y1, y2)
        return 0.1 * sum_slots(mine), 0.1 * sum_slots(theirs)

    depth_r = jnp.where(lat_even, even_lat[136:144, :], odd_lat[136:144, :])
    depth_l = jnp.where(lat_even, odd_lat[136:144, :], even_lat[136:144, :])
    mine_r, theirs_r = side_parts(ext_r, 0, depth_r, near_rows(16))
    mine_l, theirs_l = side_parts(ext_l, 4, depth_l, near_rows(17))
    in_r, in_l = lane < 8, lane >= 120
    mine = jnp.where(in_r, mine_r, jnp.where(in_l, mine_l, 0.0))
    theirs = jnp.where(in_r, theirs_r, jnp.where(in_l, theirs_l, 0.0))

    flat_own = flat_of(own_lon)
    flat_odd, flat_even = flat_of(odd_lon), flat_of(even_lon)
    flat_low = [jnp.where(lon_even, x, y) for x, y in zip(flat_odd, flat_even, strict=True)]
    flat_up = [jnp.where(lon_even, y, x) for x, y in zip(flat_odd, flat_even, strict=True)]

    rhs = [
        lower[0], own[0], upper[0],
        lower[1] + jnp.where(row >= 6, theirs, 0.0),
        own[1] + mine,
        upper[1] + jnp.where(row < 2, theirs, 0.0),
    ]
    elev = [flat_low[0], flat_own[0], flat_up[0], lower[2], own[2], upper[2]]
    diag = [flat_low[1], flat_own[1], flat_up[1], lower[3], own[3], upper[3]]
    wet = [x > 0.0 for x in (flat_low[2], flat_own[2], flat_up[2], lower[4], own[4], upper[4])]
    diag = [x + 4.0 for x in diag]
    inverse = [1.0 / x for x in diag]
    coupled = [jnp.where(a, x, 0.0) for a, x in zip(wet, inverse, strict=True)]

    def neighbours(x):
        out = []
        up = [by_rows(y, -1) for y in x]
        down = [by_rows(y, 1) for y in x]
        east = [by_lanes(y, -1) for y in x]
        west = [by_lanes(y, 1) for y in x]
        for i in range(6):
            h, c = divmod(i, 3)
            base = 3 * h
            other = 3 * (1 - h) + c
            n = jnp.where(row < 7, up[i], up[base + (c + 1) % 3])
            p = jnp.where(row > 0, down[i], down[base + (c + 2) % 3])
            e = jnp.where(lane < 127, east[i], east[other])
            w = jnp.where(lane > 0, west[i], west[other])
            out.append((n + p) + (e + w))
        return out

    sigma = SPECTRUM_MID / SPECTRUM_HALF
    ratio = 1.0 / sigma
    scaled = [x * y for x, y in zip(rhs, inverse, strict=True)]
    previous = elev
    iterate = elev[1]
    for step in range(ITERS):
        around = neighbours([jnp.where(a, x, 0.0) for a, x in zip(wet, previous, strict=True)])
        scaled = [
            (res - x) + c * n
            for res, x, c, n in zip(scaled, previous, coupled, around, strict=True)
        ]
        if step == 0:
            previous = [res / SPECTRUM_MID for res in scaled]
        else:
            following = 1.0 / (2.0 * sigma - ratio)
            keep, gain = following * ratio, 2.0 * following / SPECTRUM_HALF
            previous = [keep * x + gain * res for x, res in zip(previous, scaled, strict=True)]
            ratio = following
        iterate = iterate + previous[1]
    height[...] = iterate


def shaped(*shape):
    return jax.ShapeDtypeStruct(shape, F32)


def call(kernel, outs, ins, flops, moved, **kw):
    return pl.pallas_call(
        kernel,
        out_shape=outs,
        in_specs=ins,
        compiler_params=pltpu.CompilerParams(vmem_limit_bytes=VMEM),
        cost_estimate=pl.CostEstimate(flops=flops, bytes_accessed=moved, transcendentals=0),
        **kw,
    )


WHOLE = pl.BlockSpec(memory_space=pltpu.VMEM)
HERE = pl.BlockSpec(memory_space=pltpu.HBM)
BLOCK = 4 * LEVELS * ROWS * LANES * 4


def call_pack_lon(*args):
    return call(
        pack_lon,
        (shaped(4, LEVELS + 4, ROWS, LANES), shaped(LON_ROWS, LANES), shaped(LON_ROWS, LANES)),
        [HERE] * 8 + [WHOLE], 10**6, 2 * BLOCK,
        out_specs=(WHOLE,) * 3,
        scratch_shapes=[
            pltpu.VMEM((4, LEVELS, ROWS, LANES), F32),
            pltpu.VMEM((2, ROWS, LANES), jnp.int32),
            pltpu.VMEM((2, ROWS, LANES), F32),
            pltpu.SemaphoreType.DMA((8,)),
        ],
    )(*args)


def call_pack_lat(*args):
    return call(
        pack_lat, (shaped(LAT_ROWS, LANES), shaped(LAT_ROWS, LANES), shaped(ROWS, LANES)),
        [WHOLE] * 2 + [WHOLE], 4 * 10**6, BLOCK,
    )(*args)


def call_forcing(*args):
    return call(
        forcing, (shaped(SOLVE_ROWS, LANES),) * 2, [WHOLE] + [WHOLE] * 9, 10**6, 10**6
    )(*args)


def call_fields(*args):
    return call(
        fields, (shaped(LEVELS, ROWS, LANES),) * 4, [WHOLE] + [WHOLE] * 8, 10**7, 3 * BLOCK,
        out_specs=(HERE,) * 4,
        scratch_shapes=[
            pltpu.VMEM((4, LEVELS * ROWS, 2 * LANES), F32),
            pltpu.VMEM((4, LEVELS + 2, ROWS, LANES), F32),
            pltpu.VMEM((4, LEVELS, ROWS, LANES), F32),
            pltpu.SemaphoreType.DMA((16,)),
        ],
    )(*args)


def call_solve(*args):
    return call(solve, shaped(ROWS, LANES), [WHOLE] + [WHOLE] * 8, 10**6, 10**6)(*args)


def on_device(u, v, t, s, water, layers, diag, elev):
    lon, lat = lax.axis_size("lon"), lax.axis_size("lat")
    lon_even = [(i, i ^ 1) for i in range(lon)]
    lon_odd = [(i, (((i + 1) ^ 1) - 1) % lon) for i in range(lon)]
    lat_even = [(i, i ^ 1) for i in range(lat)]
    lat_odd = [(i, ((i + 1) ^ 1) - 1) for i in range(1, lat - 1)]
    odd = jnp.stack([lax.axis_index("lon") & 1, lax.axis_index("lat") & 1]).astype(jnp.int32)
    parity = jnp.broadcast_to(odd[:, None, None], (2, ROWS, LANES))

    raw = [
        pltpu.with_memory_space_constraint(x, pltpu.HBM)
        for x in (u, v, t, s, water, layers, diag, elev)
    ]
    masked, own_odd, own_even = call_pack_lon(*raw, parity)
    got_even = lax.ppermute(own_even, "lon", lon_even)
    got_odd = lax.ppermute(own_odd, "lon", lon_odd)
    lat_own_odd, lat_own_even, partial = call_pack_lat(masked, own_odd, parity)
    lat_got_odd = lax.ppermute(lat_own_odd, "lat", lat_odd)
    lat_got_even = lax.ppermute(lat_own_even, "lat", lat_even)

    b_odd, b_even = call_forcing(
        parity, got_even, got_odd, own_odd, own_even,
        lat_own_odd, lat_own_even, lat_got_odd, lat_got_even, partial,
    )
    b_got_odd = lax.ppermute(b_odd, "lon", lon_odd)
    b_got_even = lax.ppermute(b_even, "lon", lon_even)

    fresh = call_fields(
        parity, masked, own_odd, lat_own_odd, lat_own_even, got_odd, got_even, lat_got_odd, lat_got_even
    )
    height = call_solve(
        parity, b_got_odd, b_got_even, b_odd, own_odd, got_odd, got_even, lat_got_odd, lat_got_even
    )
    return (*fresh, height)


def solution(mesh):
    field, flat = P(None, "lon", "lat"), P("lon", "lat")
    return jax.shard_map(
        on_device,
        mesh=mesh,
        in_specs=(field,) * 4 + (flat,) * 4,
        out_specs=(field,) * 4 + (flat,),
        check_vma=False,
    )
```

```python
import jax
import jax.numpy as jnp
from jax import lax
from jax.experimental import pallas as pl
from jax.experimental.pallas import tpu as pltpu
from jax.sharding import PartitionSpec as P

ITERS = 8
LEVELS = 62
SPECTRUM_MID = 1.0
SPECTRUM_HALF = 0.995

ROWS = 8
LANES = 128
STRIP = 128
FLAT = 4 * STRIP
LON_ROWS = FLAT + 3 * ROWS
LAT_ROWS = 18 * ROWS
SOLVE_ROWS = 3 * ROWS + 5 * ROWS
VMEM = 12 * 1024 * 1024

F32 = jnp.float32
ADV = 0.1 / 12.0


def rows_of(shape=(ROWS, LANES)):
    return lax.broadcasted_iota(jnp.int32, shape, 0)


def lanes_of(shape=(ROWS, LANES)):
    return lax.broadcasted_iota(jnp.int32, shape, 1)


def by_rows(x, d):
    d %= ROWS
    return pltpu.roll(x, d, 0) if d else x


def by_lanes(x, d):
    d %= LANES
    return pltpu.roll(x, d, 1) if d else x


def scalar_mix(t, s):
    return 0.7 * t - 0.5 * s


def is_even_over(axis):
    return lax.axis_index(axis) & 1 == 0


def flat_of(ref, base=FLAT):
    return [ref[base + 8 * i : base + 8 * i + 8, :] for i in range(3)]


def pack_lon(
    u, v, t, s, water, layers, diag, elev, masked, up_first, low_first, held, held_int, held_flat, sems
):
    copies = [
        pltpu.make_async_copy(src, held.at[i], sems.at[i]) for i, src in enumerate((u, v, t, s))
    ]
    small = [
        pltpu.make_async_copy(water, held_int.at[0], sems.at[4]),
        pltpu.make_async_copy(layers, held_int.at[1], sems.at[5]),
        pltpu.make_async_copy(elev, held_flat.at[0], sems.at[6]),
        pltpu.make_async_copy(diag, held_flat.at[1], sems.at[7]),
    ]
    for copy in small[:2] + copies + small[2:]:
        copy.start()
    for copy in small[:2]:
        copy.wait()
    row = rows_of()
    group = row >> 1
    depth = held_int[0] * held_int[1]
    is_even = is_even_over("lon")

    for f in range(4):
        masked[f, 0] = jnp.zeros((ROWS, LANES), F32)
        masked[f, LEVELS + 3] = jnp.zeros((ROWS, LANES), F32)
        copies[f].wait()

        def body(g, carry, f=f):
            top = bottom = None
            for i in range(4):
                k = 4 * g + i
                m = jnp.where(k < depth, held[f, jnp.minimum(k, LEVELS - 1)], 0.0)
                masked[f, k + 1] = m
                a, b = by_rows(m, 2 * i), by_rows(m, 2 * i - 6)
                top = a if i == 0 else jnp.where(group == i, a, top)
                bottom = b if i == 0 else jnp.where(group == i, b, bottom)
            at = pl.ds(pl.multiple_of(f * STRIP + 8 * g, 8), 8)
            up_first[at, :] = jnp.where(is_even, top, bottom)
            low_first[at, :] = jnp.where(is_even, bottom, top)
            return carry

        lax.fori_loop(0, 16, body, 0, unroll=True)

    for copy in small[2:]:
        copy.wait()
    for ref in (up_first, low_first):
        ref[FLAT : FLAT + 8, :] = held_flat[0]
        ref[FLAT + 8 : FLAT + 16, :] = held_flat[1]
        ref[FLAT + 16 : FLAT + 24, :] = depth.astype(F32)


BF16 = jnp.bfloat16


def lat_matrix():
    shape = (2 * LANES, 2 * LANES)
    source = rows_of(shape) & 127
    target = lanes_of(shape)
    d = source - (target & 127)
    slope = jnp.where(d == 1, 8.0, jnp.where(d == -1, -8.0, 0.0))
    slope = slope + jnp.where(d == 2, -1.0, jnp.where(d == -2, 1.0, 0.0))
    near = jnp.where(jnp.abs(d) == 1, 1.0, 0.0)
    return jnp.where(target < LANES, slope, near).astype(BF16)


def lat_terms(x, matrix):
    high = x.astype(BF16)
    rest = (x - high.astype(F32)).astype(BF16)
    return jnp.dot(jnp.concatenate([high, rest], axis=1), matrix, preferred_element_type=F32)


def pack_lat(masked, own_lon, odd_out, even_out, partial):
    row, lane = rows_of(), lanes_of()
    high, low = lane >> 4, ((lane - 8) & 127) >> 4
    in_even = (lane & 8) == 0
    elev, diag, depth = flat_of(own_lon)
    levels = depth.astype(jnp.int32)
    is_even = is_even_over("lat")
    zero = jnp.zeros((ROWS, LANES), F32)
    matrix = lat_matrix()
    left, right = tile_lanes(depth), tile_lanes(by_lanes(depth, 8))
    odd_out[136:144, :] = jnp.where(is_even, left, right)
    even_out[136:144, :] = jnp.where(is_even, right, left)

    def tile(a, sums):
        whole, inner, sides, flux = sums
        first, second = [zero] * 4, [zero] * 4
        tracer = [
            scalar_mix(masked[2, 16 * a + i + 1], masked[3, 16 * a + i + 1]) for i in range(16)
        ]
        terms = lat_terms(jnp.concatenate(tracer, axis=0), matrix)
        for i in range(16):
            k = 16 * a + i
            m = [masked[f, k + 1] for f in range(4)]
            for f in range(4):
                if i < 8:
                    first[f] = jnp.where(high == i, by_lanes(m[f], 16 * i - 120), first[f])
                else:
                    second[f] = jnp.where(low == i - 8, by_lanes(m[f], 16 * i - 240), second[f])
            w = tracer[i]
            n1 = jnp.where(row < 7, by_rows(w, -1), 0.0)
            p1 = jnp.where(row > 0, by_rows(w, 1), 0.0)
            n2 = jnp.where(row < 6, by_rows(w, -2), 0.0)
            p2 = jnp.where(row > 1, by_rows(w, 2), 0.0)
            gx = 8.0 * (n1 - p1) - (n2 - p2)
            gy = terms[8 * i : 8 * i + 8, :LANES]
            around = (n1 + p1) + terms[8 * i : 8 * i + 8, LANES:]
            whole = whole + w
            inner = inner + jnp.where(k + 1 < levels, w, 0.0)
            sides = sides + jnp.where(k < levels, around, 0.0)
            flux = flux + (m[0] * gx + m[1] * gy)
        for f in range(4):
            right = jnp.where(in_even, first[f], second[f])
            left = by_lanes(jnp.where(in_even, second[f], first[f]), -8)
            where = pl.ds(pl.multiple_of(f * 32 + 8 * a, 8), 8)
            odd_out[where, :] = jnp.where(is_even, left, right)
            even_out[where, :] = jnp.where(is_even, right, left)
        return whole, inner, sides, flux

    whole, inner, sides, flux = lax.fori_loop(0, 4, tile, (zero,) * 4, unroll=True)
    top = scalar_mix(masked[2, 1], masked[3, 1])
    acc = 0.1 * (0.94 * whole + 0.02 * (whole - top + inner) + 0.005 * sides - ADV * flux)
    partial[...] = acc
    slot = lane >> 3
    left = right = zero
    for i, x in enumerate((acc, elev, diag, depth)):
        left = jnp.where(slot == i, by_lanes(x, 8 * i), left)
        right = jnp.where(slot == i, by_lanes(x, 8 * i - 120), right)
    odd_out[128:136, :] = jnp.where(is_even, left, right)
    even_out[128:136, :] = jnp.where(is_even, right, left)


def tile_lanes(x):
    return sum_slots(jnp.where(lanes_of() < 8, x, 0.0))


def sum_slots(x):
    for d in (8, 32):
        x = (x + by_lanes(x, d)) + (by_lanes(x, 2 * d) + by_lanes(x, 3 * d))
    return x


def wet_pack(depth, a):
    slot = lanes_of() >> 3
    return (16 * a + (slot >> 1) + 8 * (slot & 1)).astype(F32) < depth


def west_part(vel, depth, east, i):
    column = lanes_of() & 7
    y1 = jnp.where(column == 7, by_lanes(east, 7), 0.0)
    y2 = jnp.where(column >= 6, by_lanes(east, 6), 0.0)
    return 0.005 * jnp.where(wet_pack(depth, i), y1, 0.0) - ADV * vel * (8.0 * y1 - y2)


def east_part(vel, depth, west, i):
    column = lanes_of() & 7
    z1 = jnp.where(column == 0, by_lanes(west, -7), 0.0)
    z2 = jnp.where(column <= 1, by_lanes(west, -6), 0.0)
    return 0.005 * jnp.where(wet_pack(depth, i), z1, 0.0) - ADV * vel * (z2 - 8.0 * z1)


def lat_rims(a_v, a_w, a_depth, b_v, b_w, b_depth):
    a_sum = b_sum = jnp.zeros((ROWS, LANES), F32)
    for i in range(4):
        a_sum = a_sum + west_part(a_v[i], a_depth, b_w[i], i)
        b_sum = b_sum + east_part(b_v[i], b_depth, a_w[i], i)
    return 0.1 * sum_slots(a_sum), 0.1 * sum_slots(b_sum)


def four(ref, base, flag, other):
    at = [slice(base + 8 * i, base + 8 * i + 8) for i in range(4)]
    return [jnp.where(flag, ref[x, :], other[x, :]) for x in at]


def forcing(
    got_even, got_odd, own_odd, own_even,
    own_odd_lat, own_even_lat, got_odd_lat, got_even_lat, partial,
    odd_out, even_out,
):
    row, lane = rows_of(), lanes_of()
    lon_even, lat_even = is_even_over("lon"), is_even_over("lat")
    elev, diag, depth = flat_of(own_odd)
    total = elev + partial[...]

    r = row & 1
    for lower in (True, False):
        rim = row < 2 if lower else row >= 6
        tiled = jnp.where(rim, depth, 0.0)
        tiled = tiled + by_rows(tiled, 2)
        tiled = tiled + by_rows(tiled, 4)
        acc = jnp.zeros((ROWS, LANES), F32)
        own_first = lon_even if lower else jnp.logical_not(lon_even)
        for g in range(16):
            at = slice(8 * g, 8 * g + 8)
            at_t = slice(2 * STRIP + 8 * g, 2 * STRIP + 8 * g + 8)
            at_s = slice(3 * STRIP + 8 * g, 3 * STRIP + 8 * g + 8)
            vel = jnp.where(own_first, own_odd[at, :], own_even[at, :])
            w = scalar_mix(
                jnp.where(own_first, got_odd[at_t, :], got_even[at_t, :]),
                jnp.where(own_first, got_odd[at_s, :], got_even[at_s, :]),
            )
            wet = (4 * g + (row >> 1)).astype(F32) < tiled
            if lower:
                near = jnp.where(r == 0, by_rows(w, -1), 0.0)
                slope = w - 8.0 * near
            else:
                near = jnp.where(r == 1, by_rows(w, 1), 0.0)
                slope = 8.0 * near - w
            acc = acc + (0.005 * jnp.where(wet, near, 0.0) - ADV * vel * slope)
        acc = acc + by_rows(acc, 2)
        acc = acc + by_rows(acc, 4)
        total = total + jnp.where(rim, 0.1 * acc, 0.0)

    own_r = [four(own_even_lat, f * 32, lat_even, own_odd_lat) for f in range(1, 4)]
    own_l = [four(own_odd_lat, f * 32, lat_even, own_even_lat) for f in range(1, 4)]
    ext_r = [four(got_even_lat, f * 32, lat_even, got_odd_lat) for f in range(4)]
    ext_l = [four(got_odd_lat, f * 32, lat_even, got_even_lat) for f in range(4)]
    flat_r = jnp.where(lat_even, got_even_lat[128:136, :], got_odd_lat[128:136, :])
    flat_l = jnp.where(lat_even, got_odd_lat[128:136, :], got_even_lat[128:136, :])
    depth_r = jnp.where(lat_even, got_even_lat[136:144, :], got_odd_lat[136:144, :])
    depth_l = jnp.where(lat_even, got_odd_lat[136:144, :], got_even_lat[136:144, :])
    own_depth_r = jnp.where(lat_even, own_even_lat[136:144, :], own_odd_lat[136:144, :])
    own_depth_l = jnp.where(lat_even, own_odd_lat[136:144, :], own_even_lat[136:144, :])

    def mixed(pair):
        return [scalar_mix(x, y) for x, y in zip(*pair, strict=True)]

    w_r, w_l = mixed(ext_r[2:]), mixed(ext_l[2:])
    miss_own_r, miss_ext_r = lat_rims(
        own_r[0], mixed(own_r[1:]), own_depth_r, ext_r[1], w_r, depth_r
    )
    miss_ext_l, miss_own_l = lat_rims(
        ext_l[1], w_l, depth_l, own_l[0], mixed(own_l[1:]), own_depth_l
    )
    total = total + jnp.where(lane >= 126, miss_own_r, 0.0) + jnp.where(lane < 2, miss_own_l, 0.0)

    def side(i):
        return jnp.where(
            lane < 8,
            by_lanes(flat_r, -8 * i),
            jnp.where(lane >= 120, by_lanes(flat_l, 120 - 8 * i), 0.0),
        )

    elev_side = side(1)
    total_side = side(0) + elev_side
    total_side = total_side + jnp.where(lane < 2, miss_ext_r, 0.0)
    total_side = total_side + jnp.where(lane >= 126, miss_ext_l, 0.0)
    slot = lane >> 3
    sides = jnp.zeros((ROWS, LANES), F32)
    for i in range(3):
        sides = jnp.where(slot == 2 * i, by_lanes(flat_r, 8 * i - 8), sides)
        sides = jnp.where(slot == (2 * i - 1) % 16, by_lanes(flat_l, 8 * i + 112), sides)
    for ref in (odd_out, even_out):
        for i, x in enumerate((total, total_side, sides)):
            ref[8 * i : 8 * i + 8, :] = x
    packs = ext_r[0] + ext_l[0] + w_r + w_l + [depth_r, depth_l]
    group = row >> 1
    for i in range(5):
        top = bottom = jnp.zeros((ROWS, LANES), F32)
        for j, x in enumerate(packs[4 * i : 4 * i + 4]):
            top = jnp.where(group == j, by_rows(x, 2 * j), top)
            bottom = jnp.where(group == j, by_rows(x, 2 * j - 6), bottom)
        at = slice(24 + 8 * i, 32 + 8 * i)
        odd_out[at, :] = jnp.where(lon_even, top, bottom)
        even_out[at, :] = jnp.where(lon_even, bottom, top)


CHUNKS = ((0, 5), (5, 10), (10, 15))


def fields(
    masked, own_lon, own_odd_lat, own_even_lat, odd_lon, even_lon, odd_lat, even_lat,
    o1, o2, o3, o4, terms, rims, fresh, sems,
):
    row, lane = rows_of(), lanes_of()
    levels = flat_of(own_lon)[2].astype(jnp.int32)
    lon_even, lat_even = is_even_over("lon"), is_even_over("lat")
    outs = (o1, o2, o3, o4)
    at_edge = (lane < 2) | (lane >= 126)

    matrix = lat_matrix()
    for f in range(4):
        for first in range(0, LEVELS, 16):
            count = min(16, LEVELS - first)
            x = masked[f, first + 1 : first + 1 + count].reshape(count * ROWS, LANES)
            terms[f, ROWS * first : ROWS * (first + count), :] = lat_terms(x, matrix)

    in_even = (lane & 8) == 0

    def west_east(odd, even, base):
        x, y = odd[base : base + 8, :], even[base : base + 8, :]
        return jnp.where(lat_even, x, y), jnp.where(lat_even, y, x)

    depth_west, depth_east = west_east(own_odd_lat, own_even_lat, 136)
    for a in range(4):
        vel_west, vel_east = west_east(own_odd_lat, own_even_lat, 32 + 8 * a)
        for f in range(4):
            west, east = west_east(odd_lat, even_lat, f * 32 + 8 * a)
            right = west_part(vel_east, depth_east, east, a)
            left = by_lanes(east_part(vel_west, depth_west, west, a), 8)
            first = jnp.where(in_even, right, left)
            second = jnp.where(in_even, left, right)
            for i in range(8):
                rims[f, 16 * a + i] = by_lanes(first, -16 * i - 8)
                rims[f, 16 * a + 8 + i] = by_lanes(second, -16 * i - 16)

    def group(g, count):
        strips = []
        for f in range(4):
            at = pl.ds(pl.multiple_of(f * STRIP + 8 * g, 8), 8)
            x, y = odd_lon[at, :], even_lon[at, :]
            strips.append((jnp.where(lon_even, y, x), jnp.where(lon_even, x, y)))
        for j in range(count):
            k = 4 * g + j
            wet = k < levels
            center = [masked[f, k + 1] for f in range(4)]
            zonal, merid = ADV * center[0], ADV * center[1]
            at = pl.ds(pl.multiple_of(ROWS * k, ROWS), ROWS)
            for f in range(4):
                m = center[f]
                upper, lower = strips[f]
                rim = jnp.where(row < 4, by_rows(upper, -2 * j), by_rows(lower, 6 - 2 * j))
                n1 = by_rows(jnp.where(row < 1, rim, m), -1)
                n2 = by_rows(jnp.where(row < 2, rim, m), -2)
                p1 = by_rows(jnp.where(row > 6, rim, m), 1)
                p2 = by_rows(jnp.where(row > 5, rim, m), 2)
                gx = 8.0 * (n1 - p1) - (n2 - p2)
                gy = terms[f, at, :LANES]
                around = (n1 + p1) + terms[f, at, LANES:]
                column = masked[f, k] + masked[f, k + 2]
                value = 0.94 * m + 0.02 * column + 0.005 * around - (zonal * gx + merid * gy)
                fresh[f, k] = jnp.where(wet, value, 0.0) + jnp.where(at_edge, rims[f, k], 0.0)

    def body(g, carry):
        group(g, 4)
        return carry

    copies = []

    def send(first, last):
        for f in range(4):
            copies.append(
                pltpu.make_async_copy(
                    fresh.at[f, first:last], outs[f].at[first:last], sems.at[len(copies)]
                )
            )
            copies[-1].start()

    for first, last in CHUNKS:
        lax.fori_loop(first, last, body, 0, unroll=True)
        send(4 * first, 4 * last)
    group(15, LEVELS - 60)
    send(60, LEVELS)
    for copy in copies:
        copy.wait()


def solve(
    odd_b, even_b, own_b, own_lon, odd_lon, even_lon, odd_lat, even_lat, height
):
    row, lane = rows_of(), lanes_of()
    lon_even, lat_even = is_even_over("lon"), is_even_over("lat")
    lower = [jnp.where(lon_even, odd_b[8 * i : 8 * i + 8, :], even_b[8 * i : 8 * i + 8, :]) for i in range(8)]
    upper = [jnp.where(lon_even, even_b[8 * i : 8 * i + 8, :], odd_b[8 * i : 8 * i + 8, :]) for i in range(8)]
    own = [own_b[8 * i : 8 * i + 8, :] for i in range(3)]

    ext_r = [four(even_lat, f * 32, lat_even, odd_lat) for f in (0, 2, 3)]
    ext_l = [four(odd_lat, f * 32, lat_even, even_lat) for f in (0, 2, 3)]

    def lon_part(vel, wet, x1, x2):
        slope = jnp.where(row == 0, -8.0 * x1, jnp.where(row == 7, 8.0 * x1, 0.0))
        slope = slope + jnp.where(row < 2, x2, jnp.where(row >= 6, -x2, 0.0))
        near = jnp.where((row == 0) | (row == 7), x1, 0.0)
        return 0.005 * jnp.where(wet, near, 0.0) - ADV * vel * slope

    def rim_rows(tile, q, first):
        return by_rows(tile[3 + q // 4], first - 2 * (q % 4))

    def near_rows(q):
        return jnp.where(row < 4, rim_rows(upper, q, 0), rim_rows(lower, q, 6))

    def side_parts(ext, base, own_depth, near_depth):
        mine = theirs = jnp.zeros((ROWS, LANES), F32)
        for i in range(4):
            vel, w = ext[0][i], scalar_mix(ext[1][i], ext[2][i])
            qu, qw = base + i, 8 + base + i
            x2 = jnp.where(row < 4, rim_rows(lower, qw, 0), rim_rows(upper, qw, 6))
            x1 = jnp.where(row < 4, rim_rows(lower, qw, -1), rim_rows(upper, qw, 7))
            mine = mine + lon_part(vel, wet_pack(own_depth, i), x1, x2)
            y2 = jnp.where(row < 4, by_rows(w, 2), by_rows(w, -2))
            y1 = jnp.where(row < 4, by_rows(w, 1), by_rows(w, -1))
            theirs = theirs + lon_part(near_rows(qu), wet_pack(near_depth, i), y1, y2)
        return 0.1 * sum_slots(mine), 0.1 * sum_slots(theirs)

    depth_r = jnp.where(lat_even, even_lat[136:144, :], odd_lat[136:144, :])
    depth_l = jnp.where(lat_even, odd_lat[136:144, :], even_lat[136:144, :])
    mine_r, theirs_r = side_parts(ext_r, 0, depth_r, near_rows(16))
    mine_l, theirs_l = side_parts(ext_l, 4, depth_l, near_rows(17))
    in_r, in_l = lane < 8, lane >= 120
    mine = jnp.where(in_r, mine_r, jnp.where(in_l, mine_l, 0.0))
    theirs = jnp.where(in_r, theirs_r, jnp.where(in_l, theirs_l, 0.0))

    flat_own = flat_of(own_lon)
    flat_odd, flat_even = flat_of(odd_lon), flat_of(even_lon)
    flat_low = [jnp.where(lon_even, x, y) for x, y in zip(flat_odd, flat_even, strict=True)]
    flat_up = [jnp.where(lon_even, y, x) for x, y in zip(flat_odd, flat_even, strict=True)]

    rhs = [
        lower[0], own[0], upper[0],
        lower[1] + jnp.where(row >= 6, theirs, 0.0),
        own[1] + mine,
        upper[1] + jnp.where(row < 2, theirs, 0.0),
    ]
    sides = [
        [jnp.where(in_r | in_l, by_lanes(x[2], -16 * i), 0.0) for x in (lower, own, upper)]
        for i in range(3)
    ]
    elev = [flat_low[0], flat_own[0], flat_up[0]] + sides[0]
    diag = [flat_low[1], flat_own[1], flat_up[1]] + sides[1]
    wet = [x > 0.0 for x in [flat_low[2], flat_own[2], flat_up[2]] + sides[2]]
    diag = [x + 4.0 for x in diag]
    inverse = [1.0 / x for x in diag]
    coupled = [jnp.where(a, x, 0.0) for a, x in zip(wet, inverse, strict=True)]

    def neighbours(x):
        out = []
        up = [by_rows(y, -1) for y in x]
        down = [by_rows(y, 1) for y in x]
        east = [by_lanes(y, -1) for y in x]
        west = [by_lanes(y, 1) for y in x]
        for i in range(6):
            h, c = divmod(i, 3)
            base = 3 * h
            other = 3 * (1 - h) + c
            n = jnp.where(row < 7, up[i], up[base + (c + 1) % 3])
            p = jnp.where(row > 0, down[i], down[base + (c + 2) % 3])
            e = jnp.where(lane < 127, east[i], east[other])
            w = jnp.where(lane > 0, west[i], west[other])
            out.append((n + p) + (e + w))
        return out

    sigma = SPECTRUM_MID / SPECTRUM_HALF
    ratio = 1.0 / sigma
    scaled = [x * y for x, y in zip(rhs, inverse, strict=True)]
    previous = elev
    iterate = elev[1]
    for step in range(ITERS):
        around = neighbours([jnp.where(a, x, 0.0) for a, x in zip(wet, previous, strict=True)])
        scaled = [
            (res - x) + c * n
            for res, x, c, n in zip(scaled, previous, coupled, around, strict=True)
        ]
        if step == 0:
            previous = [res / SPECTRUM_MID for res in scaled]
        else:
            following = 1.0 / (2.0 * sigma - ratio)
            keep, gain = following * ratio, 2.0 * following / SPECTRUM_HALF
            previous = [keep * x + gain * res for x, res in zip(previous, scaled, strict=True)]
            ratio = following
        iterate = iterate + previous[1]
    height[...] = iterate


def shaped(*shape):
    return jax.ShapeDtypeStruct(shape, F32)


def call(kernel, outs, ins, flops, moved, **kw):
    return pl.pallas_call(
        kernel,
        out_shape=outs,
        in_specs=ins,
        compiler_params=pltpu.CompilerParams(vmem_limit_bytes=VMEM),
        cost_estimate=pl.CostEstimate(flops=flops, bytes_accessed=moved, transcendentals=0),
        **kw,
    )


WHOLE = pl.BlockSpec(memory_space=pltpu.VMEM)
HERE = pl.BlockSpec(memory_space=pltpu.HBM)
BLOCK = 4 * LEVELS * ROWS * LANES * 4


def call_pack_lon(*args):
    return call(
        pack_lon,
        (shaped(4, LEVELS + 4, ROWS, LANES), shaped(LON_ROWS, LANES), shaped(LON_ROWS, LANES)),
        [HERE] * 8, 10**6, 2 * BLOCK,
        out_specs=(WHOLE,) * 3,
        scratch_shapes=[
            pltpu.VMEM((4, LEVELS, ROWS, LANES), F32),
            pltpu.VMEM((2, ROWS, LANES), jnp.int32),
            pltpu.VMEM((2, ROWS, LANES), F32),
            pltpu.SemaphoreType.DMA((8,)),
        ],
    )(*args)


def call_pack_lat(*args):
    return call(
        pack_lat, (shaped(LAT_ROWS, LANES), shaped(LAT_ROWS, LANES), shaped(ROWS, LANES)),
        [WHOLE] * 2, 4 * 10**6, BLOCK,
    )(*args)


def call_forcing(*args):
    return call(
        forcing, (shaped(SOLVE_ROWS, LANES),) * 2, [WHOLE] * 9, 10**6, 10**6
    )(*args)


def call_fields(*args):
    return call(
        fields, (shaped(LEVELS, ROWS, LANES),) * 4, [WHOLE] * 8, 10**7, 3 * BLOCK,
        out_specs=(HERE,) * 4,
        scratch_shapes=[
            pltpu.VMEM((4, LEVELS * ROWS, 2 * LANES), F32),
            pltpu.VMEM((4, LEVELS + 2, ROWS, LANES), F32),
            pltpu.VMEM((4, LEVELS, ROWS, LANES), F32),
            pltpu.SemaphoreType.DMA((16,)),
        ],
    )(*args)


def call_solve(*args):
    return call(solve, shaped(ROWS, LANES), [WHOLE] * 8, 10**6, 10**6)(*args)


def on_device(u, v, t, s, water, layers, diag, elev):
    lon, lat = lax.axis_size("lon"), lax.axis_size("lat")
    lon_even = [(i, i ^ 1) for i in range(lon)]
    lon_odd = [(i, (((i + 1) ^ 1) - 1) % lon) for i in range(lon)]
    lat_even = [(i, i ^ 1) for i in range(lat)]
    lat_odd = [(i, ((i + 1) ^ 1) - 1) for i in range(1, lat - 1)]

    raw = [
        pltpu.with_memory_space_constraint(x, pltpu.HBM)
        for x in (u, v, t, s, water, layers, diag, elev)
    ]
    masked, own_odd, own_even = call_pack_lon(*raw)
    got_even = lax.ppermute(own_even, "lon", lon_even)
    got_odd = lax.ppermute(own_odd, "lon", lon_odd)
    lat_own_odd, lat_own_even, partial = call_pack_lat(masked, own_odd)
    lat_got_odd = lax.ppermute(lat_own_odd, "lat", lat_odd)
    lat_got_even = lax.ppermute(lat_own_even, "lat", lat_even)

    b_odd, b_even = call_forcing(
        got_even, got_odd, own_odd, own_even,
        lat_own_odd, lat_own_even, lat_got_odd, lat_got_even, partial,
    )
    b_got_odd = lax.ppermute(b_odd, "lon", lon_odd)
    b_got_even = lax.ppermute(b_even, "lon", lon_even)

    fresh = call_fields(
        masked, own_odd, lat_own_odd, lat_own_even, got_odd, got_even, lat_got_odd, lat_got_even
    )
    height = call_solve(
        b_got_odd, b_got_even, b_odd, own_odd, got_odd, got_even, lat_got_odd, lat_got_even
    )
    return (*fresh, height)


def solution(mesh):
    field, flat = P(None, "lon", "lat"), P("lon", "lat")
    return jax.shard_map(
        on_device,
        mesh=mesh,
        in_specs=(field,) * 4 + (flat,) * 4,
        out_specs=(field,) * 4 + (flat,),
        check_vma=False,
    )
```

```python
import jax
import jax.numpy as jnp
from jax import lax
from jax.experimental import pallas as pl
from jax.experimental.pallas import tpu as pltpu
from jax.sharding import PartitionSpec as P

ITERS = 8
LEVELS = 62
SPECTRUM_MID = 1.0
SPECTRUM_HALF = 0.995

ROWS = 8
LANES = 128
STRIP = 128
FLAT = 4 * STRIP
LON_ROWS = FLAT + 3 * ROWS
LAT_ROWS = 18 * ROWS
SOLVE_ROWS = 3 * ROWS + 5 * ROWS
VMEM = 12 * 1024 * 1024

F32 = jnp.float32
ADV = 0.1 / 12.0


def rows_of(shape=(ROWS, LANES)):
    return lax.broadcasted_iota(jnp.int32, shape, 0)


def lanes_of(shape=(ROWS, LANES)):
    return lax.broadcasted_iota(jnp.int32, shape, 1)


def by_rows(x, d):
    d %= ROWS
    return pltpu.roll(x, d, 0) if d else x


def by_lanes(x, d):
    d %= LANES
    return pltpu.roll(x, d, 1) if d else x


def scalar_mix(t, s):
    return 0.7 * t - 0.5 * s


def is_even_over(axis):
    return lax.axis_index(axis) & 1 == 0


def flat_of(ref, base=FLAT):
    return [ref[base + 8 * i : base + 8 * i + 8, :] for i in range(3)]


def pack_lon(
    u, v, t, s, water, layers, diag, elev, masked, up_first, low_first, held, held_int, held_flat, sems
):
    copies = [
        pltpu.make_async_copy(src, held.at[i], sems.at[i]) for i, src in enumerate((u, v, t, s))
    ]
    small = [
        pltpu.make_async_copy(water, held_int.at[0], sems.at[4]),
        pltpu.make_async_copy(layers, held_int.at[1], sems.at[5]),
        pltpu.make_async_copy(elev, held_flat.at[0], sems.at[6]),
        pltpu.make_async_copy(diag, held_flat.at[1], sems.at[7]),
    ]
    for copy in small[:2] + copies + small[2:]:
        copy.start()
    for copy in small[:2]:
        copy.wait()
    row = rows_of()
    group = row >> 1
    depth = held_int[0] * held_int[1]
    is_even = is_even_over("lon")

    for f in range(4):
        masked[f, 0] = jnp.zeros((ROWS, LANES), F32)
        masked[f, LEVELS + 3] = jnp.zeros((ROWS, LANES), F32)
        copies[f].wait()

        def body(g, carry, f=f):
            top = bottom = None
            for i in range(4):
                k = 4 * g + i
                m = jnp.where(k < depth, held[f, jnp.minimum(k, LEVELS - 1)], 0.0)
                masked[f, k + 1] = m
                a, b = by_rows(m, 2 * i), by_rows(m, 2 * i - 6)
                top = a if i == 0 else jnp.where(group == i, a, top)
                bottom = b if i == 0 else jnp.where(group == i, b, bottom)
            at = pl.ds(pl.multiple_of(f * STRIP + 8 * g, 8), 8)
            up_first[at, :] = jnp.where(is_even, top, bottom)
            low_first[at, :] = jnp.where(is_even, bottom, top)
            return carry

        lax.fori_loop(0, 16, body, 0, unroll=True)

    for copy in small[2:]:
        copy.wait()
    for ref in (up_first, low_first):
        ref[FLAT : FLAT + 8, :] = held_flat[0]
        ref[FLAT + 8 : FLAT + 16, :] = held_flat[1]
        ref[FLAT + 16 : FLAT + 24, :] = depth.astype(F32)


BF16 = jnp.bfloat16


def lat_matrix():
    shape = (2 * LANES, 2 * LANES)
    source = rows_of(shape) & 127
    target = lanes_of(shape)
    d = source - (target & 127)
    slope = jnp.where(d == 1, 8.0, jnp.where(d == -1, -8.0, 0.0))
    slope = slope + jnp.where(d == 2, -1.0, jnp.where(d == -2, 1.0, 0.0))
    near = jnp.where(jnp.abs(d) == 1, 1.0, 0.0)
    return jnp.where(target < LANES, slope, near).astype(BF16)


def lat_terms(x, matrix):
    high = x.astype(BF16)
    rest = (x - high.astype(F32)).astype(BF16)
    return jnp.dot(jnp.concatenate([high, rest], axis=1), matrix, preferred_element_type=F32)


def pack_lat(masked, own_lon, odd_out, even_out, partial):
    row, lane = rows_of(), lanes_of()
    high, low = lane >> 4, ((lane - 8) & 127) >> 4
    in_even = (lane & 8) == 0
    elev, diag, depth = flat_of(own_lon)
    levels = depth.astype(jnp.int32)
    is_even = is_even_over("lat")
    zero = jnp.zeros((ROWS, LANES), F32)
    matrix = lat_matrix()
    left, right = tile_lanes(depth), tile_lanes(by_lanes(depth, 8))
    odd_out[136:144, :] = jnp.where(is_even, left, right)
    even_out[136:144, :] = jnp.where(is_even, right, left)

    def tile(a, sums):
        whole, inner, sides, flux = sums
        first, second = [zero] * 4, [zero] * 4
        tracer = [
            scalar_mix(masked[2, 16 * a + i + 1], masked[3, 16 * a + i + 1]) for i in range(16)
        ]
        terms = lat_terms(jnp.concatenate(tracer, axis=0), matrix)
        for i in range(16):
            k = 16 * a + i
            m = [masked[f, k + 1] for f in range(4)]
            for f in range(4):
                if i < 8:
                    first[f] = jnp.where(high == i, by_lanes(m[f], 16 * i - 120), first[f])
                else:
                    second[f] = jnp.where(low == i - 8, by_lanes(m[f], 16 * i - 240), second[f])
            w = tracer[i]
            n1 = jnp.where(row < 7, by_rows(w, -1), 0.0)
            p1 = jnp.where(row > 0, by_rows(w, 1), 0.0)
            n2 = jnp.where(row < 6, by_rows(w, -2), 0.0)
            p2 = jnp.where(row > 1, by_rows(w, 2), 0.0)
            gx = 8.0 * (n1 - p1) - (n2 - p2)
            gy = terms[8 * i : 8 * i + 8, :LANES]
            around = (n1 + p1) + terms[8 * i : 8 * i + 8, LANES:]
            whole = whole + w
            inner = inner + jnp.where(k + 1 < levels, w, 0.0)
            sides = sides + jnp.where(k < levels, around, 0.0)
            flux = flux + (m[0] * gx + m[1] * gy)
        for f in range(4):
            right = jnp.where(in_even, first[f], second[f])
            left = by_lanes(jnp.where(in_even, second[f], first[f]), -8)
            where = pl.ds(pl.multiple_of(f * 32 + 8 * a, 8), 8)
            odd_out[where, :] = jnp.where(is_even, left, right)
            even_out[where, :] = jnp.where(is_even, right, left)
        return whole, inner, sides, flux

    whole, inner, sides, flux = lax.fori_loop(0, 4, tile, (zero,) * 4, unroll=True)
    top = scalar_mix(masked[2, 1], masked[3, 1])
    acc = 0.1 * (0.94 * whole + 0.02 * (whole - top + inner) + 0.005 * sides - ADV * flux)
    partial[...] = acc
    slot = lane >> 3
    left = right = zero
    for i, x in enumerate((acc, elev, diag, depth)):
        left = jnp.where(slot == i, by_lanes(x, 8 * i), left)
        right = jnp.where(slot == i, by_lanes(x, 8 * i - 120), right)
    odd_out[128:136, :] = jnp.where(is_even, left, right)
    even_out[128:136, :] = jnp.where(is_even, right, left)


def tile_lanes(x):
    return sum_slots(jnp.where(lanes_of() < 8, x, 0.0))


def sum_slots(x):
    for d in (8, 32):
        x = (x + by_lanes(x, d)) + (by_lanes(x, 2 * d) + by_lanes(x, 3 * d))
    return x


def wet_pack(depth, a):
    slot = lanes_of() >> 3
    return (16 * a + (slot >> 1) + 8 * (slot & 1)).astype(F32) < depth


def west_part(vel, depth, east, i):
    column = lanes_of() & 7
    y1 = jnp.where(column == 7, by_lanes(east, 7), 0.0)
    y2 = jnp.where(column >= 6, by_lanes(east, 6), 0.0)
    return 0.005 * jnp.where(wet_pack(depth, i), y1, 0.0) - ADV * vel * (8.0 * y1 - y2)


def east_part(vel, depth, west, i):
    column = lanes_of() & 7
    z1 = jnp.where(column == 0, by_lanes(west, -7), 0.0)
    z2 = jnp.where(column <= 1, by_lanes(west, -6), 0.0)
    return 0.005 * jnp.where(wet_pack(depth, i), z1, 0.0) - ADV * vel * (z2 - 8.0 * z1)


def lat_rims(a_v, a_w, a_depth, b_v, b_w, b_depth):
    a_sum = b_sum = jnp.zeros((ROWS, LANES), F32)
    for i in range(4):
        a_sum = a_sum + west_part(a_v[i], a_depth, b_w[i], i)
        b_sum = b_sum + east_part(b_v[i], b_depth, a_w[i], i)
    return 0.1 * sum_slots(a_sum), 0.1 * sum_slots(b_sum)


def four(ref, base, flag, other):
    at = [slice(base + 8 * i, base + 8 * i + 8) for i in range(4)]
    return [jnp.where(flag, ref[x, :], other[x, :]) for x in at]


def forcing(
    got_even, got_odd, own_odd, own_even,
    own_odd_lat, own_even_lat, got_odd_lat, got_even_lat, partial,
    odd_out, even_out,
):
    row, lane = rows_of(), lanes_of()
    lon_even, lat_even = is_even_over("lon"), is_even_over("lat")
    elev, diag, depth = flat_of(own_odd)
    total = elev + partial[...]

    r = row & 1
    for lower in (True, False):
        rim = row < 2 if lower else row >= 6
        tiled = jnp.where(rim, depth, 0.0)
        tiled = tiled + by_rows(tiled, 2)
        tiled = tiled + by_rows(tiled, 4)
        acc = jnp.zeros((ROWS, LANES), F32)
        own_first = lon_even if lower else jnp.logical_not(lon_even)
        for g in range(16):
            at = slice(8 * g, 8 * g + 8)
            at_t = slice(2 * STRIP + 8 * g, 2 * STRIP + 8 * g + 8)
            at_s = slice(3 * STRIP + 8 * g, 3 * STRIP + 8 * g + 8)
            vel = jnp.where(own_first, own_odd[at, :], own_even[at, :])
            w = scalar_mix(
                jnp.where(own_first, got_odd[at_t, :], got_even[at_t, :]),
                jnp.where(own_first, got_odd[at_s, :], got_even[at_s, :]),
            )
            wet = (4 * g + (row >> 1)).astype(F32) < tiled
            if lower:
                near = jnp.where(r == 0, by_rows(w, -1), 0.0)
                slope = w - 8.0 * near
            else:
                near = jnp.where(r == 1, by_rows(w, 1), 0.0)
                slope = 8.0 * near - w
            acc = acc + (0.005 * jnp.where(wet, near, 0.0) - ADV * vel * slope)
        acc = acc + by_rows(acc, 2)
        acc = acc + by_rows(acc, 4)
        total = total + jnp.where(rim, 0.1 * acc, 0.0)

    own_r = [four(own_even_lat, f * 32, lat_even, own_odd_lat) for f in range(1, 4)]
    own_l = [four(own_odd_lat, f * 32, lat_even, own_even_lat) for f in range(1, 4)]
    ext_r = [four(got_even_lat, f * 32, lat_even, got_odd_lat) for f in range(4)]
    ext_l = [four(got_odd_lat, f * 32, lat_even, got_even_lat) for f in range(4)]
    flat_r = jnp.where(lat_even, got_even_lat[128:136, :], got_odd_lat[128:136, :])
    flat_l = jnp.where(lat_even, got_odd_lat[128:136, :], got_even_lat[128:136, :])
    depth_r = jnp.where(lat_even, got_even_lat[136:144, :], got_odd_lat[136:144, :])
    depth_l = jnp.where(lat_even, got_odd_lat[136:144, :], got_even_lat[136:144, :])
    own_depth_r = jnp.where(lat_even, own_even_lat[136:144, :], own_odd_lat[136:144, :])
    own_depth_l = jnp.where(lat_even, own_odd_lat[136:144, :], own_even_lat[136:144, :])

    def mixed(pair):
        return [scalar_mix(x, y) for x, y in zip(*pair, strict=True)]

    w_r, w_l = mixed(ext_r[2:]), mixed(ext_l[2:])
    miss_own_r, miss_ext_r = lat_rims(
        own_r[0], mixed(own_r[1:]), own_depth_r, ext_r[1], w_r, depth_r
    )
    miss_ext_l, miss_own_l = lat_rims(
        ext_l[1], w_l, depth_l, own_l[0], mixed(own_l[1:]), own_depth_l
    )
    total = total + jnp.where(lane >= 126, miss_own_r, 0.0) + jnp.where(lane < 2, miss_own_l, 0.0)

    def side(i):
        return jnp.where(
            lane < 8,
            by_lanes(flat_r, -8 * i),
            jnp.where(lane >= 120, by_lanes(flat_l, 120 - 8 * i), 0.0),
        )

    elev_side = side(1)
    total_side = side(0) + elev_side
    total_side = total_side + jnp.where(lane < 2, miss_ext_r, 0.0)
    total_side = total_side + jnp.where(lane >= 126, miss_ext_l, 0.0)
    slot = lane >> 3
    sides = jnp.zeros((ROWS, LANES), F32)
    for i in range(3):
        sides = jnp.where(slot == 2 * i, by_lanes(flat_r, 8 * i - 8), sides)
        sides = jnp.where(slot == (2 * i - 1) % 16, by_lanes(flat_l, 8 * i + 112), sides)
    for ref in (odd_out, even_out):
        for i, x in enumerate((total, total_side, sides)):
            ref[8 * i : 8 * i + 8, :] = x
    packs = ext_r[0] + ext_l[0] + w_r + w_l + [depth_r, depth_l]
    group = row >> 1
    for i in range(5):
        top = bottom = jnp.zeros((ROWS, LANES), F32)
        for j, x in enumerate(packs[4 * i : 4 * i + 4]):
            top = jnp.where(group == j, by_rows(x, 2 * j), top)
            bottom = jnp.where(group == j, by_rows(x, 2 * j - 6), bottom)
        at = slice(24 + 8 * i, 32 + 8 * i)
        odd_out[at, :] = jnp.where(lon_even, top, bottom)
        even_out[at, :] = jnp.where(lon_even, bottom, top)


CHUNKS = ((0, 5), (5, 10), (10, 15))


def fields(
    masked, own_lon, own_odd_lat, own_even_lat, odd_lon, even_lon, odd_lat, even_lat,
    o1, o2, o3, o4, terms, rims, fresh, sems,
):
    row, lane = rows_of(), lanes_of()
    levels = flat_of(own_lon)[2].astype(jnp.int32)
    lon_even, lat_even = is_even_over("lon"), is_even_over("lat")
    outs = (o1, o2, o3, o4)
    at_edge = (lane < 2) | (lane >= 126)

    matrix = lat_matrix()
    for f in range(4):
        for first in range(0, LEVELS, 16):
            count = min(16, LEVELS - first)
            x = masked[f, first + 1 : first + 1 + count].reshape(count * ROWS, LANES)
            terms[f, ROWS * first : ROWS * (first + count), :] = lat_terms(x, matrix)

    in_even = (lane & 8) == 0

    def west_east(odd, even, base):
        x, y = odd[base : base + 8, :], even[base : base + 8, :]
        return jnp.where(lat_even, x, y), jnp.where(lat_even, y, x)

    depth_west, depth_east = west_east(own_odd_lat, own_even_lat, 136)
    for a in range(4):
        vel_west, vel_east = west_east(own_odd_lat, own_even_lat, 32 + 8 * a)
        for f in range(4):
            west, east = west_east(odd_lat, even_lat, f * 32 + 8 * a)
            right = west_part(vel_east, depth_east, east, a)
            left = by_lanes(east_part(vel_west, depth_west, west, a), 8)
            first = jnp.where(in_even, right, left)
            second = jnp.where(in_even, left, right)
            for i in range(8):
                rims[f, 16 * a + i] = by_lanes(first, -16 * i - 8)
                rims[f, 16 * a + 8 + i] = by_lanes(second, -16 * i - 16)

    def group(g, count):
        strips = []
        for f in range(4):
            at = pl.ds(pl.multiple_of(f * STRIP + 8 * g, 8), 8)
            x, y = odd_lon[at, :], even_lon[at, :]
            strips.append((jnp.where(lon_even, y, x), jnp.where(lon_even, x, y)))
        for j in range(count):
            k = 4 * g + j
            wet = k < levels
            center = [masked[f, k + 1] for f in range(4)]
            zonal, merid = ADV * center[0], ADV * center[1]
            at = pl.ds(pl.multiple_of(ROWS * k, ROWS), ROWS)
            for f in range(4):
                m = center[f]
                upper, lower = strips[f]
                rim = jnp.where(row < 4, by_rows(upper, -2 * j), by_rows(lower, 6 - 2 * j))
                n1 = by_rows(jnp.where(row < 1, rim, m), -1)
                n2 = by_rows(jnp.where(row < 2, rim, m), -2)
                p1 = by_rows(jnp.where(row > 6, rim, m), 1)
                p2 = by_rows(jnp.where(row > 5, rim, m), 2)
                gx = 8.0 * (n1 - p1) - (n2 - p2)
                gy = terms[f, at, :LANES]
                around = (n1 + p1) + terms[f, at, LANES:]
                column = masked[f, k] + masked[f, k + 2]
                value = 0.94 * m + 0.02 * column + 0.005 * around - (zonal * gx + merid * gy)
                fresh[f, k] = jnp.where(wet, value, 0.0) + jnp.where(at_edge, rims[f, k], 0.0)

    def body(g, carry):
        group(g, 4)
        return carry

    copies = []

    def send(first, last):
        for f in range(4):
            copies.append(
                pltpu.make_async_copy(
                    fresh.at[f, first:last], outs[f].at[first:last], sems.at[len(copies)]
                )
            )
            copies[-1].start()

    for first, last in CHUNKS:
        lax.fori_loop(first, last, body, 0, unroll=True)
        send(4 * first, 4 * last)
    group(15, LEVELS - 60)
    send(60, LEVELS)
    for copy in copies:
        copy.wait()


def solve(
    odd_b, even_b, own_b, own_lon, odd_lon, even_lon, odd_lat, even_lat, height
):
    row, lane = rows_of(), lanes_of()
    lon_even, lat_even = is_even_over("lon"), is_even_over("lat")
    lower = [jnp.where(lon_even, odd_b[8 * i : 8 * i + 8, :], even_b[8 * i : 8 * i + 8, :]) for i in range(8)]
    upper = [jnp.where(lon_even, even_b[8 * i : 8 * i + 8, :], odd_b[8 * i : 8 * i + 8, :]) for i in range(8)]
    own = [own_b[8 * i : 8 * i + 8, :] for i in range(3)]

    ext_r = [four(even_lat, f * 32, lat_even, odd_lat) for f in (0, 2, 3)]
    ext_l = [four(odd_lat, f * 32, lat_even, even_lat) for f in (0, 2, 3)]

    def lon_part(vel, wet, x1, x2):
        slope = jnp.where(row == 0, -8.0 * x1, jnp.where(row == 7, 8.0 * x1, 0.0))
        slope = slope + jnp.where(row < 2, x2, jnp.where(row >= 6, -x2, 0.0))
        near = jnp.where((row == 0) | (row == 7), x1, 0.0)
        return 0.005 * jnp.where(wet, near, 0.0) - ADV * vel * slope

    def rim_rows(tile, q, first):
        return by_rows(tile[3 + q // 4], first - 2 * (q % 4))

    def near_rows(q):
        return jnp.where(row < 4, rim_rows(upper, q, 0), rim_rows(lower, q, 6))

    def side_parts(ext, base, own_depth, near_depth):
        mine = theirs = jnp.zeros((ROWS, LANES), F32)
        for i in range(4):
            vel, w = ext[0][i], scalar_mix(ext[1][i], ext[2][i])
            qu, qw = base + i, 8 + base + i
            x2 = jnp.where(row < 4, rim_rows(lower, qw, 0), rim_rows(upper, qw, 6))
            x1 = jnp.where(row < 4, rim_rows(lower, qw, -1), rim_rows(upper, qw, 7))
            mine = mine + lon_part(vel, wet_pack(own_depth, i), x1, x2)
            y2 = jnp.where(row < 4, by_rows(w, 2), by_rows(w, -2))
            y1 = jnp.where(row < 4, by_rows(w, 1), by_rows(w, -1))
            theirs = theirs + lon_part(near_rows(qu), wet_pack(near_depth, i), y1, y2)
        return 0.1 * sum_slots(mine), 0.1 * sum_slots(theirs)

    depth_r = jnp.where(lat_even, even_lat[136:144, :], odd_lat[136:144, :])
    depth_l = jnp.where(lat_even, odd_lat[136:144, :], even_lat[136:144, :])
    mine_r, theirs_r = side_parts(ext_r, 0, depth_r, near_rows(16))
    mine_l, theirs_l = side_parts(ext_l, 4, depth_l, near_rows(17))
    in_r, in_l = lane < 8, lane >= 120
    mine = jnp.where(in_r, mine_r, jnp.where(in_l, mine_l, 0.0))
    theirs = jnp.where(in_r, theirs_r, jnp.where(in_l, theirs_l, 0.0))

    flat_own = flat_of(own_lon)
    flat_odd, flat_even = flat_of(odd_lon), flat_of(even_lon)
    flat_low = [jnp.where(lon_even, x, y) for x, y in zip(flat_odd, flat_even, strict=True)]
    flat_up = [jnp.where(lon_even, y, x) for x, y in zip(flat_odd, flat_even, strict=True)]

    rhs = [
        lower[0], own[0], upper[0],
        lower[1] + jnp.where(row >= 6, theirs, 0.0),
        own[1] + mine,
        upper[1] + jnp.where(row < 2, theirs, 0.0),
    ]
    sides = [
        [jnp.where(in_r | in_l, by_lanes(x[2], -16 * i), 0.0) for x in (lower, own, upper)]
        for i in range(3)
    ]
    elev = [flat_low[0], flat_own[0], flat_up[0]] + sides[0]
    diag = [flat_low[1], flat_own[1], flat_up[1]] + sides[1]
    wet = [x > 0.0 for x in [flat_low[2], flat_own[2], flat_up[2]] + sides[2]]
    diag = [x + 4.0 for x in diag]
    inverse = [1.0 / x for x in diag]
    coupled = [jnp.where(a, x, 0.0) for a, x in zip(wet, inverse, strict=True)]

    def over_rows(x):
        up = [by_rows(y, -1) for y in x]
        down = [by_rows(y, 1) for y in x]
        out = []
        for i in range(6):
            h, c = divmod(i, 3)
            n = jnp.where(row < 7, up[i], up[3 * h + (c + 1) % 3])
            p = jnp.where(row > 0, down[i], down[3 * h + (c + 2) % 3])
            out.append(n + p)
        return out

    def moved(x, d):
        turned = [by_lanes(y, -d) for y in x]
        inside = lane < LANES - d if d > 0 else lane >= -d
        return [jnp.where(inside, turned[i], turned[(i + 3) % 6]) for i in range(6)]

    def each(f, *xs):
        return [f(*x) for x in zip(*xs, strict=True)]

    sigma = SPECTRUM_MID / SPECTRUM_HALF
    ratio = 1.0 / sigma
    factors = [(0.0, 1.0 / SPECTRUM_MID)]
    for _ in range(ITERS - 1):
        following = 1.0 / (2.0 * sigma - ratio)
        factors.append((following * ratio, 2.0 * following / SPECTRUM_HALF))
        ratio = following
    scaled = each(lambda x, y: x * y, rhs, inverse)
    previous = elev
    iterate = elev[1]
    beside = [moved(coupled, 1), moved(coupled, -1)]

    def masked(x, c):
        return each(lambda y, k: jnp.where(k > 0.0, y, 0.0), x, c)

    def advance(x, res, c, z, z_next, z_last, factor):
        keep, gain = factor
        near = over_rows(z)
        res = each(
            lambda r, y, k, n, e, w: (r - y) + k * (n + (e + w)), res, x, c, near, z_next, z_last
        )
        if keep:
            x = each(lambda y, r: keep * y + gain * r, x, res)
        else:
            x = each(lambda r: gain * r, res)
        return x, res

    for step in range(0, ITERS, 2):
        z = masked(previous, coupled)
        east, west = moved(z, 1), moved(z, -1)
        far = moved(z, 2), moved(z, -2)
        r_east, r_west = moved(scaled, 1), moved(scaled, -1)
        first, second = factors[step : step + 2]
        previous, scaled = advance(previous, scaled, coupled, z, east, west, first)
        iterate = iterate + previous[1]
        d_east, _ = advance(east, r_east, beside[0], east, far[0], z, first)
        d_west, _ = advance(west, r_west, beside[1], west, z, far[1], first)
        z = masked(previous, coupled)
        previous, scaled = advance(
            previous, scaled, coupled, z, masked(d_east, beside[0]), masked(d_west, beside[1]), second
        )
        iterate = iterate + previous[1]
    height[...] = iterate


def shaped(*shape):
    return jax.ShapeDtypeStruct(shape, F32)


def call(kernel, outs, ins, flops, moved, **kw):
    return pl.pallas_call(
        kernel,
        out_shape=outs,
        in_specs=ins,
        compiler_params=pltpu.CompilerParams(vmem_limit_bytes=VMEM),
        cost_estimate=pl.CostEstimate(flops=flops, bytes_accessed=moved, transcendentals=0),
        **kw,
    )


WHOLE = pl.BlockSpec(memory_space=pltpu.VMEM)
HERE = pl.BlockSpec(memory_space=pltpu.HBM)
BLOCK = 4 * LEVELS * ROWS * LANES * 4


def call_pack_lon(*args):
    return call(
        pack_lon,
        (shaped(4, LEVELS + 4, ROWS, LANES), shaped(LON_ROWS, LANES), shaped(LON_ROWS, LANES)),
        [HERE] * 8, 10**6, 2 * BLOCK,
        out_specs=(WHOLE,) * 3,
        scratch_shapes=[
            pltpu.VMEM((4, LEVELS, ROWS, LANES), F32),
            pltpu.VMEM((2, ROWS, LANES), jnp.int32),
            pltpu.VMEM((2, ROWS, LANES), F32),
            pltpu.SemaphoreType.DMA((8,)),
        ],
    )(*args)


def call_pack_lat(*args):
    return call(
        pack_lat, (shaped(LAT_ROWS, LANES), shaped(LAT_ROWS, LANES), shaped(ROWS, LANES)),
        [WHOLE] * 2, 4 * 10**6, BLOCK,
    )(*args)


def call_forcing(*args):
    return call(
        forcing, (shaped(SOLVE_ROWS, LANES),) * 2, [WHOLE] * 9, 10**6, 10**6
    )(*args)


def call_fields(*args):
    return call(
        fields, (shaped(LEVELS, ROWS, LANES),) * 4, [WHOLE] * 8, 10**7, 3 * BLOCK,
        out_specs=(HERE,) * 4,
        scratch_shapes=[
            pltpu.VMEM((4, LEVELS * ROWS, 2 * LANES), F32),
            pltpu.VMEM((4, LEVELS + 2, ROWS, LANES), F32),
            pltpu.VMEM((4, LEVELS, ROWS, LANES), F32),
            pltpu.SemaphoreType.DMA((16,)),
        ],
    )(*args)


def call_solve(*args):
    return call(solve, shaped(ROWS, LANES), [WHOLE] * 8, 10**6, 10**6)(*args)


def on_device(u, v, t, s, water, layers, diag, elev):
    lon, lat = lax.axis_size("lon"), lax.axis_size("lat")
    lon_even = [(i, i ^ 1) for i in range(lon)]
    lon_odd = [(i, (((i + 1) ^ 1) - 1) % lon) for i in range(lon)]
    lat_even = [(i, i ^ 1) for i in range(lat)]
    lat_odd = [(i, ((i + 1) ^ 1) - 1) for i in range(1, lat - 1)]

    raw = [
        pltpu.with_memory_space_constraint(x, pltpu.HBM)
        for x in (u, v, t, s, water, layers, diag, elev)
    ]
    masked, own_odd, own_even = call_pack_lon(*raw)
    got_even = lax.ppermute(own_even, "lon", lon_even)
    got_odd = lax.ppermute(own_odd, "lon", lon_odd)
    lat_own_odd, lat_own_even, partial = call_pack_lat(masked, own_odd)
    lat_got_odd = lax.ppermute(lat_own_odd, "lat", lat_odd)
    lat_got_even = lax.ppermute(lat_own_even, "lat", lat_even)

    b_odd, b_even = call_forcing(
        got_even, got_odd, own_odd, own_even,
        lat_own_odd, lat_own_even, lat_got_odd, lat_got_even, partial,
    )
    b_got_odd = lax.ppermute(b_odd, "lon", lon_odd)
    b_got_even = lax.ppermute(b_even, "lon", lon_even)

    fresh = call_fields(
        masked, own_odd, lat_own_odd, lat_own_even, got_odd, got_even, lat_got_odd, lat_got_even
    )
    height = call_solve(
        b_got_odd, b_got_even, b_odd, own_odd, got_odd, got_even, lat_got_odd, lat_got_even
    )
    return (*fresh, height)


def solution(mesh):
    field, flat = P(None, "lon", "lat"), P("lon", "lat")
    return jax.shard_map(
        on_device,
        mesh=mesh,
        in_specs=(field,) * 4 + (flat,) * 4,
        out_specs=(field,) * 4 + (flat,),
        check_vma=False,
    )
```
